32 devices in a mesh: groups: 2 (over x), tile: 16 (over z, y, core).
Axes of the slice: x: 2, y: 2, z: 4, core: 2. Of those that a mesh axis runs over, the one named last changes fastest.
Arguments:
- spectrum: float32 [40, 36, 32, 128], P(None, None, ('groups', 'tile')), parts along dimension 2, may hold values from 0 to 1
- sea_mask: int32 [32, 128], P(('groups', 'tile')), parts along dimension 0, may hold values from 0 to 1, as said below
- card_deal: int32 [32, 128], P(('groups', 'tile')), parts along dimension 0, may hold values from -1 to 255, as said below
- wind: float32 [2, 32, 128], P(None, ('groups', 'tile')), parts along dimension 1, may hold values from -5 to 5
Outputs:
- spectrum_out: float32 [40, 36, 32, 128], P(None, None, ('groups', 'tile')), parts along dimension 2
- card_energy: float32 [512], P(('groups', 'tile')), parts along dimension 0
The draws below stay inside these ranges and needn't reach their ends.
There are 2 independent parts, one for each index of `groups`. The reference program is written for one: setup_inputs(seed, part) draws one part's arguments, and reference() takes and returns one part's arrays. A program takes and returns all parts, laid end to end along the dimension named above; each array names one. Nothing has to cross between parts.
Inputs may be any that keep to these rules, and one draw needn't show every extreme that they name: `sea_mask`: each row is sea (1) from its first cell up to a coastline and land (0) beyond. One tile of 1 row, placed by the seed, is all sea; the other tiles hold 8 times q or q + 1 sea points each, q = r // 15 with r = 16 (8) / 8, so that the window holds 256 sea points; within a tile the rows' sea counts differ by at most one, the first rows holding more. `card_deal`: land cells hold -1. Sea cells, numbered i = 0, 1, ... in row-major order over the window, hold c * 16 + s with card c = (i + o) mod 16 for an offset o drawn from the seed and slot s = i // 16. Every card holds exactly 16 points, and at most 8 points of one tile, a count that the all-sea tile reaches on every card.
All inputs are finite; a program needn't handle non-finite values.
Results may differ from the reference program's by a relative error of at most 0.0001.
Values sent between devices are 32-bit elements; how exact they have to be, the bound alone decides.
No kernel may reach another device: no remote copies, remote signals or barrier semaphores. Data moves between devices by JAX's collectives and lax.ppermute only.
A program may use at most 64 MiB of HBM per device.

```python
import math
import jax
import jax.numpy as jnp
from jax import lax

NK = 40
NTH = 36
CX = 1
NY = 128
STEPS = 2
SUB = 8
NX = 16
CARD_SLOTS = 16
N_TILE = 16


def sea_plan(key):
    tile_count = NX // CX
    cell_count = CX * NY
    capacity = cell_count // tile_count
    spread = tile_count * (tile_count - 8) // 8
    base_units = spread // (tile_count - 1)
    extra_units = spread % (tile_count - 1)
    coastal = base_units + (jnp.arange(tile_count - 1, dtype=jnp.int32) < extra_units).astype(jnp.int32)
    counts = jnp.concatenate([coastal, jnp.array([tile_count], dtype=jnp.int32)]) * capacity
    order = jax.random.permutation(jax.random.fold_in(key, 7), tile_count)
    tile_sea = counts[order]
    row_ids = jnp.arange(CX, dtype=jnp.int32)
    lengths = tile_sea[:, None] // CX + (row_ids[None, :] < tile_sea[:, None] % CX).astype(jnp.int32)
    column = jnp.arange(NY, dtype=jnp.int32)
    mask_out = (column[None, None, :] < lengths[:, :, None]).astype(jnp.int32).reshape(NX, NY)
    offset = jax.random.randint(jax.random.fold_in(key, 11), (), 0, tile_count)
    flat_mask = mask_out.reshape(-1)
    numbers = jnp.cumsum(flat_mask) - 1
    card_ids = (numbers + offset) % tile_count
    slot_ids = numbers // tile_count
    deal_out = jnp.where(flat_mask == 1, card_ids * (cell_count // 8) + slot_ids, -1).astype(jnp.int32)
    return (mask_out, deal_out.reshape(NX, NY))


def draw_sea_mask(key, part):
    return sea_plan(key)[0]


def draw_card_deal(key, part):
    return sea_plan(key)[1]


def block_scale(rng, extent, cuts, least, largest):
    def one(axis_at, parts):
        steps = jax.random.uniform(jax.random.fold_in(jax.random.fold_in(rng, 6), axis_at), (parts,), jnp.float32, least / len(cuts), largest / len(cuts))
        return jnp.repeat(jnp.exp(steps), extent[axis_at] // parts).reshape((-1,) + (1,) * (len(extent) - axis_at - 1))

    loudness = one(*cuts[0])
    for cut in cuts[1:]:
        loudness = loudness * one(*cut)
    return loudness


def scatter_about(stream_key, shape, scale, most, cuts=(), kind=jnp.bfloat16):
    result = scale * jax.random.normal(stream_key, shape, jnp.float32)
    if cuts:
        result = result * block_scale(stream_key, shape, cuts, -0.22, 0.18)
    return jnp.clip(result, -most, most).astype(kind)


def setup_inputs(seed: int = 0, part: int = 0) -> dict:
    arg_keys = jax.random.split(jax.random.key(seed), 5)
    part_splits = jax.random.split(jax.random.fold_in(arg_keys[4], part), 5)
    spectrum = jnp.clip(1.0 * jax.random.uniform(part_splits[0], (NK, NTH, NX, NY), jnp.float32) ** block_scale(part_splits[0], (NK, NTH, NX, NY), ((2, 16),), -0.2, 0.2), 0.0, 1.0)
    sea_mask = draw_sea_mask(jax.random.fold_in(jax.random.fold_in(arg_keys[4], part), 71), part)
    card_deal = draw_card_deal(jax.random.fold_in(jax.random.fold_in(arg_keys[4], part), 71), part)
    wind = scatter_about(part_splits[3], (2, NX, NY), 1.5, 5.0, ((1, 16),), jnp.float32)
    return dict(spectrum=spectrum, sea_mask=sea_mask, card_deal=card_deal, wind=wind)


COURANT_TOP = 0.7
WIND_RATE = 0.15
DECAY_RATE = 0.3
QUAD_RATE = 0.5
LIMITER = 0.25
ANGLE_UP = -11.48
ANGLE_DOWN = 33.56
SHIFT_UP = math.log(1.25) / math.log(1.1)
SHIFT_DOWN = math.log(0.75) / math.log(1.1)
GAIN_UP = 1.25 ** -4
GAIN_DOWN = 0.75 ** -4
GAIN_BOTH = 0.9375 ** -4


def courant(freq_count, dir_count):
    speeds = COURANT_TOP * 1.1 ** (-jnp.arange(freq_count, dtype=jnp.float32))
    angles = 2.0 * math.pi * jnp.arange(dir_count, dtype=jnp.float32) / dir_count
    return speeds[:, None] * jnp.cos(angles)[None, :], speeds[:, None] * jnp.sin(angles)[None, :]


def advect(values, padded, courant_x, courant_y):
    left_row = padded[..., :-2, :]
    right_row = padded[..., 2:, :]
    widths = [(0, 0)] * (values.ndim - 1) + [(1, 1)]
    wide = jnp.pad(values, widths)
    below = wide[..., :-2]
    above = wide[..., 2:]
    return (values - jnp.maximum(courant_x, 0.0) * (values - left_row)
            - jnp.maximum(-courant_x, 0.0) * (values - right_row)
            - jnp.maximum(courant_y, 0.0) * (values - below)
            - jnp.maximum(-courant_y, 0.0) * (values - above))


def shift_freq(values, offset):
    count = values.shape[0]
    if offset >= count or -offset >= count:
        return jnp.zeros_like(values)
    if offset >= 0:
        return jnp.concatenate([values[offset:], jnp.zeros((offset,) + values.shape[1:], values.dtype)], axis=0)
    return jnp.concatenate([jnp.zeros((-offset,) + values.shape[1:], values.dtype), values[:count + offset]], axis=0)


def interp(values, along_freq, along_dir):
    base_k = math.floor(along_freq)
    part_k = along_freq - base_k
    shifted = (1.0 - part_k) * shift_freq(values, base_k) + part_k * shift_freq(values, base_k + 1)
    base_j = math.floor(along_dir)
    part_j = along_dir - base_j
    return (1.0 - part_j) * jnp.roll(shifted, -base_j, axis=1) + part_j * jnp.roll(shifted, -base_j - 1, axis=1)


def interp_adjoint(values, along_freq, along_dir):
    base_j = math.floor(along_dir)
    part_j = along_dir - base_j
    turned = (1.0 - part_j) * jnp.roll(values, base_j, axis=1) + part_j * jnp.roll(values, base_j + 1, axis=1)
    base_k = math.floor(along_freq)
    part_k = along_freq - base_k
    return (1.0 - part_k) * shift_freq(turned, -base_k) + part_k * shift_freq(turned, -base_k - 1)


def source_rate(spec, wind_east, wind_north):
    freq_count, dir_count = spec.shape[0], spec.shape[1]
    levels = 3.0 ** (jnp.arange(freq_count, dtype=jnp.float32) / (freq_count - 1))
    angles = 2.0 * math.pi * jnp.arange(dir_count, dtype=jnp.float32) / dir_count
    weights = levels / (dir_count * jnp.sum(levels))
    steepness = jnp.sum(spec * weights[:, None, None], axis=(0, 1))
    drive = wind_east[None, None, :] * jnp.cos(angles)[None, :, None] + wind_north[None, None, :] * jnp.sin(angles)[None, :, None]
    wind_input = WIND_RATE * jnp.maximum(0.5 * levels[:, None, None] * drive - 1.0, 0.0) * spec
    dissipation = -DECAY_RATE * levels[:, None, None] * steepness[None, None, :] * spec
    nonlinear = jnp.zeros_like(spec)
    for mirror in (1.0, -1.0):
        turn_up = mirror * ANGLE_UP * dir_count / 360.0
        turn_down = mirror * ANGLE_DOWN * dir_count / 360.0
        plus_part = interp(spec, SHIFT_UP, turn_up)
        minus_part = interp(spec, SHIFT_DOWN, turn_down)
        quad = QUAD_RATE * levels[:, None, None] * (spec * spec * (GAIN_UP * plus_part + GAIN_DOWN * minus_part)
                                                   - 2.0 * GAIN_BOTH * spec * plus_part * minus_part)
        nonlinear = nonlinear - 2.0 * quad + interp_adjoint(quad, SHIFT_UP, turn_up) + interp_adjoint(quad, SHIFT_DOWN, turn_down)
    return wind_input + nonlinear + dissipation


def source_update(spec, wind_east, wind_north):
    for sub_index in range(SUB):
        total = source_rate(spec, wind_east, wind_north)
        spec = spec + (LIMITER / SUB) * jnp.tanh(total / LIMITER)
    return spec


def reference(spectrum, sea_mask, card_deal, wind):
    sea_frac = sea_mask.astype(jnp.float32)
    courant_x, courant_y = courant(NK, NTH)
    field_now = spectrum * sea_frac[None, None]
    block_cells = CX * NY

    def advect_freq(args):
        layer, cour_x, cour_y = args
        padded = jnp.pad(layer, ((0, 0), (1, 1), (0, 0)))
        return advect(layer, padded, cour_x[:, None, None], cour_y[:, None, None]) * sea_frac[None]

    def update_block(args):
        block, east_part, north_part = args
        return source_update(block, east_part, north_part)

    east_blocks = wind[0].reshape(N_TILE, block_cells)
    north_blocks = wind[1].reshape(N_TILE, block_cells)
    for step_index in range(STEPS):
        advected = lax.map(advect_freq, (field_now, courant_x, courant_y))
        blocked = jnp.moveaxis(advected.reshape(NK, NTH, N_TILE, block_cells), 2, 0)
        updated = lax.map(update_block, (blocked, east_blocks, north_blocks))
        field_now = jnp.moveaxis(updated, 0, 2).reshape(NK, NTH, NX, NY) * sea_frac[None, None]
    cell_energy = jnp.mean(field_now, axis=(0, 1)).reshape(-1)
    deal_flat = card_deal.reshape(-1)
    put_index = jnp.where(deal_flat >= 0, deal_flat, N_TILE * CARD_SLOTS).astype(jnp.int32)
    card_energy = jnp.zeros((N_TILE * CARD_SLOTS,), jnp.float32).at[put_index].set(cell_energy, mode="drop")
    return field_now, card_energy
```

```python
import functools
import math

import jax
import jax.numpy as jnp
import numpy as np
from jax import lax
from jax.experimental import pallas as pl
from jax.experimental.pallas import tpu as pltpu
from jax.sharding import PartitionSpec as P

STEPS = 2
SUB = 8
COURANT_TOP = 0.7
WIND_RATE = 0.15
DECAY_RATE = 0.3
QUAD_RATE = 0.5
LIMITER = 0.25
ANGLE_UP = -11.48
ANGLE_DOWN = 33.56
SHIFT_UP = math.log(1.25) / math.log(1.1)
SHIFT_DOWN = math.log(0.75) / math.log(1.1)
GAIN_UP = 1.25 ** (-4)
GAIN_DOWN = 0.75 ** (-4)
GAIN_BOTH = 0.9375 ** (-4)

LANES = 128
ROWS = 8
PAD = 4


def split(offset):
    base = math.floor(offset)
    return base, offset - base


GAIN = 2.0 * GAIN_BOTH / (GAIN_UP * GAIN_DOWN)
UP_K, UP_W = split(SHIFT_UP)
DOWN_K, DOWN_W = split(SHIFT_DOWN)


def directions(count):
    angles = 2.0 * math.pi * np.arange(count) / count
    return np.cos(angles), np.sin(angles)


def tables(freq_count, dir_count):
    levels = 3.0 ** (np.arange(freq_count) / (freq_count - 1))
    speeds = COURANT_TOP * 1.1 ** (-np.arange(freq_count, dtype=np.float64))
    up_j, up_z = split(ANGLE_UP * dir_count / 360.0)
    near_up = max(up_z, 1.0 - up_z)
    rate = (1.0 - UP_W) * near_up / LIMITER
    rows = [
        speeds,
        rate * QUAD_RATE * GAIN * GAIN * levels,
        GAIN / LIMITER * WIND_RATE * 0.5 * levels,
        GAIN / (dir_count * np.sum(levels)) * levels,
        GAIN / LIMITER * DECAY_RATE * levels,
    ]
    return np.broadcast_to(
        np.stack(rows)[:, :, None], (len(rows), freq_count, LANES)
    ).astype(np.float32)


def pack_order(dir_count, freq_count, forward):
    cosines, _ = directions(dir_count)
    chosen = [j for j in range(dir_count) if (cosines[j] > 0) == forward]
    return [(j, kb) for j in chosen for kb in range(freq_count // ROWS)]


def pack_rows(dir_count, freq_count, edge):
    most = max(len(pack_order(dir_count, freq_count, f)) for f in (True, False))
    per = LANES // edge
    return -(-most // per) * ROWS


def pack(fetch, order, edge, lane):
    per = LANES // edge
    out = []
    for start in range(0, len(order), per):
        total = None
        for b, item in enumerate(order[start:start + per]):
            value = fetch(*item)
            if b == 0:
                total = value
            else:
                total = jnp.where(lane // edge == b, pltpu.roll(value, edge * b, 1), total)
        out.append(total)
    return out


def store_packs(fetch, pair_ref, next_ref, parity, freq_count, dir_count, edge, lane):
    for forward in (True, False):
        packs = pack(fetch, pack_order(dir_count, freq_count, forward), edge, lane)
        to_pair = parity == (0 if forward else 1)

        @pl.when(to_pair)
        def _():
            for g, value in enumerate(packs):
                pair_ref[pl.ds(g * ROWS, ROWS), :] = value

        @pl.when(jnp.logical_not(to_pair))
        def _():
            for g, value in enumerate(packs):
                next_ref[pl.ds(g * ROWS, ROWS), :] = value


def edges_kernel(freq_count, dir_count, edge, parity_ref, in_ref, mask_ref, pair_ref, next_ref):
    lane = lax.broadcasted_iota(jnp.int32, (ROWS, LANES), 1)
    mask = mask_ref[...].astype(jnp.float32)

    def fetch(j, kb):
        return in_ref[pl.ds(kb * ROWS * dir_count + j, ROWS, stride=dir_count), :] * mask

    store_packs(fetch, pair_ref, next_ref, parity_ref[0], freq_count, dir_count, edge, lane)


def step_kernel(
    freq_count, dir_count, edge, first, last,
    parity_ref, in_ref, mask_ref, wind_ref, table_ref, pair_ref, next_ref, *rest
):
    if last:
        deal_ref, out_ref, energy_ref = rest[:3]
        rest = rest[3:]
    else:
        out_ref, pair_out, next_out = rest[:3]
        rest = rest[3:]
    e_ref, u_ref, d_ref, n_ref, w_ref, acc_ref, c_ref, back_ref = rest
    blocks = freq_count // ROWS
    cosines, sines = directions(dir_count)
    lane = lax.broadcasted_iota(jnp.int32, (ROWS, LANES), 1)
    mask = mask_ref[...].astype(jnp.float32)
    half = mask * (1.0 / GAIN)
    parity = parity_ref[0]

    zero = jnp.zeros((PAD, LANES), jnp.float32)
    for j in range(dir_count):
        for ref in (e_ref, u_ref, d_ref):
            ref[j, pl.ds(0, PAD), :] = zero
            ref[j, pl.ds(PAD + freq_count, PAD), :] = zero

    @pl.when(parity == 0)
    def _():
        back_ref[0] = next_ref[...]
        back_ref[1] = pair_ref[...]

    @pl.when(parity == 1)
    def _():
        back_ref[0] = pair_ref[...]
        back_ref[1] = next_ref[...]

    place = {}
    for forward in (True, False):
        for i, item in enumerate(pack_order(dir_count, freq_count, forward)):
            place[item] = (0 if forward else 1, i)
    per = LANES // edge
    for kb in range(blocks):
        speed = table_ref[0, pl.ds(kb * ROWS, ROWS), :]
        drive_rate = table_ref[2, pl.ds(kb * ROWS, ROWS), :]
        total = jnp.zeros((ROWS, LANES), jnp.float32)
        for j in range(dir_count):
            if first:
                here = in_ref[pl.ds(kb * ROWS * dir_count + j, ROWS, stride=dir_count), :] * mask
            else:
                here = in_ref[j, pl.ds(kb * ROWS, ROWS), :]
            side, i = place[(j, kb)]
            beside = back_ref[side, pl.ds(i // per * ROWS, ROWS), :]
            turn = (-(i % per) * edge) % LANES
            if turn:
                beside = pltpu.roll(beside, turn, 1)
            beside = jnp.where(lane < edge, beside, 0.0)
            if sines[j] > 0:
                along = jnp.where(lane == 0, 0.0, pltpu.roll(here, 1, 1))
            else:
                along = jnp.where(lane == LANES - 1, 0.0, pltpu.roll(here, LANES - 1, 1))
            moved = (
                here
                - speed * float(abs(cosines[j])) * (here - beside)
                - speed * float(abs(sines[j])) * (here - along)
            ) * half
            e_ref[j, pl.ds(PAD + kb * ROWS, ROWS), :] = moved
            total = total + moved
            drive = wind_ref[0:1, :] * float(cosines[j]) + wind_ref[1:2, :] * float(sines[j])
            w_ref[j, pl.ds(kb * ROWS, ROWS), :] = jnp.maximum(
                drive_rate * drive - GAIN / LIMITER * WIND_RATE, 0.0
            )
        acc_ref[pl.ds(kb * ROWS, ROWS), :] = total

    up_j, up_z = split(ANGLE_UP * dir_count / 360.0)
    down_j, down_z = split(ANGLE_DOWN * dir_count / 360.0)
    up_near, up_far = up_j + 1, up_j
    up_weight, up_rest = up_z, (1.0 - up_z) / up_z
    down_near, down_far = down_j, down_j + 1
    down_weight, down_rest = 1.0 - down_z, down_z / (1.0 - down_z)
    up_scale = GAIN_UP * GAIN * up_weight
    down_scale = GAIN_DOWN * GAIN * down_weight
    fold = (1.0 - UP_W) * up_weight
    up_tail = UP_W / (1.0 - UP_W)
    down_head = (1.0 - DOWN_W) * down_weight / fold
    down_tail = DOWN_W * down_weight / fold
    own = -2.0 / fold

    def stage_a(kb, carry):
        base = kb * ROWS
        strength = table_ref[1, pl.ds(base, ROWS), :]
        up, up_c, down, down_c, quads = {}, {}, {}, {}, {}

        def read(j, offset):
            return e_ref[j, pl.ds(base + PAD + offset, ROWS), :]

        def get_up(j):
            j %= dir_count
            if j not in up:
                up[j] = (up_scale * (1.0 - UP_W)) * read(j, UP_K) + (up_scale * UP_W) * read(j, UP_K + 1)
                up_c[j] = up[j] * up_rest
            return up[j], up_c[j]

        def get_down(j):
            j %= dir_count
            if j not in down:
                down[j] = (down_scale * (1.0 - DOWN_W)) * read(j, DOWN_K) + (
                    down_scale * DOWN_W
                ) * read(j, DOWN_K + 1)
                down_c[j] = down[j] * down_rest
            return down[j], down_c[j]

        def get_quads(j):
            j %= dir_count
            if j not in quads:
                here = read(j, 0)
                gain = here * strength
                pair = []
                for sign in (1, -1):
                    plus = get_up(j + sign * up_near)[0] + get_up(j + sign * up_far)[1]
                    minus = get_down(j + sign * down_near)[0] + get_down(j + sign * down_far)[1]
                    pair.append(gain * (here * (plus + minus) - plus * minus))
                quads[j] = pair
            return quads[j]

        for j in range(dir_count):
            u_ref[j, pl.ds(base + PAD, ROWS), :] = (
                get_quads(j - up_near)[0] + get_quads(j + up_near)[1]
            ) + up_rest * (get_quads(j - up_far)[0] + get_quads(j + up_far)[1])
            d_ref[j, pl.ds(base + PAD, ROWS), :] = (
                get_quads(j - down_near)[0] + get_quads(j + down_near)[1]
            ) + down_rest * (get_quads(j - down_far)[0] + get_quads(j + down_far)[1])
            n_ref[j, pl.ds(base, ROWS), :] = own * (get_quads(j)[0] + get_quads(j)[1])
        return carry

    def stage_b(kb, carry):
        base = kb * ROWS
        decay = c_ref[pl.ds(base, ROWS), :]
        total = jnp.zeros((ROWS, LANES), jnp.float32)
        for j in range(dir_count):
            here = e_ref[j, pl.ds(base + PAD, ROWS), :]
            rate = here * (w_ref[j, pl.ds(base, ROWS), :] - decay) + n_ref[j, pl.ds(base, ROWS), :]
            rate = rate + (
                u_ref[j, pl.ds(base + PAD - UP_K, ROWS), :]
                + up_tail * u_ref[j, pl.ds(base + PAD - UP_K - 1, ROWS), :]
            )
            rate = rate + (
                down_head * d_ref[j, pl.ds(base + PAD - DOWN_K, ROWS), :]
                + down_tail * d_ref[j, pl.ds(base + PAD - DOWN_K - 1, ROWS), :]
            )
            here = here + (LIMITER / SUB / GAIN) * jnp.tanh(rate)
            e_ref[j, pl.ds(base + PAD, ROWS), :] = here
            total = total + here
        acc_ref[pl.ds(base, ROWS), :] = total
        return carry

    def sub_step(index, carry):
        steepness = jnp.sum(acc_ref[...] * table_ref[3], axis=0, keepdims=True)
        c_ref[...] = steepness * table_ref[4]
        lax.fori_loop(0, blocks, stage_a, 0)
        lax.fori_loop(0, blocks, stage_b, 0)
        return carry

    lax.fori_loop(0, SUB, sub_step, 0)

    full = mask * GAIN

    def result(j, kb):
        return e_ref[j, pl.ds(PAD + kb * ROWS, ROWS), :] * full

    for kb in range(blocks):
        for j in range(dir_count):
            if last:
                out_ref[pl.ds(kb * ROWS * dir_count + j, ROWS, stride=dir_count), :] = result(j, kb)
            else:
                out_ref[j, pl.ds(kb * ROWS, ROWS), :] = result(j, kb)
    if last:
        energy = jnp.sum(acc_ref[...], axis=0, keepdims=True) * (full * (1.0 / (freq_count * dir_count)))
        slots = energy_ref.shape[1]
        chosen = (
            deal_ref[...] == lax.broadcasted_iota(jnp.int32, (LANES, slots), 1)
        ).astype(jnp.float32)
        energy_ref[...] = jnp.dot(
            jnp.broadcast_to(energy, (ROWS, LANES)), chosen,
            precision=lax.Precision.HIGHEST, preferred_element_type=jnp.float32,
        )[0:1]
    else:
        store_packs(result, pair_out, next_out, parity, freq_count, dir_count, edge, lane)


def coast_width(tile_count, cell_count):
    capacity = cell_count // tile_count
    spread = tile_count * (tile_count - 8) // 8
    most = -(-spread // (tile_count - 1)) * capacity
    width = ROWS
    while width < most:
        width *= 2
    return min(width, LANES)


def shards(spectrum, sea_mask, card_deal, wind):
    freq_count, dir_count, row_count, row_width = spectrum.shape
    cell_count = row_count * row_width
    tile_count = lax.axis_size("tile")
    slot_count = cell_count // 8
    edge = coast_width(tile_count, cell_count)
    here = lax.axis_index("tile")
    parity = (here % 2).astype(jnp.int32).reshape(1)
    flat = spectrum.reshape(freq_count * dir_count, cell_count)
    mask = sea_mask.reshape(1, cell_count)
    winds = wind.reshape(2, cell_count)
    deal = card_deal.reshape(cell_count, 1)
    table = jnp.asarray(tables(freq_count, dir_count))
    rows = pack_rows(dir_count, freq_count, edge)
    packed = jax.ShapeDtypeStruct((rows, LANES), jnp.float32)
    smem = pl.BlockSpec(memory_space=pltpu.SMEM)
    vmem = pl.BlockSpec(memory_space=pltpu.VMEM)
    params = pltpu.CompilerParams(vmem_limit_bytes=48 * 1024 * 1024)
    padded = pltpu.VMEM((dir_count, freq_count + 2 * PAD, LANES), jnp.float32)
    plain = pltpu.VMEM((dir_count, freq_count, LANES), jnp.float32)
    column = pltpu.VMEM((freq_count, LANES), jnp.float32)
    scratch = [padded, padded, padded, plain, plain, column, column, pltpu.VMEM((2, rows, LANES), jnp.float32)]

    def exchange(pair_out, next_out):
        next_in = lax.ppermute(
            next_out, "tile",
            [(i, i + 1 if i % 2 else i - 1) for i in range(1, tile_count - 1)],
        )
        pair_in = lax.ppermute(pair_out, "tile", [(i, i ^ 1) for i in range(tile_count)])
        return pair_in, next_in

    pair_in, next_in = exchange(*pl.pallas_call(
        functools.partial(edges_kernel, freq_count, dir_count, edge),
        out_shape=(packed, packed),
        in_specs=[smem, vmem, vmem],
        out_specs=(vmem, vmem),
        compiler_params=params,
        name="edges",
    )(parity, flat, mask))
    field, pair_out, next_out = pl.pallas_call(
        functools.partial(step_kernel, freq_count, dir_count, edge, True, False),
        out_shape=(jax.ShapeDtypeStruct((dir_count, freq_count, LANES), jnp.float32), packed, packed),
        in_specs=[smem] + [vmem] * 6,
        out_specs=(vmem,) * 3,
        scratch_shapes=scratch,
        compiler_params=params,
        name="first_step",
    )(parity, flat, mask, winds, table, pair_in, next_in)
    pair_in, next_in = exchange(pair_out, next_out)
    out, energy = pl.pallas_call(
        functools.partial(step_kernel, freq_count, dir_count, edge, False, True),
        out_shape=(
            jax.ShapeDtypeStruct((freq_count * dir_count, LANES), jnp.float32),
            jax.ShapeDtypeStruct((1, tile_count * slot_count), jnp.float32),
        ),
        in_specs=[smem] + [vmem] * 7,
        out_specs=(vmem,) * 2,
        scratch_shapes=scratch,
        compiler_params=params,
        name="second_step",
    )(parity, field, mask, winds, table, pair_in, next_in, deal)
    shared = lax.all_to_all(
        energy.reshape(tile_count, slot_count), "tile", split_axis=0, concat_axis=0, tiled=True
    )
    card_energy = jnp.sum(shared, axis=0)
    return out.reshape(freq_count, dir_count, row_count, row_width), card_energy


def solution(mesh):
    placed = (
        P(None, None, ("groups", "tile"), None),
        P(("groups", "tile"), None),
        P(("groups", "tile"), None),
        P(None, ("groups", "tile"), None),
    )
    return jax.shard_map(
        shards,
        mesh=mesh,
        in_specs=placed,
        out_specs=(P(None, None, ("groups", "tile"), None), P(("groups", "tile"))),
        check_vma=False,
    )
```

```python
import functools
import math

import jax
import jax.numpy as jnp
import numpy as np
from jax import lax
from jax.experimental import pallas as pl
from jax.experimental.pallas import tpu as pltpu
from jax.sharding import PartitionSpec as P

STEPS = 2
SUB = 8
COURANT_TOP = 0.7
WIND_RATE = 0.15
DECAY_RATE = 0.3
QUAD_RATE = 0.5
LIMITER = 0.25
ANGLE_UP = -11.48
ANGLE_DOWN = 33.56
SHIFT_UP = math.log(1.25) / math.log(1.1)
SHIFT_DOWN = math.log(0.75) / math.log(1.1)
GAIN_UP = 1.25 ** (-4)
GAIN_DOWN = 0.75 ** (-4)
GAIN_BOTH = 0.9375 ** (-4)

LANES = 128
ROWS = 8
PAD = 4


def split(offset):
    base = math.floor(offset)
    return base, offset - base


GAIN = 2.0 * GAIN_BOTH / (GAIN_UP * GAIN_DOWN)
UP_K, UP_W = split(SHIFT_UP)
DOWN_K, DOWN_W = split(SHIFT_DOWN)


def directions(count):
    angles = 2.0 * math.pi * np.arange(count) / count
    return np.cos(angles), np.sin(angles)


def tables(freq_count, dir_count):
    levels = 3.0 ** (np.arange(freq_count) / (freq_count - 1))
    speeds = COURANT_TOP * 1.1 ** (-np.arange(freq_count, dtype=np.float64))
    up_j, up_z = split(ANGLE_UP * dir_count / 360.0)
    near_up = max(up_z, 1.0 - up_z)
    rate = (1.0 - UP_W) * near_up / LIMITER
    rows = [
        speeds,
        rate * QUAD_RATE * GAIN * GAIN * levels,
        GAIN / LIMITER * WIND_RATE * 0.5 * levels,
        GAIN / (dir_count * np.sum(levels)) * levels,
        GAIN / LIMITER * DECAY_RATE * levels,
    ]
    return np.broadcast_to(
        np.stack(rows)[:, :, None], (len(rows), freq_count, LANES)
    ).astype(np.float32)


def pack_order(dir_count, freq_count, forward):
    cosines, _ = directions(dir_count)
    chosen = [j for j in range(dir_count) if (cosines[j] > 0) == forward]
    return [(j, kb) for j in chosen for kb in range(freq_count // ROWS)]


def pack_rows(dir_count, freq_count, edge):
    most = max(len(pack_order(dir_count, freq_count, f)) for f in (True, False))
    per = LANES // edge
    return -(-most // per) * ROWS


def pack(fetch, order, edge, lane):
    per = LANES // edge
    out = []
    for start in range(0, len(order), per):
        total = None
        for b, item in enumerate(order[start:start + per]):
            value = fetch(*item)
            if b == 0:
                total = value
            else:
                total = jnp.where(lane // edge == b, pltpu.roll(value, edge * b, 1), total)
        out.append(total)
    return out


def store_packs(fetch, pair_ref, next_ref, parity, freq_count, dir_count, edge, lane):
    for forward in (True, False):
        packs = pack(fetch, pack_order(dir_count, freq_count, forward), edge, lane)
        to_pair = parity == (0 if forward else 1)

        @pl.when(to_pair)
        def _():
            for g, value in enumerate(packs):
                pair_ref[pl.ds(g * ROWS, ROWS), :] = value

        @pl.when(jnp.logical_not(to_pair))
        def _():
            for g, value in enumerate(packs):
                next_ref[pl.ds(g * ROWS, ROWS), :] = value


def edges_kernel(freq_count, dir_count, edge, parity_ref, in_ref, mask_ref, pair_ref, next_ref):
    lane = lax.broadcasted_iota(jnp.int32, (ROWS, LANES), 1)
    mask = mask_ref[...].astype(jnp.float32)

    def fetch(j, kb):
        return in_ref[pl.ds(kb * ROWS * dir_count + j, ROWS, stride=dir_count), :] * mask

    store_packs(fetch, pair_ref, next_ref, parity_ref[0], freq_count, dir_count, edge, lane)


def step_kernel(
    freq_count, dir_count, edge, slot_count, first, last,
    parity_ref, in_ref, mask_ref, wind_ref, table_ref, pair_ref, next_ref, *rest
):
    if last:
        deal_ref, out_ref, energy_ref = rest[:3]
        rest = rest[3:]
    else:
        out_ref, pair_out, next_out = rest[:3]
        rest = rest[3:]
    e_ref, u_ref, d_ref, n_ref, w_ref, acc_ref, c_ref, back_ref = rest
    blocks = freq_count // ROWS
    cosines, sines = directions(dir_count)
    lane = lax.broadcasted_iota(jnp.int32, (ROWS, LANES), 1)
    mask = mask_ref[...].astype(jnp.float32)
    half = mask * (1.0 / GAIN)
    parity = parity_ref[0]

    zero = jnp.zeros((PAD, LANES), jnp.float32)
    for j in range(dir_count):
        for ref in (e_ref, u_ref, d_ref):
            ref[j, pl.ds(0, PAD), :] = zero
            ref[j, pl.ds(PAD + freq_count, PAD), :] = zero

    inner = (parity_ref[1] == 0).astype(jnp.float32)

    @pl.when(parity == 0)
    def _():
        back_ref[0] = next_ref[...] * inner
        back_ref[1] = pair_ref[...]

    @pl.when(parity == 1)
    def _():
        back_ref[0] = pair_ref[...]
        back_ref[1] = next_ref[...] * inner

    place = {}
    for forward in (True, False):
        for i, item in enumerate(pack_order(dir_count, freq_count, forward)):
            place[item] = (0 if forward else 1, i)
    per = LANES // edge
    for kb in range(blocks):
        speed = table_ref[0, pl.ds(kb * ROWS, ROWS), :]
        drive_rate = table_ref[2, pl.ds(kb * ROWS, ROWS), :]
        total = jnp.zeros((ROWS, LANES), jnp.float32)
        for j in range(dir_count):
            if first:
                here = in_ref[pl.ds(kb * ROWS * dir_count + j, ROWS, stride=dir_count), :] * mask
            else:
                here = in_ref[j, pl.ds(kb * ROWS, ROWS), :]
            side, i = place[(j, kb)]
            beside = back_ref[side, pl.ds(i // per * ROWS, ROWS), :]
            turn = (-(i % per) * edge) % LANES
            if turn:
                beside = pltpu.roll(beside, turn, 1)
            beside = jnp.where(lane < edge, beside, 0.0)
            if sines[j] > 0:
                along = jnp.where(lane == 0, 0.0, pltpu.roll(here, 1, 1))
            else:
                along = jnp.where(lane == LANES - 1, 0.0, pltpu.roll(here, LANES - 1, 1))
            moved = (
                here
                - speed * float(abs(cosines[j])) * (here - beside)
                - speed * float(abs(sines[j])) * (here - along)
            ) * half
            e_ref[j, pl.ds(PAD + kb * ROWS, ROWS), :] = moved
            total = total + moved
            drive = wind_ref[0:1, :] * float(cosines[j]) + wind_ref[1:2, :] * float(sines[j])
            w_ref[j, pl.ds(kb * ROWS, ROWS), :] = jnp.maximum(
                drive_rate * drive - GAIN / LIMITER * WIND_RATE, 0.0
            )
        acc_ref[pl.ds(kb * ROWS, ROWS), :] = total

    up_j, up_z = split(ANGLE_UP * dir_count / 360.0)
    down_j, down_z = split(ANGLE_DOWN * dir_count / 360.0)
    up_near, up_far = up_j + 1, up_j
    up_weight, up_rest = up_z, (1.0 - up_z) / up_z
    down_near, down_far = down_j, down_j + 1
    down_weight, down_rest = 1.0 - down_z, down_z / (1.0 - down_z)
    up_scale = GAIN_UP * GAIN * up_weight
    down_scale = GAIN_DOWN * GAIN * down_weight
    fold = (1.0 - UP_W) * up_weight
    up_tail = UP_W / (1.0 - UP_W)
    down_head = (1.0 - DOWN_W) * down_weight / fold
    down_tail = DOWN_W * down_weight / fold
    own = -2.0 / fold

    def stage_a(kb, carry):
        base = kb * ROWS
        strength = table_ref[1, pl.ds(base, ROWS), :]
        up, up_c, down, down_c, quads = {}, {}, {}, {}, {}

        def read(j, offset):
            return e_ref[j, pl.ds(base + PAD + offset, ROWS), :]

        def get_up(j):
            j %= dir_count
            if j not in up:
                up[j] = (up_scale * (1.0 - UP_W)) * read(j, UP_K) + (up_scale * UP_W) * read(j, UP_K + 1)
                up_c[j] = up[j] * up_rest
            return up[j], up_c[j]

        def get_down(j):
            j %= dir_count
            if j not in down:
                down[j] = (down_scale * (1.0 - DOWN_W)) * read(j, DOWN_K) + (
                    down_scale * DOWN_W
                ) * read(j, DOWN_K + 1)
                down_c[j] = down[j] * down_rest
            return down[j], down_c[j]

        def get_quads(j):
            j %= dir_count
            if j not in quads:
                here = read(j, 0)
                gain = here * strength
                pair = []
                for sign in (1, -1):
                    plus = get_up(j + sign * up_near)[0] + get_up(j + sign * up_far)[1]
                    minus = get_down(j + sign * down_near)[0] + get_down(j + sign * down_far)[1]
                    pair.append(gain * (here * (plus + minus) - plus * minus))
                quads[j] = pair
            return quads[j]

        for j in range(dir_count):
            u_ref[j, pl.ds(base + PAD, ROWS), :] = (
                get_quads(j - up_near)[0] + get_quads(j + up_near)[1]
            ) + up_rest * (get_quads(j - up_far)[0] + get_quads(j + up_far)[1])
            d_ref[j, pl.ds(base + PAD, ROWS), :] = (
                get_quads(j - down_near)[0] + get_quads(j + down_near)[1]
            ) + down_rest * (get_quads(j - down_far)[0] + get_quads(j + down_far)[1])
            n_ref[j, pl.ds(base, ROWS), :] = own * (get_quads(j)[0] + get_quads(j)[1])
        return carry

    def stage_b(kb, carry):
        base = kb * ROWS
        decay = c_ref[pl.ds(base, ROWS), :]
        total = jnp.zeros((ROWS, LANES), jnp.float32)
        for j in range(dir_count):
            here = e_ref[j, pl.ds(base + PAD, ROWS), :]
            rate = here * (w_ref[j, pl.ds(base, ROWS), :] - decay) + n_ref[j, pl.ds(base, ROWS), :]
            rate = rate + (
                u_ref[j, pl.ds(base + PAD - UP_K, ROWS), :]
                + up_tail * u_ref[j, pl.ds(base + PAD - UP_K - 1, ROWS), :]
            )
            rate = rate + (
                down_head * d_ref[j, pl.ds(base + PAD - DOWN_K, ROWS), :]
                + down_tail * d_ref[j, pl.ds(base + PAD - DOWN_K - 1, ROWS), :]
            )
            here = here + (LIMITER / SUB / GAIN) * jnp.tanh(rate)
            e_ref[j, pl.ds(base + PAD, ROWS), :] = here
            total = total + here
        acc_ref[pl.ds(base, ROWS), :] = total
        return carry

    def sub_step(index, carry):
        steepness = jnp.sum(acc_ref[...] * table_ref[3], axis=0, keepdims=True)
        c_ref[...] = steepness * table_ref[4]
        lax.fori_loop(0, blocks, stage_a, 0)
        lax.fori_loop(0, blocks, stage_b, 0)
        return carry

    lax.fori_loop(0, SUB, sub_step, 0)

    full = mask * GAIN

    def result(j, kb):
        return e_ref[j, pl.ds(PAD + kb * ROWS, ROWS), :] * full

    for kb in range(blocks):
        for j in range(dir_count):
            if last:
                out_ref[pl.ds(kb * ROWS * dir_count + j, ROWS, stride=dir_count), :] = result(j, kb)
            else:
                out_ref[j, pl.ds(kb * ROWS, ROWS), :] = result(j, kb)
    if last:
        energy = jnp.sum(acc_ref[...], axis=0, keepdims=True) * (full * (1.0 / (freq_count * dir_count)))
        deal = deal_ref[...]
        cards = energy_ref.shape[0]
        card = lax.broadcasted_iota(jnp.int32, (cards, LANES), 0) * slot_count
        slot = lax.broadcasted_iota(jnp.int32, (LANES, LANES), 0)
        to_card = jnp.where((deal >= card) & (deal < card + slot_count), energy, 0.0)
        to_slot = (lax.rem(jnp.maximum(deal, 0), slot_count) == slot).astype(jnp.float32)
        energy_ref[...] = lax.dot_general(
            to_card, to_slot, (((1,), (1,)), ((), ())),
            precision=lax.Precision.HIGHEST, preferred_element_type=jnp.float32,
        )
    else:
        store_packs(result, pair_out, next_out, parity, freq_count, dir_count, edge, lane)


def coast_width(tile_count, cell_count):
    capacity = cell_count // tile_count
    spread = tile_count * (tile_count - 8) // 8
    most = -(-spread // (tile_count - 1)) * capacity
    width = ROWS
    while width < most:
        width *= 2
    return min(width, LANES)


def shards(spectrum, sea_mask, card_deal, wind):
    freq_count, dir_count, row_count, row_width = spectrum.shape
    cell_count = row_count * row_width
    tile_count = lax.axis_size("tile")
    slot_count = cell_count // 8
    edge = coast_width(tile_count, cell_count)
    here = lax.axis_index("tile")
    at_end = (here == 0) | (here == tile_count - 1)
    parity = jnp.stack([here % 2, at_end.astype(jnp.int32)])
    flat = spectrum.reshape(freq_count * dir_count, cell_count)
    mask = sea_mask.reshape(1, cell_count)
    winds = wind.reshape(2, cell_count)
    deal = card_deal.reshape(1, cell_count)
    table = jnp.asarray(tables(freq_count, dir_count))
    rows = pack_rows(dir_count, freq_count, edge)
    packed = jax.ShapeDtypeStruct((rows, LANES), jnp.float32)
    smem = pl.BlockSpec(memory_space=pltpu.SMEM)
    vmem = pl.BlockSpec(memory_space=pltpu.VMEM)
    params = pltpu.CompilerParams(vmem_limit_bytes=48 * 1024 * 1024)
    padded = pltpu.VMEM((dir_count, freq_count + 2 * PAD, LANES), jnp.float32)
    plain = pltpu.VMEM((dir_count, freq_count, LANES), jnp.float32)
    column = pltpu.VMEM((freq_count, LANES), jnp.float32)
    scratch = [padded, padded, padded, plain, plain, column, column, pltpu.VMEM((2, rows, LANES), jnp.float32)]

    group_count = lax.axis_size("groups")
    chip_swap = []
    for g in range(group_count):
        for i in range(tile_count):
            other, there = g, (i + 1 if i % 2 else i - 1)
            if not 0 <= there < tile_count:
                other, there = (g ^ 1 if g ^ 1 < group_count else g), i
            chip_swap.append((g * tile_count + i, other * tile_count + there))

    def exchange(pair_out, next_out):
        next_in = lax.ppermute(next_out, ("groups", "tile"), chip_swap)
        pair_in = lax.ppermute(pair_out, "tile", [(i, i ^ 1) for i in range(tile_count)])
        return pair_in, next_in

    pair_in, next_in = exchange(*pl.pallas_call(
        functools.partial(edges_kernel, freq_count, dir_count, edge),
        out_shape=(packed, packed),
        in_specs=[smem, vmem, vmem],
        out_specs=(vmem, vmem),
        compiler_params=params,
        name="edges",
    )(parity, flat, mask))
    field, pair_out, next_out = pl.pallas_call(
        functools.partial(step_kernel, freq_count, dir_count, edge, slot_count, True, False),
        out_shape=(jax.ShapeDtypeStruct((dir_count, freq_count, LANES), jnp.float32), packed, packed),
        in_specs=[smem] + [vmem] * 6,
        out_specs=(vmem,) * 3,
        scratch_shapes=scratch,
        compiler_params=params,
        name="first_step",
    )(parity, flat, mask, winds, table, pair_in, next_in)
    pair_in, next_in = exchange(pair_out, next_out)
    out, energy = pl.pallas_call(
        functools.partial(step_kernel, freq_count, dir_count, edge, slot_count, False, True),
        out_shape=(
            jax.ShapeDtypeStruct((freq_count * dir_count, LANES), jnp.float32),
            jax.ShapeDtypeStruct((tile_count, LANES), jnp.float32),
        ),
        in_specs=[smem] + [vmem] * 7,
        out_specs=(vmem,) * 2,
        scratch_shapes=scratch,
        compiler_params=params,
        name="second_step",
    )(parity, field, mask, winds, table, pair_in, next_in, deal)
    shared = lax.all_to_all(
        energy.reshape(tile_count, 1, LANES), "tile", split_axis=0, concat_axis=0, tiled=True
    )
    card_energy = jnp.sum(shared, axis=(0, 1))[:slot_count]
    return out.reshape(freq_count, dir_count, row_count, row_width), card_energy


def solution(mesh):
    placed = (
        P(None, None, ("groups", "tile"), None),
        P(("groups", "tile"), None),
        P(("groups", "tile"), None),
        P(None, ("groups", "tile"), None),
    )
    return jax.shard_map(
        shards,
        mesh=mesh,
        in_specs=placed,
        out_specs=(P(None, None, ("groups", "tile"), None), P(("groups", "tile"))),
        check_vma=False,
    )
```

```python
import functools
import math

import jax
import jax.numpy as jnp
import numpy as np
from jax import lax
from jax.experimental import pallas as pl
from jax.experimental.pallas import tpu as pltpu
from jax.sharding import PartitionSpec as P

STEPS = 2
SUB = 8
COURANT_TOP = 0.7
WIND_RATE = 0.15
DECAY_RATE = 0.3
QUAD_RATE = 0.5
LIMITER = 0.25
ANGLE_UP = -11.48
ANGLE_DOWN = 33.56
SHIFT_UP = math.log(1.25) / math.log(1.1)
SHIFT_DOWN = math.log(0.75) / math.log(1.1)
GAIN_UP = 1.25 ** (-4)
GAIN_DOWN = 0.75 ** (-4)
GAIN_BOTH = 0.9375 ** (-4)

LANES = 128
ROWS = 8
PAD = 4


def split(offset):
    base = math.floor(offset)
    return base, offset - base


GAIN = 2.0 * GAIN_BOTH / (GAIN_UP * GAIN_DOWN)
UP_K, UP_W = split(SHIFT_UP)
DOWN_K, DOWN_W = split(SHIFT_DOWN)

COAST = 16
NEAR = 42
REST = 14
FAR = COAST + REST + NEAR


class Pack:
    def __init__(self, blocks, width, dir_count, offset):
        self.blocks, self.width, self.offset = blocks, width, offset
        self.slabs = dir_count // blocks
        self.dir_count = dir_count

    def direction(self, block, slab):
        return (block * self.slabs + slab + self.offset) % self.dir_count

    def find(self, j):
        return divmod((j - self.offset) % self.dir_count, self.slabs)

    def next_block(self, value, lane):
        last = (self.blocks - 1) * self.width
        ahead = turn(value, -self.width)
        if self.blocks * self.width == LANES:
            return ahead
        return jnp.where(lane < last, ahead, turn(value, last))

    def block_before(self, value, lane):
        last = (self.blocks - 1) * self.width
        behind = turn(value, self.width)
        if self.blocks * self.width == LANES:
            return behind
        return jnp.where(lane >= self.width, behind, turn(value, -last))

    def over_blocks(self, value, lane):
        if self.blocks == 4:
            value = value + turn(value, 2 * self.width)
            return value + turn(value, self.width)
        total = value
        for b in range(1, self.blocks):
            total = total + turn(value, -b * self.width)
        spread = total
        for b in range(1, self.blocks):
            spread = jnp.where(lane >= b * self.width, turn(total, b * self.width), spread)
        return spread

    def rows(self):
        angles = 2.0 * math.pi * np.arange(self.dir_count) / self.dir_count
        out = np.zeros((4, 16, LANES))
        for r in range(self.slabs):
            for b in range(self.blocks):
                at = slice(b * self.width, (b + 1) * self.width)
                angle = angles[self.direction(b, r)]
                out[:, r, at] = np.array(
                    [math.cos(angle), math.sin(angle), abs(math.cos(angle)), abs(math.sin(angle))]
                )[:, None]
        return out.astype(np.float32)


def turn(value, by):
    by %= LANES
    return pltpu.roll(value, by, 1) if by else value


def lanes():
    return lax.broadcasted_iota(jnp.int32, (ROWS, LANES), 1)


def within(lane, first, count):
    return (lane >= first) & (lane < first + count)


def sine_up(j, dir_count):
    return math.sin(2.0 * math.pi * j / dir_count) > 0


def tables(freq_count, dir_count):
    levels = 3.0 ** (np.arange(freq_count) / (freq_count - 1))
    speeds = COURANT_TOP * 1.1 ** (-np.arange(freq_count, dtype=np.float64))
    up_j, up_z = split(ANGLE_UP * dir_count / 360.0)
    rate = (1.0 - UP_W) * up_z / LIMITER
    rows = [
        speeds,
        rate * QUAD_RATE * GAIN * GAIN * levels,
        GAIN / LIMITER * WIND_RATE * 0.5 * levels,
        GAIN / (dir_count * np.sum(levels)) * levels,
        GAIN / LIMITER * DECAY_RATE * levels,
    ]
    return np.broadcast_to(
        np.stack(rows)[:, :, None], (len(rows), freq_count, LANES)
    ).astype(np.float32)


def clear(ref, slabs, freq_count):
    zero = jnp.zeros((PAD, LANES), jnp.float32)
    for r in range(slabs):
        ref[r, pl.ds(0, PAD), :] = zero
        ref[r, pl.ds(PAD + freq_count, PAD), :] = zero


def set_wind(pack, freq_count, table_ref, angle_ref, aux, w_ref):
    for r in range(pack.slabs):
        drive = aux[0:1] * angle_ref[0, r:r + 1, :] + aux[1:2] * angle_ref[1, r:r + 1, :]
        for kb in range(freq_count // ROWS):
            at = pl.ds(kb * ROWS, ROWS)
            w_ref[r, at, :] = jnp.maximum(table_ref[2, at, :] * drive - GAIN / LIMITER * WIND_RATE, 0.0)


def sub_steps(pack, freq_count, table_ref, e_ref, u_ref, d_ref, n_ref, w_ref, acc_ref, c_ref):
    slabs, blocks = pack.slabs, freq_count // ROWS
    lane = lanes()
    up_j, up_z = split(ANGLE_UP * pack.dir_count / 360.0)
    down_j, down_z = split(ANGLE_DOWN * pack.dir_count / 360.0)
    up_near, up_far = up_j + 1, up_j
    up_weight, up_rest = up_z, (1.0 - up_z) / up_z
    down_near, down_far = down_j, down_j + 1
    down_weight, down_rest = 1.0 - down_z, down_z / (1.0 - down_z)
    up_scale = GAIN_UP * GAIN * up_weight
    down_scale = GAIN_DOWN * GAIN * down_weight
    fold = (1.0 - UP_W) * up_weight
    up_tail = UP_W / (1.0 - UP_W)
    down_head = (1.0 - DOWN_W) * down_weight / fold
    down_tail = DOWN_W * down_weight / fold
    own = -2.0 / fold

    def around(known, make, r):
        if r not in known:
            if r < 0:
                known[r] = pack.block_before(around(known, make, r + slabs), lane)
            elif r >= slabs:
                known[r] = pack.next_block(around(known, make, r - slabs), lane)
            else:
                known[r] = make(r)
        return known[r]

    def stage_a(kb):
        base = kb * ROWS
        strength = table_ref[1, pl.ds(base, ROWS), :]
        up, down, more, less, up_c, down_c = {}, {}, {}, {}, {}, {}

        def read(r, offset):
            return e_ref[r, pl.ds(base + PAD + offset, ROWS), :]

        def make_up(r):
            return (up_scale * (1.0 - UP_W)) * read(r, UP_K) + (up_scale * UP_W) * read(r, UP_K + 1)

        def make_down(r):
            return (down_scale * (1.0 - DOWN_W)) * read(r, DOWN_K) + (down_scale * DOWN_W) * read(r, DOWN_K + 1)

        def get_up(r):
            return around(up, make_up, r)

        def get_down(r):
            return around(down, make_down, r)

        def get_up_c(r):
            if r not in up_c:
                up_c[r] = get_up(r) * up_rest
            return up_c[r]

        def get_down_c(r):
            if r not in down_c:
                down_c[r] = get_down(r) * down_rest
            return down_c[r]

        def make_quad(r, sign):
            here = read(r, 0)
            plus = get_up(r + sign * up_near) + get_up_c(r + sign * up_far)
            minus = get_down(r + sign * down_near) + get_down_c(r + sign * down_far)
            return (here * strength) * (here * (plus + minus) - plus * minus)

        def get_more(r):
            return around(more, lambda r: make_quad(r, 1), r)

        def get_less(r):
            return around(less, lambda r: make_quad(r, -1), r)

        for r in range(slabs):
            u_ref[r, pl.ds(base + PAD, ROWS), :] = (
                get_more(r - up_near) + get_less(r + up_near)
            ) + up_rest * (get_more(r - up_far) + get_less(r + up_far))
            d_ref[r, pl.ds(base + PAD, ROWS), :] = (
                get_more(r - down_near) + get_less(r + down_near)
            ) + down_rest * (get_more(r - down_far) + get_less(r + down_far))
            n_ref[r, pl.ds(base, ROWS), :] = own * (get_more(r) + get_less(r))

    def stage_b(kb):
        base = kb * ROWS
        decay = c_ref[pl.ds(base, ROWS), :]
        total = jnp.zeros((ROWS, LANES), jnp.float32)
        for r in range(slabs):
            here = e_ref[r, pl.ds(base + PAD, ROWS), :]
            rate = here * (w_ref[r, pl.ds(base, ROWS), :] - decay) + n_ref[r, pl.ds(base, ROWS), :]
            rate = rate + (
                u_ref[r, pl.ds(base + PAD - UP_K, ROWS), :]
                + up_tail * u_ref[r, pl.ds(base + PAD - UP_K - 1, ROWS), :]
            )
            rate = rate + (
                down_head * d_ref[r, pl.ds(base + PAD - DOWN_K, ROWS), :]
                + down_tail * d_ref[r, pl.ds(base + PAD - DOWN_K - 1, ROWS), :]
            )
            here = here + (LIMITER / SUB / GAIN) * jnp.tanh(rate)
            e_ref[r, pl.ds(base + PAD, ROWS), :] = here
            total = total + here
        acc_ref[pl.ds(base, ROWS), :] = total

    def sub_step(index, carry):
        steepness = jnp.sum(acc_ref[...] * table_ref[3], axis=0, keepdims=True)
        steepness = pack.over_blocks(jnp.broadcast_to(steepness, (ROWS, LANES)), lane)[0:1]
        c_ref[...] = steepness * table_ref[4]
        for kb in range(blocks):
            stage_a(kb)
        for kb in range(blocks):
            stage_b(kb)
        return carry

    lax.fori_loop(0, SUB, sub_step, 0)


def slab_at(r, kb, freq_count):
    return pl.ds(r * freq_count + kb * ROWS, ROWS)


SQUEEZE = (0, COAST, 4 * COAST, 5 * COAST)


def flow_mask(lane, width, wanted):
    block = lane // width
    forward = ((block == 0) | (block == 3)).astype(jnp.int32)
    return (forward == wanted) & (lane % width < COAST)


def squeeze(fetch, count, chosen):
    out = []
    for start in range(0, count, len(SQUEEZE)):
        total = None
        for i in range(start, min(count, start + len(SQUEEZE))):
            value = turn(jnp.where(chosen, fetch(i), 0.0), SQUEEZE[i - start])
            total = value if total is None else total + value
        out.append(total)
    return out


def loosen(ref, i):
    g, part = divmod(i, len(SQUEEZE))
    return turn(ref[pl.ds(g * ROWS, ROWS), :], -SQUEEZE[part])


def spread_kernel(
    one, two, freq_count, code_ref, spec_hbm, mask_hbm, wind_hbm, deal_hbm, table_ref,
    one_own, one_send, two_own, two_send, cross_ref, row_ref,
    spec_ref, mask_ref, wind_ref, deal_ref, moved_ref, sems,
):
    dir_count = one.dir_count
    blocks = freq_count // ROWS
    copies = [
        pltpu.make_async_copy(src, dst, sems.at[i])
        for i, (src, dst) in enumerate(
            [(mask_hbm, mask_ref), (wind_hbm, wind_ref), (deal_hbm, deal_ref), (spec_hbm, spec_ref)]
        )
    ]
    for copy in copies:
        copy.start()
    for copy in copies:
        copy.wait()
    lane = lanes()
    mask = mask_ref[...].astype(jnp.float32)
    half = mask * (1.0 / GAIN)
    parity = code_ref[0] % 2
    angles = 2.0 * math.pi * np.arange(dir_count) / dir_count

    aux = jnp.concatenate(
        [
            wind_ref[...] * mask,
            (deal_ref[...] + 1).astype(jnp.float32) * mask,
            mask,
            jnp.zeros((ROWS - 4, LANES), jnp.float32),
        ],
        axis=0,
    )
    row_ref[...] = jnp.concatenate(
        [mask, jnp.broadcast_to(mask[:, LANES - 1:LANES], (1, LANES)), jnp.zeros((ROWS - 2, LANES), jnp.float32)], axis=0
    )

    def pack_row(pack, values, first, slot, count):
        total = None
        for b, value in enumerate(values):
            at = b * pack.width + slot
            value = turn(value, at - first)
            keep = within(lane, at, count)
            total = jnp.where(keep, value, 0.0 if total is None else total)
        return total

    def put_aux(ref, pack, first, slot, count):
        ref[pl.ds(pack.slabs * freq_count, ROWS), :] = pack_row(pack, [aux] * pack.blocks, first, slot, count)

    put_aux(one_own, one, COAST + REST, 0, NEAR)
    put_aux(one_send, one, FAR, 0, NEAR)
    put_aux(two_own, two, 0, 0, COAST + REST)
    put_aux(two_send, two, FAR + NEAR, COAST, REST)

    def field(j, kb):
        return spec_ref[pl.ds(kb * ROWS * dir_count + j, ROWS, stride=dir_count), :] * mask

    for kb in range(blocks):
        speed = table_ref[0, pl.ds(kb * ROWS, ROWS), :]

        def move(j):
            here = field(j, kb)
            if sine_up(j, dir_count):
                along = jnp.where(lane == 0, 0.0, turn(here, 1))
            else:
                along = jnp.where(lane == LANES - 1, 0.0, turn(here, -1))
            moved = (
                here
                - speed * float(abs(math.cos(angles[j]))) * here
                - speed * float(abs(math.sin(angles[j]))) * (here - along)
            ) * half
            moved_ref[j, pl.ds(kb * ROWS, ROWS), :] = moved
            return moved

        for r in range(one.slabs):
            moved = [move(one.direction(b, r)) for b in range(one.blocks)]
            at = slab_at(r, kb, freq_count)
            one_own[at, :] = pack_row(one, moved, COAST + REST, 0, NEAR)
            one_send[at, :] = pack_row(one, moved, FAR, 0, NEAR)
        for r in range(two.slabs):
            at = slab_at(r, kb, freq_count)
            chosen = [two.direction(b, r) for b in range(two.blocks)]
            raw = pack_row(two, [field(j, kb) for j in chosen], 0, 0, two.width)
            two_own[at, :] = raw
            moved = [moved_ref[j, pl.ds(kb * ROWS, ROWS), :] for j in chosen]
            sent = pack_row(two, moved, FAR + NEAR, COAST, REST)
            two_send[at, :] = jnp.where(lane % two.width < COAST, raw, sent)

    def fetch(i):
        return two_own[pl.ds(i * ROWS, ROWS), :]

    chosen = flow_mask(lane, two.width, parity)
    for g, value in enumerate(squeeze(fetch, two.slabs * blocks, chosen)):
        cross_ref[pl.ds(g * ROWS, ROWS), :] = value


def take_column(pack, fetch, slot_up, slot_down, kb, lane):
    total = jnp.zeros((ROWS, LANES), jnp.float32)
    for r in range(pack.slabs):
        value = fetch(r, kb)
        for b in range(pack.blocks):
            j = pack.direction(b, r)
            at = b * pack.width + (slot_up if sine_up(j, pack.dir_count) else slot_down)
            total = jnp.where(lane == j, turn(value, j - at), total)
    return total


def store_state(pack, freq_count, e_ref, scale, out_ref):
    for r in range(pack.slabs):
        for kb in range(freq_count // ROWS):
            out_ref[slab_at(r, kb, freq_count), :] = e_ref[r, pl.ds(PAD + kb * ROWS, ROWS), :] * scale


def one_kernel(one, freq_count, last, table_ref, angle_ref, *refs):
    if last:
        row_ref, in_ref, local_ref, column_ref, out_ref, energy_ref = refs[:6]
        scratch = refs[6:]
    else:
        own_ref, got_ref, out_ref, column_ref = refs[:4]
        scratch = refs[4:]
    e_ref, u_ref, d_ref, n_ref, w_ref, acc_ref, c_ref = scratch
    blocks = freq_count // ROWS
    lane = lanes()
    for ref in (e_ref, u_ref, d_ref):
        clear(ref, one.slabs, freq_count)
    aux_at = pl.ds(one.slabs * freq_count, ROWS)
    if last:
        aux = in_ref[aux_at, :]
        owner = jnp.broadcast_to(row_ref[1:2, :], (ROWS, LANES)) > 0.5
        up = (lane >= 1) & (lane < one.dir_count // 2 + 1)
    else:
        aux = own_ref[aux_at, :] + got_ref[aux_at, :]
        out_ref[aux_at, :] = aux
    mask = aux[3:4]
    set_wind(one, freq_count, table_ref, angle_ref, aux, w_ref)
    for kb in range(blocks):
        at = pl.ds(kb * ROWS, ROWS)
        total = jnp.zeros((ROWS, LANES), jnp.float32)
        if last:
            speed = table_ref[0, at, :]
            beyond = jnp.where(up == owner, local_ref[at, :], column_ref[at, :])
        for r in range(one.slabs):
            if last:
                here = in_ref[slab_at(r, kb, freq_count), :]
                along = jnp.where(angle_ref[1, r:r + 1, :] > 0, turn(here, 1), turn(here, -1))
                for b in range(one.blocks):
                    j = one.direction(b, r)
                    to = b * one.width + (0 if sine_up(j, one.dir_count) else NEAR - 1)
                    along = jnp.where(lane == to, turn(beyond, to - j), along)
                start = (
                    here
                    - speed * angle_ref[2, r:r + 1, :] * here
                    - speed * angle_ref[3, r:r + 1, :] * (here - along)
                ) * (mask * (1.0 / GAIN))
            else:
                start = own_ref[slab_at(r, kb, freq_count), :] + got_ref[slab_at(r, kb, freq_count), :]
            e_ref[r, pl.ds(PAD + kb * ROWS, ROWS), :] = start
            total = total + start
        acc_ref[at, :] = total
    sub_steps(one, freq_count, table_ref, e_ref, u_ref, d_ref, n_ref, w_ref, acc_ref, c_ref)
    store_state(one, freq_count, e_ref, mask * GAIN, out_ref)
    if last:
        energy = jnp.sum(acc_ref[...], axis=0, keepdims=True) * (mask * GAIN / (freq_count * one.dir_count))
        energy_ref[...] = jnp.concatenate(
            [energy, aux[2:3] - 1.0, jnp.zeros((ROWS - 2, LANES), jnp.float32)], axis=0
        )
    else:
        for kb in range(blocks):
            column_ref[pl.ds(kb * ROWS, ROWS), :] = take_column(
                one, lambda r, kb: out_ref[slab_at(r, kb, freq_count), :], NEAR - 1, 0, kb, lane
            )


def two_kernel(two, freq_count, slot_count, last, code_ref, table_ref, angle_ref, row_ref, *refs):
    if last:
        in_ref, pair_ref, cross_ref, local_ref, other_ref, out_ref, energy_ref = refs[:7]
        scratch = refs[7:]
    else:
        own_ref, got_ref, cross_ref, out_ref, column_ref, pair_out, cross_out = refs[:7]
        scratch = refs[7:]
    e_ref, u_ref, d_ref, n_ref, w_ref, acc_ref, c_ref = scratch
    blocks = freq_count // ROWS
    lane = lanes()
    slot = lane % two.width
    for ref in (e_ref, u_ref, d_ref):
        clear(ref, two.slabs, freq_count)
    aux_at = pl.ds(two.slabs * freq_count, ROWS)
    parity = code_ref[0] % 2
    inner = (code_ref[0] < 2).astype(jnp.float32)
    owner = jnp.broadcast_to(row_ref[1:2, :], (ROWS, LANES)) > 0.5
    from_cross = flow_mask(lane, two.width, 1 - parity)
    from_pair = flow_mask(lane, two.width, parity)
    if last:
        aux = in_ref[aux_at, :]
        mask = aux[3:4]
    else:
        first = own_ref[aux_at, :]
        aux = first + got_ref[aux_at, :]
        out_ref[aux_at, :] = aux
        mask = first[3:4]
    set_wind(two, freq_count, table_ref, angle_ref, aux, w_ref)
    for kb in range(blocks):
        at = pl.ds(kb * ROWS, ROWS)
        speed = table_ref[0, at, :]
        total = jnp.zeros((ROWS, LANES), jnp.float32)
        for r in range(two.slabs):
            rows = slab_at(r, kb, freq_count)
            i = r * blocks + kb
            across = loosen(cross_ref, i) * inner
            if last:
                here = in_ref[rows, :]
                beside = loosen(pair_ref, i)
            else:
                here = own_ref[rows, :]
                beside = got_ref[rows, :]
            beside = jnp.where(from_cross, across, jnp.where(from_pair, beside, 0.0))
            along = jnp.where(angle_ref[1, r:r + 1, :] > 0, turn(here, 1), turn(here, -1))
            if last:
                beyond = local_ref[at, :]
                for b in range(two.blocks):
                    j = two.direction(b, r)
                    start = b * two.width
                    if sine_up(j, two.dir_count):
                        to = start + COAST
                        along = jnp.where((lane == to) & ~owner, turn(beyond, to - j), along)
                    else:
                        to = start + COAST + REST - 1
                        along = jnp.where((lane == to) & owner, turn(beyond, to - j), along)
                        along = jnp.where((lane == start + COAST - 1) & ~owner, 0.0, along)
            else:
                along = jnp.where((slot == 0) & (angle_ref[1, r:r + 1, :] > 0), 0.0, along)
            start = (
                here
                - speed * angle_ref[2, r:r + 1, :] * (here - beside)
                - speed * angle_ref[3, r:r + 1, :] * (here - along)
            ) * (mask * (1.0 / GAIN))
            if not last:
                start = start + jnp.where(slot >= COAST, got_ref[rows, :], 0.0)
            e_ref[r, pl.ds(PAD + kb * ROWS, ROWS), :] = start
            total = total + start
        acc_ref[at, :] = total
    sub_steps(two, freq_count, table_ref, e_ref, u_ref, d_ref, n_ref, w_ref, acc_ref, c_ref)
    scale = aux[3:4] * GAIN
    store_state(two, freq_count, e_ref, scale, out_ref)
    if last:
        energy = jnp.sum(acc_ref[...], axis=0, keepdims=True) * (scale / (freq_count * two.dir_count))
        total = None
        for energy, deal in ((energy, aux[2:3] - 1.0), (other_ref[0:1], other_ref[1:2])):
            deal = deal.astype(jnp.int32)
            cards = energy_ref.shape[0]
            card = lax.broadcasted_iota(jnp.int32, (cards, LANES), 0) * slot_count
            place = lax.broadcasted_iota(jnp.int32, (LANES, LANES), 0)
            to_card = jnp.where((deal >= card) & (deal < card + slot_count), energy, 0.0)
            to_slot = (lax.rem(jnp.maximum(deal, 0), slot_count) == place).astype(jnp.float32)
            part = lax.dot_general(
                to_card, to_slot, (((1,), (1,)), ((), ())),
                precision=lax.Precision.HIGHEST, preferred_element_type=jnp.float32,
            )
            total = part if total is None else total + part
        energy_ref[...] = total
    else:
        for kb in range(blocks):
            column_ref[pl.ds(kb * ROWS, ROWS), :] = take_column(
                two, lambda r, kb: out_ref[slab_at(r, kb, freq_count), :], COAST + REST - 1, COAST, kb, lane
            )
        for ref, wanted in ((pair_out, 1 - parity), (cross_out, parity)):
            chosen = flow_mask(lane, two.width, wanted)
            for g, value in enumerate(
                squeeze(lambda i: out_ref[pl.ds(i * ROWS, ROWS), :], two.slabs * blocks, chosen)
            ):
                ref[pl.ds(g * ROWS, ROWS), :] = value


def gather_kernel(one, two, freq_count, row_ref, one_ref, one_got, two_ref, two_got, out_ref):
    dir_count = one.dir_count
    lane = lanes()
    mask = row_ref[0:1, :]
    for kb in range(freq_count // ROWS):
        for j in range(dir_count):
            b, r = one.find(j)
            at = slab_at(r, kb, freq_count)
            shift = b * one.width
            value = turn(one_ref[at, :], COAST + REST - shift)
            value = jnp.where(lane < FAR, value, turn(one_got[at, :], FAR - shift))
            b, r = two.find(j)
            at = slab_at(r, kb, freq_count)
            shift = b * two.width
            value = jnp.where(lane < COAST + REST, turn(two_ref[at, :], -shift), value)
            value = jnp.where(lane >= FAR + NEAR, turn(two_got[at, :], FAR + NEAR - COAST - shift), value)
            out_ref[pl.ds(kb * ROWS * dir_count + j, ROWS, stride=dir_count), :] = value * mask


def coast_width(tile_count, cell_count):
    capacity = cell_count // tile_count
    spread = tile_count * (tile_count - 8) // 8
    return -(-spread // (tile_count - 1)) * capacity


def shards(spectrum, sea_mask, card_deal, wind):
    freq_count, dir_count, row_count, row_width = spectrum.shape
    cell_count = row_count * row_width
    tile_count = lax.axis_size("tile")
    slot_count = cell_count // 8
    assert row_count == 1 and cell_count == LANES and coast_width(tile_count, cell_count) <= COAST
    here = lax.axis_index("tile")
    at_end = (here == 0) | (here == tile_count - 1)
    code = (here % 2 + 2 * at_end.astype(jnp.int32)).astype(jnp.int32).reshape(1)
    one, two = Pack(3, NEAR, dir_count, 0), Pack(4, 32, dir_count, 1)
    table = jnp.asarray(tables(freq_count, dir_count))
    one_rows, two_rows = one.slabs * freq_count, two.slabs * freq_count
    squeezed = -(-two_rows // ROWS // len(SQUEEZE)) * ROWS

    def array(*shape):
        return jax.ShapeDtypeStruct(shape, jnp.float32)

    smem = pl.BlockSpec(memory_space=pltpu.SMEM)
    vmem = pl.BlockSpec(memory_space=pltpu.VMEM)
    hbm = pl.BlockSpec(memory_space=pl.ANY)

    def params(elements, steps=SUB):
        work = elements * LANES * steps
        return dict(
            compiler_params=pltpu.CompilerParams(vmem_limit_bytes=48 * 1024 * 1024),
            cost_estimate=pl.CostEstimate(flops=50 * work, bytes_accessed=4 * work, transcendentals=work),
        )

    def scratch(pack):
        padded = pltpu.VMEM((pack.slabs, freq_count + 2 * PAD, LANES), jnp.float32)
        plain = pltpu.VMEM((pack.slabs, freq_count, LANES), jnp.float32)
        column = pltpu.VMEM((freq_count, LANES), jnp.float32)
        return [padded, padded, padded, plain, plain, column, column]

    group_count = lax.axis_size("groups")
    chip_swap = []
    for g in range(group_count):
        for i in range(tile_count):
            other, there = g, (i + 1 if i % 2 else i - 1)
            if not 0 <= there < tile_count:
                other, there = (g ^ 1 if g ^ 1 < group_count else g), i
            chip_swap.append((g * tile_count + i, other * tile_count + there))

    def to_pair(value):
        return lax.ppermute(value, "tile", [(i, i ^ 1) for i in range(tile_count)])

    def to_next(value):
        return lax.ppermute(value, ("groups", "tile"), chip_swap)

    one_angles, two_angles = jnp.asarray(one.rows()), jnp.asarray(two.rows())
    one_own, one_send, two_own, two_send, cross, row = pl.pallas_call(
        functools.partial(spread_kernel, one, two, freq_count),
        out_shape=(
            array(one_rows + ROWS, LANES), array(one_rows + ROWS, LANES),
            array(two_rows + ROWS, LANES), array(two_rows + ROWS, LANES),
            array(squeezed, LANES), array(ROWS, LANES),
        ),
        in_specs=[smem, hbm, hbm, hbm, hbm, vmem],
        out_specs=(vmem,) * 6,
        scratch_shapes=[
            pltpu.VMEM((freq_count * dir_count, LANES), jnp.float32),
            pltpu.VMEM((1, LANES), jnp.int32),
            pltpu.VMEM((2, LANES), jnp.float32),
            pltpu.VMEM((1, LANES), jnp.int32),
            pltpu.VMEM((dir_count, freq_count, LANES), jnp.float32),
            pltpu.SemaphoreType.DMA((4,)),
        ],
        name="spread",
        **params(1440, 1),
    )(
        code, spectrum.reshape(freq_count * dir_count, cell_count), sea_mask,
        wind.reshape(2, cell_count), card_deal, table,
    )
    one_got = to_pair(one_send)
    cross_got = to_next(cross)
    two_got = to_pair(two_send)
    one_state, one_column = pl.pallas_call(
        functools.partial(one_kernel, one, freq_count, False),
        out_shape=(array(one_rows + ROWS, LANES), array(freq_count, LANES)),
        in_specs=[vmem] * 4,
        out_specs=(vmem,) * 2,
        scratch_shapes=scratch(one),
        name="first_one",
        **params(one_rows),
    )(table, one_angles, one_own, one_got)
    column_got = to_pair(one_column)
    two_state, two_column, pair, cross = pl.pallas_call(
        functools.partial(two_kernel, two, freq_count, slot_count, False),
        out_shape=(
            array(two_rows + ROWS, LANES), array(freq_count, LANES), array(squeezed, LANES), array(squeezed, LANES),
        ),
        in_specs=[smem] + [vmem] * 6,
        out_specs=(vmem,) * 4,
        scratch_shapes=scratch(two),
        name="first_two",
        **params(two_rows),
    )(code, table, two_angles, row, two_own, two_got, cross_got)
    cross_got = to_next(cross)
    pair_got = to_pair(pair)
    one_state, one_energy = pl.pallas_call(
        functools.partial(one_kernel, one, freq_count, True),
        out_shape=(array(one_rows, LANES), array(ROWS, LANES)),
        in_specs=[vmem] * 6,
        out_specs=(vmem,) * 2,
        scratch_shapes=scratch(one),
        name="second_one",
        **params(one_rows),
    )(table, one_angles, row, one_state, two_column, column_got)
    one_got = to_pair(one_state)
    two_state, energy = pl.pallas_call(
        functools.partial(two_kernel, two, freq_count, slot_count, True),
        out_shape=(array(two_rows, LANES), array(tile_count, LANES)),
        in_specs=[smem] + [vmem] * 8,
        out_specs=(vmem,) * 2,
        scratch_shapes=scratch(two),
        name="second_two",
        **params(two_rows),
    )(code, table, two_angles, row, two_state, pair_got, cross_got, one_column, one_energy)
    two_got = to_pair(two_state)
    out = pl.pallas_call(
        functools.partial(gather_kernel, one, two, freq_count),
        out_shape=array(freq_count * dir_count, LANES),
        in_specs=[vmem] * 5,
        out_specs=vmem,
        name="gather",
        **params(1440, 1),
    )(row, one_state, one_got, two_state, two_got)
    shared = lax.all_to_all(
        energy.reshape(tile_count, 1, LANES), "tile", split_axis=0, concat_axis=0, tiled=True
    )
    card_energy = jnp.sum(shared, axis=(0, 1))[:slot_count]
    return out.reshape(freq_count, dir_count, row_count, row_width), card_energy


def solution(mesh):
    placed = (
        P(None, None, ("groups", "tile"), None),
        P(("groups", "tile"), None),
        P(("groups", "tile"), None),
        P(None, ("groups", "tile"), None),
    )
    return jax.shard_map(
        shards,
        mesh=mesh,
        in_specs=placed,
        out_specs=(P(None, None, ("groups", "tile"), None), P(("groups", "tile"))),
        check_vma=False,
    )
```

```python
import functools
import math

import jax
import jax.numpy as jnp
import numpy as np
from jax import lax
from jax.experimental import pallas as pl
from jax.experimental.pallas import tpu as pltpu
from jax.sharding import PartitionSpec as P

STEPS = 2
SUB = 8
COURANT_TOP = 0.7
WIND_RATE = 0.15
DECAY_RATE = 0.3
QUAD_RATE = 0.5
LIMITER = 0.25
ANGLE_UP = -11.48
ANGLE_DOWN = 33.56
SHIFT_UP = math.log(1.25) / math.log(1.1)
SHIFT_DOWN = math.log(0.75) / math.log(1.1)
GAIN_UP = 1.25 ** (-4)
GAIN_DOWN = 0.75 ** (-4)
GAIN_BOTH = 0.9375 ** (-4)

LANES = 128
ROWS = 8
PAD = 4


def split(offset):
    base = math.floor(offset)
    return base, offset - base


GAIN = 2.0 * GAIN_BOTH / (GAIN_UP * GAIN_DOWN)
UP_K, UP_W = split(SHIFT_UP)
DOWN_K, DOWN_W = split(SHIFT_DOWN)

COAST = 16
NEAR = 42
REST = 14
FAR = COAST + REST + NEAR


class Pack:
    def __init__(self, blocks, width, dir_count, offset):
        self.blocks, self.width, self.offset = blocks, width, offset
        self.slabs = dir_count // blocks
        self.dir_count = dir_count

    def direction(self, block, slab):
        return (block * self.slabs + slab + self.offset) % self.dir_count

    def find(self, j):
        return divmod((j - self.offset) % self.dir_count, self.slabs)

    def next_block(self, value, lane):
        if self.blocks * self.width == LANES:
            return turn(value, -self.width)
        last = (self.blocks - 1) * self.width
        return jnp.take_along_axis(value, jnp.where(lane < last, lane + self.width, lane - last), axis=1)

    def block_before(self, value, lane):
        if self.blocks * self.width == LANES:
            return turn(value, self.width)
        last = (self.blocks - 1) * self.width
        source = jnp.where(lane >= self.width, lane - self.width, lane + last)
        return jnp.take_along_axis(value, jnp.minimum(source, LANES - 1), axis=1)

    def over_blocks(self, value, lane):
        if self.blocks == 4:
            value = value + turn(value, 2 * self.width)
            return value + turn(value, self.width)
        total = value
        for b in range(1, self.blocks):
            total = total + turn(value, -b * self.width)
        spread = total
        for b in range(1, self.blocks):
            spread = jnp.where(lane >= b * self.width, turn(total, b * self.width), spread)
        return spread

    def rows(self):
        angles = 2.0 * math.pi * np.arange(self.dir_count) / self.dir_count
        out = np.zeros((4, 16, LANES))
        for r in range(self.slabs):
            for b in range(self.blocks):
                at = slice(b * self.width, (b + 1) * self.width)
                angle = angles[self.direction(b, r)]
                out[:, r, at] = np.array(
                    [math.cos(angle), math.sin(angle), abs(math.cos(angle)), abs(math.sin(angle))]
                )[:, None]
        return out.astype(np.float32)


def turn(value, by):
    by %= LANES
    return pltpu.roll(value, by, 1) if by else value


def lanes():
    return lax.broadcasted_iota(jnp.int32, (ROWS, LANES), 1)


def within(lane, first, count):
    return (lane >= first) & (lane < first + count)


def sine_up(j, dir_count):
    return math.sin(2.0 * math.pi * j / dir_count) > 0


def tables(freq_count, dir_count):
    levels = 3.0 ** (np.arange(freq_count) / (freq_count - 1))
    speeds = COURANT_TOP * 1.1 ** (-np.arange(freq_count, dtype=np.float64))
    up_j, up_z = split(ANGLE_UP * dir_count / 360.0)
    rate = (1.0 - UP_W) * up_z / LIMITER
    rows = [
        speeds,
        rate * QUAD_RATE * GAIN * GAIN * levels,
        GAIN / LIMITER * WIND_RATE * 0.5 * levels,
        GAIN / (dir_count * np.sum(levels)) * levels,
        GAIN / LIMITER * DECAY_RATE * levels,
    ]
    return np.broadcast_to(
        np.stack(rows)[:, :, None], (len(rows), freq_count, LANES)
    ).astype(np.float32)


def clear(ref, slabs, freq_count):
    zero = jnp.zeros((PAD, LANES), jnp.float32)
    for r in range(slabs):
        ref[r, pl.ds(0, PAD), :] = zero
        ref[r, pl.ds(PAD + freq_count, PAD), :] = zero


def set_wind(pack, freq_count, table_ref, angle_ref, aux, w_ref):
    for r in range(pack.slabs):
        drive = aux[0:1] * angle_ref[0, r:r + 1, :] + aux[1:2] * angle_ref[1, r:r + 1, :]
        for kb in range(freq_count // ROWS):
            at = pl.ds(kb * ROWS, ROWS)
            w_ref[r, at, :] = jnp.maximum(table_ref[2, at, :] * drive - GAIN / LIMITER * WIND_RATE, 0.0)


def sub_steps(pack, freq_count, table_ref, e_ref, u_ref, d_ref, n_ref, w_ref, acc_ref, c_ref):
    slabs, blocks = pack.slabs, freq_count // ROWS
    lane = lanes()
    up_j, up_z = split(ANGLE_UP * pack.dir_count / 360.0)
    down_j, down_z = split(ANGLE_DOWN * pack.dir_count / 360.0)
    up_near, up_far = up_j + 1, up_j
    up_weight, up_rest = up_z, (1.0 - up_z) / up_z
    down_near, down_far = down_j, down_j + 1
    down_weight, down_rest = 1.0 - down_z, down_z / (1.0 - down_z)
    up_scale = GAIN_UP * GAIN * up_weight
    down_scale = GAIN_DOWN * GAIN * down_weight
    fold = (1.0 - UP_W) * up_weight
    up_tail = UP_W / (1.0 - UP_W)
    down_head = (1.0 - DOWN_W) * down_weight / fold
    down_tail = DOWN_W * down_weight / fold
    own = -2.0 / fold

    def around(known, make, r):
        if r not in known:
            if r < 0:
                known[r] = pack.block_before(around(known, make, r + slabs), lane)
            elif r >= slabs:
                known[r] = pack.next_block(around(known, make, r - slabs), lane)
            else:
                known[r] = make(r)
        return known[r]

    def stage_a(kb):
        base = kb * ROWS
        strength = table_ref[1, pl.ds(base, ROWS), :]
        up, down, more, less, up_c, down_c = {}, {}, {}, {}, {}, {}

        def read(r, offset):
            return e_ref[r, pl.ds(base + PAD + offset, ROWS), :]

        def make_up(r):
            return (up_scale * (1.0 - UP_W)) * read(r, UP_K) + (up_scale * UP_W) * read(r, UP_K + 1)

        def make_down(r):
            return (down_scale * (1.0 - DOWN_W)) * read(r, DOWN_K) + (down_scale * DOWN_W) * read(r, DOWN_K + 1)

        def get_up(r):
            return around(up, make_up, r)

        def get_down(r):
            return around(down, make_down, r)

        def get_up_c(r):
            if r not in up_c:
                up_c[r] = get_up(r) * up_rest
            return up_c[r]

        def get_down_c(r):
            if r not in down_c:
                down_c[r] = get_down(r) * down_rest
            return down_c[r]

        def make_quad(r, sign):
            here = read(r, 0)
            plus = get_up(r + sign * up_near) + get_up_c(r + sign * up_far)
            minus = get_down(r + sign * down_near) + get_down_c(r + sign * down_far)
            return (here * strength) * (here * (plus + minus) - plus * minus)

        def get_more(r):
            return around(more, lambda r: make_quad(r, 1), r)

        def get_less(r):
            return around(less, lambda r: make_quad(r, -1), r)

        for r in range(slabs):
            u_ref[r, pl.ds(base + PAD, ROWS), :] = (
                get_more(r - up_near) + get_less(r + up_near)
            ) + up_rest * (get_more(r - up_far) + get_less(r + up_far))
            d_ref[r, pl.ds(base + PAD, ROWS), :] = (
                get_more(r - down_near) + get_less(r + down_near)
            ) + down_rest * (get_more(r - down_far) + get_less(r + down_far))
            n_ref[r, pl.ds(base, ROWS), :] = own * (get_more(r) + get_less(r))

    def stage_b(kb):
        base = kb * ROWS
        decay = c_ref[pl.ds(base, ROWS), :]
        total = jnp.zeros((ROWS, LANES), jnp.float32)
        for r in range(slabs):
            here = e_ref[r, pl.ds(base + PAD, ROWS), :]
            rate = here * (w_ref[r, pl.ds(base, ROWS), :] - decay) + n_ref[r, pl.ds(base, ROWS), :]
            rate = rate + (
                u_ref[r, pl.ds(base + PAD - UP_K, ROWS), :]
                + up_tail * u_ref[r, pl.ds(base + PAD - UP_K - 1, ROWS), :]
            )
            rate = rate + (
                down_head * d_ref[r, pl.ds(base + PAD - DOWN_K, ROWS), :]
                + down_tail * d_ref[r, pl.ds(base + PAD - DOWN_K - 1, ROWS), :]
            )
            here = here + (LIMITER / SUB / GAIN) * jnp.tanh(rate)
            e_ref[r, pl.ds(base + PAD, ROWS), :] = here
            total = total + here
        acc_ref[pl.ds(base, ROWS), :] = total

    def sub_step(index, carry):
        steepness = jnp.sum(acc_ref[...] * table_ref[3], axis=0, keepdims=True)
        steepness = pack.over_blocks(jnp.broadcast_to(steepness, (ROWS, LANES)), lane)[0:1]
        c_ref[...] = steepness * table_ref[4]
        for kb in range(blocks):
            stage_a(kb)
        for kb in range(blocks):
            stage_b(kb)
        return carry

    lax.fori_loop(0, SUB, sub_step, 0)


def slab_at(r, kb, freq_count):
    return pl.ds(r * freq_count + kb * ROWS, ROWS)


SQUEEZE = (0, COAST, 4 * COAST, 5 * COAST)


def flow_mask(lane, width, wanted):
    block = lane // width
    forward = ((block == 0) | (block == 3)).astype(jnp.int32)
    return (forward == wanted) & (lane % width < COAST)


def squeeze(fetch, count, chosen):
    out = []
    for start in range(0, count, len(SQUEEZE)):
        total = None
        for i in range(start, min(count, start + len(SQUEEZE))):
            value = turn(jnp.where(chosen, fetch(i), 0.0), SQUEEZE[i - start])
            total = value if total is None else total + value
        out.append(total)
    return out


def loosen(ref, i):
    g, part = divmod(i, len(SQUEEZE))
    return turn(ref[pl.ds(g * ROWS, ROWS), :], -SQUEEZE[part])


def spread_kernel(
    one, two, freq_count, code_ref, spec_hbm, mask_hbm, wind_hbm, deal_hbm, table_hbm,
    one_own, one_send, two_own, two_send, cross_ref, row_ref,
    spec_ref, mask_ref, wind_ref, deal_ref, table_ref, raw_ref, moved_ref, sems,
):
    dir_count = one.dir_count
    blocks = freq_count // ROWS
    chunk = ROWS * dir_count
    pairs = [(mask_hbm, mask_ref), (wind_hbm, wind_ref), (deal_hbm, deal_ref), (table_hbm, table_ref)]
    small = len(pairs)
    for kb in range(blocks):
        rows = pl.ds(kb * chunk, chunk)
        pairs.append((spec_hbm.at[rows], spec_ref.at[rows]))
    copies = [pltpu.make_async_copy(src, dst, sems.at[i]) for i, (src, dst) in enumerate(pairs)]
    for copy in copies:
        copy.start()
    for copy in copies[:small]:
        copy.wait()
    lane = lanes()
    mask = mask_ref[...].astype(jnp.float32)
    half = mask * (1.0 / GAIN)
    parity = code_ref[0] % 2
    angles = 2.0 * math.pi * np.arange(dir_count) / dir_count

    aux = jnp.concatenate(
        [
            wind_ref[...] * mask,
            (deal_ref[...] + 1).astype(jnp.float32) * mask,
            mask,
            jnp.zeros((ROWS - 4, LANES), jnp.float32),
        ],
        axis=0,
    )
    row_ref[...] = jnp.concatenate(
        [mask, jnp.broadcast_to(mask[:, LANES - 1:LANES], (1, LANES)), jnp.zeros((ROWS - 2, LANES), jnp.float32)], axis=0
    )

    def pack_row(pack, values, first, slot, count):
        total = None
        for b, value in enumerate(values):
            at = b * pack.width + slot
            value = turn(value, at - first)
            keep = within(lane, at, count)
            total = jnp.where(keep, value, 0.0 if total is None else total)
        return total

    def put_aux(ref, pack, first, slot, count):
        ref[pl.ds(pack.slabs * freq_count, ROWS), :] = pack_row(pack, [aux] * pack.blocks, first, slot, count)

    put_aux(one_own, one, COAST + REST, 0, NEAR)
    put_aux(one_send, one, FAR, 0, NEAR)
    put_aux(two_own, two, 0, 0, COAST + REST)
    put_aux(two_send, two, FAR + NEAR, COAST, REST)

    for kb in range(blocks):
        copies[small + kb].wait()
        speed = table_ref[0, pl.ds(kb * ROWS, ROWS), :]

        def move(j):
            here = spec_ref[pl.ds(kb * chunk + j, ROWS, stride=dir_count), :] * mask
            raw_ref[j] = here
            if sine_up(j, dir_count):
                along = jnp.where(lane == 0, 0.0, turn(here, 1))
            else:
                along = jnp.where(lane == LANES - 1, 0.0, turn(here, -1))
            moved = (
                here
                - speed * float(abs(math.cos(angles[j]))) * here
                - speed * float(abs(math.sin(angles[j]))) * (here - along)
            ) * half
            moved_ref[j] = moved
            return moved

        for r in range(one.slabs):
            moved = [move(one.direction(b, r)) for b in range(one.blocks)]
            at = slab_at(r, kb, freq_count)
            one_own[at, :] = pack_row(one, moved, COAST + REST, 0, NEAR)
            one_send[at, :] = pack_row(one, moved, FAR, 0, NEAR)
        for r in range(two.slabs):
            at = slab_at(r, kb, freq_count)
            chosen = [two.direction(b, r) for b in range(two.blocks)]
            raw = pack_row(two, [raw_ref[j] for j in chosen], 0, 0, two.width)
            two_own[at, :] = raw
            sent = pack_row(two, [moved_ref[j] for j in chosen], FAR + NEAR, COAST, REST)
            two_send[at, :] = jnp.where(lane % two.width < COAST, raw, sent)

    def fetch(i):
        return two_own[pl.ds(i * ROWS, ROWS), :]

    chosen = flow_mask(lane, two.width, parity)
    for g, value in enumerate(squeeze(fetch, two.slabs * blocks, chosen)):
        cross_ref[pl.ds(g * ROWS, ROWS), :] = value


def take_column(pack, fetch, slot_up, slot_down, kb, lane):
    total = jnp.zeros((ROWS, LANES), jnp.float32)
    for r in range(pack.slabs):
        value = fetch(r, kb)
        for b in range(pack.blocks):
            j = pack.direction(b, r)
            at = b * pack.width + (slot_up if sine_up(j, pack.dir_count) else slot_down)
            total = jnp.where(lane == j, turn(value, j - at), total)
    return total


def store_state(pack, freq_count, e_ref, scale, out_ref):
    for r in range(pack.slabs):
        for kb in range(freq_count // ROWS):
            out_ref[slab_at(r, kb, freq_count), :] = e_ref[r, pl.ds(PAD + kb * ROWS, ROWS), :] * scale


def one_kernel(one, freq_count, last, table_ref, angle_ref, *refs):
    if last:
        row_ref, in_ref, local_ref, column_ref, out_ref, energy_ref = refs[:6]
        scratch = refs[6:]
    else:
        own_ref, got_ref, out_ref, column_ref = refs[:4]
        scratch = refs[4:]
    e_ref, u_ref, d_ref, n_ref, w_ref, acc_ref, c_ref = scratch
    blocks = freq_count // ROWS
    lane = lanes()
    for ref in (e_ref, u_ref, d_ref):
        clear(ref, one.slabs, freq_count)
    aux_at = pl.ds(one.slabs * freq_count, ROWS)
    if last:
        aux = in_ref[aux_at, :]
        owner = jnp.broadcast_to(row_ref[1:2, :], (ROWS, LANES)) > 0.5
        up = (lane >= 1) & (lane < one.dir_count // 2 + 1)
    else:
        aux = own_ref[aux_at, :] + got_ref[aux_at, :]
        out_ref[aux_at, :] = aux
    mask = aux[3:4]
    set_wind(one, freq_count, table_ref, angle_ref, aux, w_ref)
    for kb in range(blocks):
        at = pl.ds(kb * ROWS, ROWS)
        total = jnp.zeros((ROWS, LANES), jnp.float32)
        if last:
            speed = table_ref[0, at, :]
            beyond = jnp.where(up == owner, local_ref[at, :], column_ref[at, :])
        for r in range(one.slabs):
            if last:
                here = in_ref[slab_at(r, kb, freq_count), :]
                along = jnp.where(angle_ref[1, r:r + 1, :] > 0, turn(here, 1), turn(here, -1))
                for b in range(one.blocks):
                    j = one.direction(b, r)
                    to = b * one.width + (0 if sine_up(j, one.dir_count) else NEAR - 1)
                    along = jnp.where(lane == to, turn(beyond, to - j), along)
                start = (
                    here
                    - speed * angle_ref[2, r:r + 1, :] * here
                    - speed * angle_ref[3, r:r + 1, :] * (here - along)
                ) * (mask * (1.0 / GAIN))
            else:
                start = own_ref[slab_at(r, kb, freq_count), :] + got_ref[slab_at(r, kb, freq_count), :]
            e_ref[r, pl.ds(PAD + kb * ROWS, ROWS), :] = start
            total = total + start
        acc_ref[at, :] = total
    sub_steps(one, freq_count, table_ref, e_ref, u_ref, d_ref, n_ref, w_ref, acc_ref, c_ref)
    store_state(one, freq_count, e_ref, mask * GAIN, out_ref)
    if last:
        energy = jnp.sum(acc_ref[...], axis=0, keepdims=True) * (mask * GAIN / (freq_count * one.dir_count))
        energy_ref[...] = jnp.concatenate(
            [energy, aux[2:3] - 1.0, jnp.zeros((ROWS - 2, LANES), jnp.float32)], axis=0
        )
    else:
        for kb in range(blocks):
            column_ref[pl.ds(kb * ROWS, ROWS), :] = take_column(
                one, lambda r, kb: out_ref[slab_at(r, kb, freq_count), :], NEAR - 1, 0, kb, lane
            )


def two_kernel(two, freq_count, slot_count, last, code_ref, table_ref, angle_ref, row_ref, *refs):
    if last:
        in_ref, pair_ref, cross_ref, local_ref, other_ref, out_ref, energy_ref = refs[:7]
        scratch = refs[7:]
    else:
        own_ref, got_ref, cross_ref, out_ref, column_ref, pair_out, cross_out = refs[:7]
        scratch = refs[7:]
    e_ref, u_ref, d_ref, n_ref, w_ref, acc_ref, c_ref = scratch
    blocks = freq_count // ROWS
    lane = lanes()
    slot = lane % two.width
    for ref in (e_ref, u_ref, d_ref):
        clear(ref, two.slabs, freq_count)
    aux_at = pl.ds(two.slabs * freq_count, ROWS)
    parity = code_ref[0] % 2
    inner = (code_ref[0] < 2).astype(jnp.float32)
    owner = jnp.broadcast_to(row_ref[1:2, :], (ROWS, LANES)) > 0.5
    from_cross = flow_mask(lane, two.width, 1 - parity)
    from_pair = flow_mask(lane, two.width, parity)
    if last:
        aux = in_ref[aux_at, :]
        mask = aux[3:4]
    else:
        first = own_ref[aux_at, :]
        aux = first + got_ref[aux_at, :]
        out_ref[aux_at, :] = aux
        mask = first[3:4]
    set_wind(two, freq_count, table_ref, angle_ref, aux, w_ref)
    for kb in range(blocks):
        at = pl.ds(kb * ROWS, ROWS)
        speed = table_ref[0, at, :]
        total = jnp.zeros((ROWS, LANES), jnp.float32)
        for r in range(two.slabs):
            rows = slab_at(r, kb, freq_count)
            i = r * blocks + kb
            across = loosen(cross_ref, i) * inner
            if last:
                here = in_ref[rows, :]
                beside = loosen(pair_ref, i)
            else:
                here = own_ref[rows, :]
                beside = got_ref[rows, :]
            beside = jnp.where(from_cross, across, jnp.where(from_pair, beside, 0.0))
            along = jnp.where(angle_ref[1, r:r + 1, :] > 0, turn(here, 1), turn(here, -1))
            if last:
                beyond = local_ref[at, :]
                for b in range(two.blocks):
                    j = two.direction(b, r)
                    start = b * two.width
                    if sine_up(j, two.dir_count):
                        to = start + COAST
                        along = jnp.where((lane == to) & ~owner, turn(beyond, to - j), along)
                    else:
                        to = start + COAST + REST - 1
                        along = jnp.where((lane == to) & owner, turn(beyond, to - j), along)
                        along = jnp.where((lane == start + COAST - 1) & ~owner, 0.0, along)
            else:
                along = jnp.where((slot == 0) & (angle_ref[1, r:r + 1, :] > 0), 0.0, along)
            start = (
                here
                - speed * angle_ref[2, r:r + 1, :] * (here - beside)
                - speed * angle_ref[3, r:r + 1, :] * (here - along)
            ) * (mask * (1.0 / GAIN))
            if not last:
                start = start + jnp.where(slot >= COAST, got_ref[rows, :], 0.0)
            e_ref[r, pl.ds(PAD + kb * ROWS, ROWS), :] = start
            total = total + start
        acc_ref[at, :] = total
    sub_steps(two, freq_count, table_ref, e_ref, u_ref, d_ref, n_ref, w_ref, acc_ref, c_ref)
    scale = aux[3:4] * GAIN
    store_state(two, freq_count, e_ref, scale, out_ref)
    if last:
        energy = jnp.sum(acc_ref[...], axis=0, keepdims=True) * (scale / (freq_count * two.dir_count))
        total = None
        for energy, deal in ((energy, aux[2:3] - 1.0), (other_ref[0:1], other_ref[1:2])):
            deal = deal.astype(jnp.int32)
            cards = energy_ref.shape[0]
            card = lax.broadcasted_iota(jnp.int32, (cards, LANES), 0) * slot_count
            place = lax.broadcasted_iota(jnp.int32, (LANES, LANES), 0)
            to_card = jnp.where((deal >= card) & (deal < card + slot_count), energy, 0.0)
            to_slot = (lax.rem(jnp.maximum(deal, 0), slot_count) == place).astype(jnp.float32)
            part = lax.dot_general(
                to_card, to_slot, (((1,), (1,)), ((), ())),
                precision=lax.Precision.HIGHEST, preferred_element_type=jnp.float32,
            )
            total = part if total is None else total + part
        energy_ref[...] = total
    else:
        for kb in range(blocks):
            column_ref[pl.ds(kb * ROWS, ROWS), :] = take_column(
                two, lambda r, kb: out_ref[slab_at(r, kb, freq_count), :], COAST + REST - 1, COAST, kb, lane
            )
        for ref, wanted in ((pair_out, 1 - parity), (cross_out, parity)):
            chosen = flow_mask(lane, two.width, wanted)
            for g, value in enumerate(
                squeeze(lambda i: out_ref[pl.ds(i * ROWS, ROWS), :], two.slabs * blocks, chosen)
            ):
                ref[pl.ds(g * ROWS, ROWS), :] = value


def gather_kernel(one, two, freq_count, row_ref, one_ref, one_got, two_ref, two_got, out_ref):
    dir_count = one.dir_count
    lane = lanes()
    mask = row_ref[0:1, :]
    for kb in range(freq_count // ROWS):
        for j in range(dir_count):
            b, r = one.find(j)
            at = slab_at(r, kb, freq_count)
            shift = b * one.width
            value = turn(one_ref[at, :], COAST + REST - shift)
            value = jnp.where(lane < FAR, value, turn(one_got[at, :], FAR - shift))
            b, r = two.find(j)
            at = slab_at(r, kb, freq_count)
            shift = b * two.width
            value = jnp.where(lane < COAST + REST, turn(two_ref[at, :], -shift), value)
            value = jnp.where(lane >= FAR + NEAR, turn(two_got[at, :], FAR + NEAR - COAST - shift), value)
            out_ref[pl.ds(kb * ROWS * dir_count + j, ROWS, stride=dir_count), :] = value * mask


def coast_width(tile_count, cell_count):
    capacity = cell_count // tile_count
    spread = tile_count * (tile_count - 8) // 8
    return -(-spread // (tile_count - 1)) * capacity


def shards(spectrum, sea_mask, card_deal, wind):
    freq_count, dir_count, row_count, row_width = spectrum.shape
    cell_count = row_count * row_width
    tile_count = lax.axis_size("tile")
    slot_count = cell_count // 8
    assert row_count == 1 and cell_count == LANES and coast_width(tile_count, cell_count) <= COAST
    here = lax.axis_index("tile")
    at_end = (here == 0) | (here == tile_count - 1)
    code = (here % 2 + 2 * at_end.astype(jnp.int32)).astype(jnp.int32).reshape(1)
    one, two = Pack(3, NEAR, dir_count, 0), Pack(4, 32, dir_count, 1)
    table = jnp.asarray(tables(freq_count, dir_count))
    one_rows, two_rows = one.slabs * freq_count, two.slabs * freq_count
    squeezed = -(-two_rows // ROWS // len(SQUEEZE)) * ROWS

    def array(*shape):
        return jax.ShapeDtypeStruct(shape, jnp.float32)

    smem = pl.BlockSpec(memory_space=pltpu.SMEM)
    vmem = pl.BlockSpec(memory_space=pltpu.VMEM)
    hbm = pl.BlockSpec(memory_space=pltpu.HBM)

    def params(rows, steps=SUB):
        return dict(
            compiler_params=pltpu.CompilerParams(vmem_limit_bytes=48 * 1024 * 1024),
            cost_estimate=pl.CostEstimate(
                flops=rows // ROWS * steps * 8_000_000, bytes_accessed=8 * rows * LANES, transcendentals=0
            ),
        )

    def scratch(pack):
        padded = pltpu.VMEM((pack.slabs, freq_count + 2 * PAD, LANES), jnp.float32)
        plain = pltpu.VMEM((pack.slabs, freq_count, LANES), jnp.float32)
        column = pltpu.VMEM((freq_count, LANES), jnp.float32)
        return [padded, padded, padded, plain, plain, column, column]

    group_count = lax.axis_size("groups")
    chip_swap = []
    for g in range(group_count):
        for i in range(tile_count):
            other, there = g, (i + 1 if i % 2 else i - 1)
            if not 0 <= there < tile_count:
                other, there = (g ^ 1 if g ^ 1 < group_count else g), i
            chip_swap.append((g * tile_count + i, other * tile_count + there))

    def to_pair(value):
        return lax.ppermute(value, "tile", [(i, i ^ 1) for i in range(tile_count)])

    def to_next(value):
        return lax.ppermute(value, ("groups", "tile"), chip_swap)

    one_angles, two_angles = jnp.asarray(one.rows()), jnp.asarray(two.rows())
    one_own, one_send, two_own, two_send, cross, row = pl.pallas_call(
        functools.partial(spread_kernel, one, two, freq_count),
        out_shape=(
            array(one_rows + ROWS, LANES), array(one_rows + ROWS, LANES),
            array(two_rows + ROWS, LANES), array(two_rows + ROWS, LANES),
            array(squeezed, LANES), array(ROWS, LANES),
        ),
        in_specs=[smem] + [hbm] * 5,
        out_specs=(vmem,) * 6,
        scratch_shapes=[
            pltpu.VMEM((freq_count * dir_count, LANES), jnp.float32),
            pltpu.VMEM((1, LANES), jnp.int32),
            pltpu.VMEM((2, LANES), jnp.float32),
            pltpu.VMEM((1, LANES), jnp.int32),
            pltpu.VMEM(table.shape, jnp.float32),
            pltpu.VMEM((dir_count, ROWS, LANES), jnp.float32),
            pltpu.VMEM((dir_count, ROWS, LANES), jnp.float32),
            pltpu.SemaphoreType.DMA((4 + freq_count // ROWS,)),
        ],
        name="spread",
        **params(1440, 1),
    )(
        code, spectrum.reshape(freq_count * dir_count, cell_count), sea_mask,
        wind.reshape(2, cell_count), card_deal, table,
    )
    one_got = to_pair(one_send)
    cross_got = to_next(cross)
    two_got = to_pair(two_send)
    one_state, one_column = pl.pallas_call(
        functools.partial(one_kernel, one, freq_count, False),
        out_shape=(array(one_rows + ROWS, LANES), array(freq_count, LANES)),
        in_specs=[vmem] * 4,
        out_specs=(vmem,) * 2,
        scratch_shapes=scratch(one),
        name="first_one",
        **params(one_rows),
    )(table, one_angles, one_own, one_got)
    column_got = to_pair(one_column)
    two_state, two_column, pair, cross = pl.pallas_call(
        functools.partial(two_kernel, two, freq_count, slot_count, False),
        out_shape=(
            array(two_rows + ROWS, LANES), array(freq_count, LANES), array(squeezed, LANES), array(squeezed, LANES),
        ),
        in_specs=[smem] + [vmem] * 6,
        out_specs=(vmem,) * 4,
        scratch_shapes=scratch(two),
        name="first_two",
        **params(two_rows),
    )(code, table, two_angles, row, two_own, two_got, cross_got)
    cross_got = to_next(cross)
    pair_got = to_pair(pair)
    one_state, one_energy = pl.pallas_call(
        functools.partial(one_kernel, one, freq_count, True),
        out_shape=(array(one_rows, LANES), array(ROWS, LANES)),
        in_specs=[vmem] * 6,
        out_specs=(vmem,) * 2,
        scratch_shapes=scratch(one),
        name="second_one",
        **params(one_rows),
    )(table, one_angles, row, one_state, two_column, column_got)
    one_got = to_pair(one_state)
    two_state, energy = pl.pallas_call(
        functools.partial(two_kernel, two, freq_count, slot_count, True),
        out_shape=(array(two_rows, LANES), array(tile_count, LANES)),
        in_specs=[smem] + [vmem] * 8,
        out_specs=(vmem,) * 2,
        scratch_shapes=scratch(two),
        name="second_two",
        **params(two_rows),
    )(code, table, two_angles, row, two_state, pair_got, cross_got, one_column, one_energy)
    two_got = to_pair(two_state)
    out = pl.pallas_call(
        functools.partial(gather_kernel, one, two, freq_count),
        out_shape=array(freq_count * dir_count, LANES),
        in_specs=[vmem] * 5,
        out_specs=vmem,
        name="gather",
        **params(1440, 1),
    )(row, one_state, one_got, two_state, two_got)
    shared = lax.all_to_all(
        energy.reshape(tile_count, 1, LANES), "tile", split_axis=0, concat_axis=0, tiled=True
    )
    card_energy = jnp.sum(shared, axis=(0, 1))[:slot_count]
    return out.reshape(freq_count, dir_count, row_count, row_width), card_energy


def solution(mesh):
    placed = (
        P(None, None, ("groups", "tile"), None),
        P(("groups", "tile"), None),
        P(("groups", "tile"), None),
        P(None, ("groups", "tile"), None),
    )
    return jax.shard_map(
        shards,
        mesh=mesh,
        in_specs=placed,
        out_specs=(P(None, None, ("groups", "tile"), None), P(("groups", "tile"))),
        check_vma=False,
    )
```

```python
import functools
import math

import jax
import jax.numpy as jnp
import numpy as np
from jax import lax
from jax.experimental import pallas as pl
from jax.experimental.pallas import tpu as pltpu
from jax.sharding import PartitionSpec as P

STEPS = 2
SUB = 8
COURANT_TOP = 0.7
WIND_RATE = 0.15
DECAY_RATE = 0.3
QUAD_RATE = 0.5
LIMITER = 0.25
ANGLE_UP = -11.48
ANGLE_DOWN = 33.56
SHIFT_UP = math.log(1.25) / math.log(1.1)
SHIFT_DOWN = math.log(0.75) / math.log(1.1)
GAIN_UP = 1.25 ** (-4)
GAIN_DOWN = 0.75 ** (-4)
GAIN_BOTH = 0.9375 ** (-4)

LANES = 128
ROWS = 8
PAD = 4


def split(offset):
    base = math.floor(offset)
    return base, offset - base


GAIN = 2.0 * GAIN_BOTH / (GAIN_UP * GAIN_DOWN)
STATE = SUB / LIMITER
UP_K, UP_W = split(SHIFT_UP)
DOWN_K, DOWN_W = split(SHIFT_DOWN)

COAST = 16
NEAR = 42
REST = 14
FAR = COAST + REST + NEAR


class Pack:
    def __init__(self, blocks, width, dir_count, offset):
        self.blocks, self.width, self.offset = blocks, width, offset
        self.slabs = dir_count // blocks
        self.dir_count = dir_count

    def direction(self, block, slab):
        return (block * self.slabs + slab + self.offset) % self.dir_count

    def find(self, j):
        return divmod((j - self.offset) % self.dir_count, self.slabs)

    def next_block(self, value, lane):
        if self.blocks * self.width == LANES:
            return turn(value, -self.width)
        last = (self.blocks - 1) * self.width
        return jnp.take_along_axis(value, jnp.where(lane < last, lane + self.width, lane - last), axis=1)

    def block_before(self, value, lane):
        if self.blocks * self.width == LANES:
            return turn(value, self.width)
        last = (self.blocks - 1) * self.width
        source = jnp.where(lane >= self.width, lane - self.width, lane + last)
        return jnp.take_along_axis(value, jnp.minimum(source, LANES - 1), axis=1)

    def over_blocks(self, value, lane):
        if self.blocks == 4:
            value = value + turn(value, 2 * self.width)
            return value + turn(value, self.width)
        total = value
        for b in range(1, self.blocks):
            total = total + turn(value, -b * self.width)
        spread = total
        for b in range(1, self.blocks):
            spread = jnp.where(lane >= b * self.width, turn(total, b * self.width), spread)
        return spread

    def rows(self):
        angles = 2.0 * math.pi * np.arange(self.dir_count) / self.dir_count
        out = np.zeros((4, self.slabs, LANES))
        for r in range(self.slabs):
            for b in range(self.blocks):
                at = slice(b * self.width, (b + 1) * self.width)
                angle = angles[self.direction(b, r)]
                out[:, r, at] = np.array(
                    [math.cos(angle), math.sin(angle), abs(math.cos(angle)), abs(math.sin(angle))]
                )[:, None]
        return np.broadcast_to(out[:, :, None, :], (4, self.slabs, ROWS, LANES)).astype(np.float32)


def turn(value, by):
    by %= LANES
    return pltpu.roll(value, by, 1) if by else value


def lanes():
    return lax.broadcasted_iota(jnp.int32, (ROWS, LANES), 1)


def every_row(value, row):
    return jnp.broadcast_to(value[row:row + 1, :], (ROWS, LANES))


def within(lane, first, count):
    return (lane >= first) & (lane < first + count)


def sine_up(j, dir_count):
    return math.sin(2.0 * math.pi * j / dir_count) > 0


def tables(freq_count, dir_count):
    levels = 3.0 ** (np.arange(freq_count) / (freq_count - 1))
    speeds = COURANT_TOP * 1.1 ** (-np.arange(freq_count, dtype=np.float64))
    up_j, up_z = split(ANGLE_UP * dir_count / 360.0)
    rate = (1.0 - UP_W) * up_z / LIMITER
    rows = [
        speeds,
        rate * QUAD_RATE / (GAIN * STATE ** 3) * levels,
        WIND_RATE * 0.5 / (LIMITER * STATE) * levels,
        levels / (dir_count * np.sum(levels) * STATE),
        DECAY_RATE / (LIMITER * STATE) * levels,
    ]
    return np.broadcast_to(
        np.stack(rows)[:, :, None], (len(rows), freq_count, LANES)
    ).astype(np.float32)


def clear(ref, slabs, freq_count):
    zero = jnp.zeros((PAD, LANES), jnp.float32)
    for r in range(slabs):
        ref[r, pl.ds(0, PAD), :] = zero
        ref[r, pl.ds(PAD + freq_count, PAD), :] = zero


def set_wind(pack, freq_count, table_ref, angle_ref, aux, w_ref):
    east, north = every_row(aux, 0), every_row(aux, 1)
    for r in range(pack.slabs):
        drive = east * angle_ref[0, r] + north * angle_ref[1, r]
        for kb in range(freq_count // ROWS):
            at = pl.ds(kb * ROWS, ROWS)
            w_ref[r, at, :] = jnp.maximum(table_ref[2, at, :] * drive - WIND_RATE / (LIMITER * STATE), 0.0)


def sub_steps(pack, freq_count, table_ref, e_ref, u_ref, d_ref, n_ref, w_ref, acc_ref, c_ref):
    slabs, blocks = pack.slabs, freq_count // ROWS
    lane = lanes()
    up_j, up_z = split(ANGLE_UP * pack.dir_count / 360.0)
    down_j, down_z = split(ANGLE_DOWN * pack.dir_count / 360.0)
    up_near, up_far = up_j + 1, up_j
    up_weight, up_rest = up_z, (1.0 - up_z) / up_z
    down_near, down_far = down_j, down_j + 1
    down_weight, down_rest = 1.0 - down_z, down_z / (1.0 - down_z)
    up_scale = GAIN_UP * GAIN * up_weight
    down_scale = GAIN_DOWN * GAIN * down_weight
    fold = (1.0 - UP_W) * up_weight
    up_tail = UP_W / (1.0 - UP_W)
    down_head = (1.0 - DOWN_W) * down_weight / fold
    down_tail = DOWN_W * down_weight / fold
    own = -2.0 / fold

    def around(known, make, r):
        if r not in known:
            if r < 0:
                known[r] = pack.block_before(around(known, make, r + slabs), lane)
            elif r >= slabs:
                known[r] = pack.next_block(around(known, make, r - slabs), lane)
            else:
                known[r] = make(r)
        return known[r]

    def stage_a(kb):
        base = kb * ROWS
        strength = table_ref[1, pl.ds(base, ROWS), :]
        up, down, more, less, up_c, down_c = {}, {}, {}, {}, {}, {}

        def read(r, offset):
            return e_ref[r, pl.ds(base + PAD + offset, ROWS), :]

        def make_up(r):
            return (up_scale * (1.0 - UP_W)) * read(r, UP_K) + (up_scale * UP_W) * read(r, UP_K + 1)

        def make_down(r):
            return (down_scale * (1.0 - DOWN_W)) * read(r, DOWN_K) + (down_scale * DOWN_W) * read(r, DOWN_K + 1)

        def get_up(r):
            return around(up, make_up, r)

        def get_down(r):
            return around(down, make_down, r)

        def get_up_c(r):
            if r not in up_c:
                up_c[r] = get_up(r) * up_rest
            return up_c[r]

        def get_down_c(r):
            if r not in down_c:
                down_c[r] = get_down(r) * down_rest
            return down_c[r]

        def make_quad(r, sign):
            here = read(r, 0)
            plus = get_up(r + sign * up_near) + get_up_c(r + sign * up_far)
            minus = get_down(r + sign * down_near) + get_down_c(r + sign * down_far)
            return (here * strength) * (here * (plus + minus) - plus * minus)

        def get_more(r):
            return around(more, lambda r: make_quad(r, 1), r)

        def get_less(r):
            return around(less, lambda r: make_quad(r, -1), r)

        if slabs > 9:
            for r in (slabs - 2, slabs - 1, 0, 1):
                get_up(r)
            for r in (*range(slabs - 4, slabs), *range(4)):
                get_down(r)
            for r in (-2, -1, slabs, slabs + 1):
                get_up(r)
            for r in (*range(-4, 0), *range(slabs, slabs + 4)):
                get_down(r)
            for r in (*range(slabs - 4, slabs), 0, 1):
                get_more(r)
            for r in (slabs - 2, slabs - 1, *range(4)):
                get_less(r)
            for r in (*range(-4, 0), slabs, slabs + 1):
                get_more(r)
            for r in (-2, -1, *range(slabs, slabs + 4)):
                get_less(r)
            order = (*range(4, slabs - 4), *range(4), *range(slabs - 4, slabs))
        else:
            order = range(slabs)
        for r in order:
            u_ref[r, pl.ds(base + PAD, ROWS), :] = (
                get_more(r - up_near) + get_less(r + up_near)
            ) + up_rest * (get_more(r - up_far) + get_less(r + up_far))
            d_ref[r, pl.ds(base + PAD, ROWS), :] = (
                get_more(r - down_near) + get_less(r + down_near)
            ) + down_rest * (get_more(r - down_far) + get_less(r + down_far))
            n_ref[r, pl.ds(base, ROWS), :] = own * (get_more(r) + get_less(r))

    def stage_b(kb):
        base = kb * ROWS
        decay = c_ref[pl.ds(base, ROWS), :]
        total = jnp.zeros((ROWS, LANES), jnp.float32)
        for r in range(slabs):
            here = e_ref[r, pl.ds(base + PAD, ROWS), :]
            rate = here * (w_ref[r, pl.ds(base, ROWS), :] - decay) + n_ref[r, pl.ds(base, ROWS), :]
            rate = rate + (
                u_ref[r, pl.ds(base + PAD - UP_K, ROWS), :]
                + up_tail * u_ref[r, pl.ds(base + PAD - UP_K - 1, ROWS), :]
            )
            rate = rate + (
                down_head * d_ref[r, pl.ds(base + PAD - DOWN_K, ROWS), :]
                + down_tail * d_ref[r, pl.ds(base + PAD - DOWN_K - 1, ROWS), :]
            )
            here = here + jnp.tanh(rate)
            e_ref[r, pl.ds(base + PAD, ROWS), :] = here
            total = total + here
        acc_ref[pl.ds(base, ROWS), :] = total

    def sub_step(index, carry):
        steepness = jnp.sum(acc_ref[...] * table_ref[3], axis=0, keepdims=True)
        steepness = pack.over_blocks(jnp.broadcast_to(steepness, (ROWS, LANES)), lane)[0:1]
        c_ref[...] = steepness * table_ref[4]
        for kb in range(blocks):
            stage_a(kb)
        for kb in range(blocks):
            stage_b(kb)
        return carry

    lax.fori_loop(0, SUB, sub_step, 0)


def slab_at(r, kb, freq_count):
    return pl.ds(r * freq_count + kb * ROWS, ROWS)


SQUEEZE = (0, COAST, 4 * COAST, 5 * COAST)


def flow_mask(lane, width, wanted):
    block = lane // width
    forward = ((block == 0) | (block == 3)).astype(jnp.int32)
    return (forward == wanted) & (lane % width < COAST)


def squeeze(fetch, count, chosen):
    out = []
    for start in range(0, count, len(SQUEEZE)):
        total = None
        for i in range(start, min(count, start + len(SQUEEZE))):
            value = turn(jnp.where(chosen, fetch(i), 0.0), SQUEEZE[i - start])
            total = value if total is None else total + value
        out.append(total)
    return out


def loosen(ref, i):
    g, part = divmod(i, len(SQUEEZE))
    return turn(ref[pl.ds(g * ROWS, ROWS), :], -SQUEEZE[part])


def unpack_turn(value, pack):
    return turn(value, -pack.width)


def near_kernel(one, freq_count, spec_hbm, own_ref, send_ref, spec_ref, sems):
    dir_count = one.dir_count
    blocks = freq_count // ROWS
    chunk = ROWS * dir_count
    copies = []
    for kb in range(blocks):
        rows = pl.ds(kb * chunk, chunk)
        copies.append(pltpu.make_async_copy(spec_hbm.at[rows], spec_ref.at[rows], sems.at[kb]))
        copies[kb].start()
    lane = lanes()
    angles = 2.0 * math.pi * np.arange(dir_count) / dir_count
    first = COAST + REST
    row = lax.broadcasted_iota(jnp.int32, (ROWS, LANES), 0)
    for kb in range(blocks):
        copies[kb].wait()
        speed = COURANT_TOP * STATE * jnp.exp((row + kb * ROWS).astype(jnp.float32) * (-math.log(1.1)))
        for some in range(0, one.slabs, 4):
            slabs = range(some, some + 4)
            keys = [(r, b) for r in slabs for b in range(one.blocks)]
            here = {
                (r, b): spec_ref[pl.ds(kb * chunk + one.direction(b, r), ROWS, stride=dir_count), :] for r, b in keys
            }
            along, moved = {}, {}
            for r, b in keys:
                if sine_up(one.direction(b, r), dir_count):
                    along[r, b] = turn(here[r, b], 1)
                else:
                    along[r, b] = jnp.where(lane == LANES - 1, 0.0, turn(here[r, b], -1))
            for r, b in keys:
                angle = angles[one.direction(b, r)]
                cosine, sine = float(abs(math.cos(angle))), float(abs(math.sin(angle)))
                value = here[r, b] * (STATE - speed * (cosine + sine)) + along[r, b] * (speed * sine)
                moved[r, b] = turn(value, b * one.width - first)
            own, sent = {}, {}
            for r in slabs:
                own[r] = sent[r] = moved[r, 0]
                for b in range(1, one.blocks):
                    at = b * one.width
                    ahead = (at + one.width) % LANES
                    own[r] = jnp.where(lane >= at, moved[r, b], own[r])
                    reached = lane >= ahead
                    if b == one.blocks - 1:
                        reached = reached | (lane < one.width - (LANES - ahead))
                    sent[r] = jnp.where(reached, moved[r, b], sent[r])
            sent = {r: unpack_turn(sent[r], one) for r in slabs}
            for r in slabs:
                own_ref[slab_at(r, kb, freq_count), :] = own[r]
                send_ref[slab_at(r, kb, freq_count), :] = sent[r]


def pack_aux(pack, aux, first, slot, count):
    lane = lanes()
    total = jnp.zeros((ROWS, LANES), jnp.float32)
    for b in range(pack.blocks):
        at = b * pack.width + slot
        total = jnp.where(within(lane, at, count), turn(aux, at - first), total)
    return total


def aux_kernel(one, two, mask_ref, wind_ref, deal_ref, row_ref, own_ref, send_ref):
    mask = mask_ref[...].astype(jnp.float32)
    aux = jnp.concatenate(
        [
            wind_ref[...] * mask,
            (deal_ref[...] + 1).astype(jnp.float32) * mask,
            mask,
            jnp.zeros((ROWS - 4, LANES), jnp.float32),
        ],
        axis=0,
    )
    row_ref[...] = jnp.concatenate(
        [mask, jnp.broadcast_to(mask[:, LANES - 1:LANES], (1, LANES)), jnp.zeros((ROWS - 2, LANES), jnp.float32)], axis=0
    )
    own_ref[pl.ds(0, ROWS), :] = pack_aux(one, aux, COAST + REST, 0, NEAR)
    own_ref[pl.ds(ROWS, ROWS), :] = pack_aux(two, aux, 0, 0, COAST + REST)
    send_ref[pl.ds(0, ROWS), :] = pack_aux(one, aux, FAR, 0, NEAR)
    send_ref[pl.ds(ROWS, ROWS), :] = pack_aux(two, aux, FAR + NEAR, COAST, REST)


def coast_kernel(two, freq_count, code_ref, spec_hbm, row_ref, own_ref, send_ref, cross_ref, spec_ref, sems):
    dir_count = two.dir_count
    blocks = freq_count // ROWS
    chunk = ROWS * dir_count
    copies = []
    for kb in range(blocks):
        rows = pl.ds(kb * chunk, chunk)
        copies.append(pltpu.make_async_copy(spec_hbm.at[rows], spec_ref.at[rows], sems.at[kb]))
        copies[kb].start()
    lane = lanes()
    slot = lane % two.width
    mask = every_row(row_ref[...], 0)
    for kb in range(blocks):
        copies[kb].wait()
        done = []
        for r in range(two.slabs):
            own, sent = None, None
            for b in range(two.blocks):
                j = two.direction(b, r)
                here = spec_ref[pl.ds(kb * chunk + j, ROWS, stride=dir_count), :] * mask
                here = turn(here, b * two.width)
                block = within(lane, b * two.width, two.width)
                behind = within(lane, (b - 1) % two.blocks * two.width, two.width)
                own = here if b == 0 else jnp.where(block, here, own)
                sent = here if b == 0 else jnp.where(behind, here, sent)
            done.append((own, jnp.where(slot < COAST, own, sent)))
        for r, (own, sent) in enumerate(done):
            own_ref[slab_at(r, kb, freq_count), :] = own
            send_ref[slab_at(r, kb, freq_count), :] = sent

    chosen = flow_mask(lane, two.width, code_ref[0] % 2)
    for g, value in enumerate(squeeze(lambda i: own_ref[pl.ds(i * ROWS, ROWS), :], two.slabs * blocks, chosen)):
        cross_ref[pl.ds(g * ROWS, ROWS), :] = value


def take_column(pack, fetch, slot_up, slot_down, kb, lane):
    total = jnp.zeros((ROWS, LANES), jnp.float32)
    for r in range(pack.slabs):
        value = fetch(r, kb)
        for b in range(pack.blocks):
            j = pack.direction(b, r)
            at = b * pack.width + (slot_up if sine_up(j, pack.dir_count) else slot_down)
            total = jnp.where(lane == j, turn(value, j - at), total)
    return total


def store_state(pack, freq_count, e_ref, scale, out_ref):
    for r in range(pack.slabs):
        blocks = range(freq_count // ROWS)
        done = [e_ref[r, pl.ds(PAD + kb * ROWS, ROWS), :] * scale for kb in blocks]
        for kb in blocks:
            out_ref[slab_at(r, kb, freq_count), :] = done[kb]


def one_kernel(one, freq_count, last, table_ref, angle_ref, *refs):
    if last:
        row_ref, in_ref, local_ref, column_ref, out_ref, energy_ref = refs[:6]
        scratch = refs[6:]
    else:
        row_ref, own_ref, got_ref, own_aux, got_aux, out_ref, column_ref = refs[:7]
        scratch = refs[7:]
    e_ref, u_ref, d_ref, n_ref, w_ref, acc_ref, c_ref, known_ref = scratch
    known_ref[...] = table_ref[...]
    blocks = freq_count // ROWS
    lane = lanes()
    for ref in (e_ref, u_ref, d_ref):
        clear(ref, one.slabs, freq_count)
    aux_at = pl.ds(one.slabs * freq_count, ROWS)
    owner = jnp.broadcast_to(row_ref[1:2, :], (ROWS, LANES)) > 0.5
    if last:
        aux = in_ref[aux_at, :]
        up = (lane >= 1) & (lane < one.dir_count // 2 + 1)
    else:
        aux = jnp.where(owner, own_aux[pl.ds(0, ROWS), :], got_aux[pl.ds(0, ROWS), :])
        out_ref[aux_at, :] = aux
    mask = every_row(aux, 3)
    set_wind(one, freq_count, table_ref, angle_ref, aux, w_ref)
    for kb in range(blocks):
        at = pl.ds(kb * ROWS, ROWS)
        total = jnp.zeros((ROWS, LANES), jnp.float32)
        if last:
            speed = table_ref[0, at, :]
            beyond = jnp.where(up == owner, local_ref[at, :], column_ref[at, :])
        done = []
        if last:
            state = [in_ref[slab_at(r, kb, freq_count), :] for r in range(one.slabs)]
            below = [turn(value, 1) for value in state]
            above = [turn(value, -1) for value in state]
        for r in range(one.slabs):
            if last:
                here = state[r]
                along = jnp.where(angle_ref[1, r] > 0, below[r], above[r])
                for b in range(one.blocks):
                    j = one.direction(b, r)
                    to = b * one.width + (0 if sine_up(j, one.dir_count) else NEAR - 1)
                    along = jnp.where(lane == to, turn(beyond, to - j), along)
                start = (
                    here
                    - speed * angle_ref[2, r] * here
                    - speed * angle_ref[3, r] * (here - along)
                ) * (mask * STATE)
            else:
                start = jnp.where(owner, own_ref[slab_at(r, kb, freq_count), :], got_ref[slab_at(r, kb, freq_count), :])
            done.append(start)
            total = total + start
        for r, start in enumerate(done):
            e_ref[r, pl.ds(PAD + kb * ROWS, ROWS), :] = start
        acc_ref[at, :] = total
    sub_steps(one, freq_count, known_ref, e_ref, u_ref, d_ref, n_ref, w_ref, acc_ref, c_ref)
    store_state(one, freq_count, e_ref, mask * (1.0 / STATE), out_ref)
    if last:
        energy = jnp.sum(acc_ref[...], axis=0, keepdims=True) * (mask[0:1] * (1.0 / (STATE * freq_count * one.dir_count)))
        energy_ref[...] = jnp.concatenate(
            [energy, aux[2:3] - 1.0, jnp.zeros((ROWS - 2, LANES), jnp.float32)], axis=0
        )
    else:
        for kb in range(blocks):
            column_ref[pl.ds(kb * ROWS, ROWS), :] = take_column(
                one, lambda r, kb: out_ref[slab_at(r, kb, freq_count), :], NEAR - 1, 0, kb, lane
            )


def two_kernel(two, freq_count, slot_count, last, code_ref, table_ref, angle_ref, row_ref, *refs):
    if last:
        in_ref, pair_ref, cross_ref, local_ref, other_ref, out_ref, energy_ref = refs[:7]
        scratch = refs[7:]
    else:
        own_ref, got_ref, own_aux, got_aux, cross_ref, out_ref, column_ref, pair_out, cross_out = refs[:9]
        scratch = refs[9:]
    e_ref, u_ref, d_ref, n_ref, w_ref, acc_ref, c_ref, known_ref = scratch
    known_ref[...] = table_ref[...]
    blocks = freq_count // ROWS
    lane = lanes()
    slot = lane % two.width
    for ref in (e_ref, u_ref, d_ref):
        clear(ref, two.slabs, freq_count)
    aux_at = pl.ds(two.slabs * freq_count, ROWS)
    parity = code_ref[0] % 2
    inner = (code_ref[0] < 2).astype(jnp.float32)
    owner = jnp.broadcast_to(row_ref[1:2, :], (ROWS, LANES)) > 0.5
    from_cross = flow_mask(lane, two.width, 1 - parity)
    from_pair = flow_mask(lane, two.width, parity)
    if last:
        aux = in_ref[aux_at, :]
        mask = every_row(aux, 3)
    else:
        second = pl.ds(ROWS, ROWS)
        aux = own_aux[second, :] + got_aux[second, :]
        out_ref[aux_at, :] = aux
        mask, got_mask = every_row(own_aux[second, :], 3), every_row(got_aux[second, :], 3)
    set_wind(two, freq_count, table_ref, angle_ref, aux, w_ref)
    for kb in range(blocks):
        at = pl.ds(kb * ROWS, ROWS)
        speed = table_ref[0, at, :]
        total = jnp.zeros((ROWS, LANES), jnp.float32)
        done = []
        slabs = range(two.slabs)
        upward = [angle_ref[1, r] > 0 for r in slabs]
        flow_x = [speed * angle_ref[2, r] for r in slabs]
        flow_y = [speed * angle_ref[3, r] for r in slabs]

        def neighbours(values):
            below = [turn(value, 1) for value in values]
            above = [turn(value, -1) for value in values]
            return [jnp.where(upward[r], below[r], above[r]) for r in slabs]

        here = [(in_ref if last else own_ref)[slab_at(r, kb, freq_count), :] for r in slabs]
        along = neighbours(here)
        across = [loosen(cross_ref, r * blocks + kb) * inner for r in slabs]
        if last:
            beside = [loosen(pair_ref, r * blocks + kb) for r in slabs]
        else:
            beside = [got_ref[slab_at(r, kb, freq_count), :] for r in slabs]
        for r in slabs:
            nearby = jnp.where(from_cross, across[r], jnp.where(from_pair, beside[r], 0.0))
            if last:
                beyond = local_ref[at, :]
                for b in range(two.blocks):
                    j = two.direction(b, r)
                    start = b * two.width
                    if sine_up(j, two.dir_count):
                        to = start + COAST
                        along[r] = jnp.where((lane == to) & ~owner, turn(beyond, to - j), along[r])
                    else:
                        to = start + COAST + REST - 1
                        along[r] = jnp.where((lane == to) & owner, turn(beyond, to - j), along[r])
                        along[r] = jnp.where((lane == start + COAST - 1) & ~owner, 0.0, along[r])
            else:
                along[r] = jnp.where((slot == 0) & upward[r], 0.0, along[r])
            done.append(
                (here[r] - flow_x[r] * (here[r] - nearby) - flow_y[r] * (here[r] - along[r])) * (mask * STATE)
            )
        if not last:
            here = [turn(beside[r], COAST + REST) for r in slabs]
            along = neighbours(here)
            for r in slabs:
                nearby = jnp.where((slot == COAST + REST - 1) & ~upward[r], 0.0, along[r])
                done[r] = done[r] + (
                    here[r] - flow_x[r] * here[r] - flow_y[r] * (here[r] - nearby)
                ) * (got_mask * STATE)
        for r in slabs:
            total = total + done[r]
        for r, start in enumerate(done):
            e_ref[r, pl.ds(PAD + kb * ROWS, ROWS), :] = start
        acc_ref[at, :] = total
    sub_steps(two, freq_count, known_ref, e_ref, u_ref, d_ref, n_ref, w_ref, acc_ref, c_ref)
    scale = every_row(aux, 3) * (1.0 / STATE)
    store_state(two, freq_count, e_ref, scale, out_ref)
    if last:
        energy = jnp.sum(acc_ref[...], axis=0, keepdims=True) * (scale[0:1] / (freq_count * two.dir_count))
        total = None
        for energy, deal in ((energy, aux[2:3] - 1.0), (other_ref[0:1], other_ref[1:2])):
            deal = deal.astype(jnp.int32)
            cards = energy_ref.shape[0]
            card = lax.broadcasted_iota(jnp.int32, (cards, LANES), 0) * slot_count
            place = lax.broadcasted_iota(jnp.int32, (LANES, LANES), 0)
            to_card = jnp.where((deal >= card) & (deal < card + slot_count), energy, 0.0)
            to_slot = (lax.rem(jnp.maximum(deal, 0), slot_count) == place).astype(jnp.float32)
            part = lax.dot_general(
                to_card, to_slot, (((1,), (1,)), ((), ())),
                precision=lax.Precision.HIGHEST, preferred_element_type=jnp.float32,
            )
            total = part if total is None else total + part
        energy_ref[...] = total
    else:
        for kb in range(blocks):
            column_ref[pl.ds(kb * ROWS, ROWS), :] = take_column(
                two, lambda r, kb: out_ref[slab_at(r, kb, freq_count), :], COAST + REST - 1, COAST, kb, lane
            )
        for ref, wanted in ((pair_out, 1 - parity), (cross_out, parity)):
            chosen = flow_mask(lane, two.width, wanted)
            for g, value in enumerate(
                squeeze(lambda i: out_ref[pl.ds(i * ROWS, ROWS), :], two.slabs * blocks, chosen)
            ):
                ref[pl.ds(g * ROWS, ROWS), :] = value


def gather_kernel(
    one, two, freq_count, row_ref, one_ref, one_got, two_ref, two_got, shared_ref, out_hbm, energy_ref, out_ref, sems
):
    dir_count = one.dir_count
    chunk = ROWS * dir_count
    lane = lanes()
    mask = every_row(row_ref[...], 0)
    energy_ref[...] = jnp.sum(shared_ref[...], axis=0, keepdims=True)[:, :energy_ref.shape[1]]
    copies = []
    for kb in range(freq_count // ROWS):
        near = [turn(one_got[slab_at(r, kb, freq_count), :], one.width) for r in range(one.slabs)]
        coast = [turn(two_got[slab_at(r, kb, freq_count), :], -(COAST + REST)) for r in range(two.slabs)]
        for some in range(0, dir_count, 12):
            js = range(some, some + 12)
            value, rest = {}, {}
            for j in js:
                b, r = one.find(j)
                start = b * one.width
                mixed = jnp.where(within(lane, start, one.width), one_ref[slab_at(r, kb, freq_count), :], near[r])
                value[j] = turn(mixed, COAST + REST - start)
            for j in js:
                b, r = two.find(j)
                start = b * two.width
                mixed = jnp.where(within(lane, start, COAST + REST), two_ref[slab_at(r, kb, freq_count), :], coast[r])
                rest[j] = turn(mixed, -start)
            for j in js:
                whole = jnp.where(within(lane, COAST + REST, 2 * NEAR), value[j], rest[j]) * mask
                out_ref[pl.ds(kb * chunk + j, ROWS, stride=dir_count), :] = whole
        rows = pl.ds(kb * chunk, chunk)
        copies.append(pltpu.make_async_copy(out_ref.at[rows], out_hbm.at[rows], sems.at[kb]))
        copies[kb].start()
    for copy in copies:
        copy.wait()


def coast_width(tile_count, cell_count):
    capacity = cell_count // tile_count
    spread = tile_count * (tile_count - 8) // 8
    return -(-spread // (tile_count - 1)) * capacity


def shards(spectrum, sea_mask, card_deal, wind):
    freq_count, dir_count, row_count, row_width = spectrum.shape
    cell_count = row_count * row_width
    tile_count = lax.axis_size("tile")
    slot_count = cell_count // 8
    assert row_count == 1 and cell_count == LANES and coast_width(tile_count, cell_count) <= COAST
    here = lax.axis_index("tile")
    at_end = (here == 0) | (here == tile_count - 1)
    code = (here % 2 + 2 * at_end.astype(jnp.int32)).astype(jnp.int32).reshape(1)
    one, two = Pack(3, NEAR, dir_count, 0), Pack(4, 32, dir_count, 1)
    table = jnp.asarray(tables(freq_count, dir_count))
    one_rows, two_rows = one.slabs * freq_count, two.slabs * freq_count
    squeezed = -(-two_rows // ROWS // len(SQUEEZE)) * ROWS

    def array(*shape):
        return jax.ShapeDtypeStruct(shape, jnp.float32)

    smem = pl.BlockSpec(memory_space=pltpu.SMEM)
    vmem = pl.BlockSpec(memory_space=pltpu.VMEM)
    hbm = pl.BlockSpec(memory_space=pltpu.HBM)

    def params(rows, steps=SUB, vmem=48):
        return dict(
            compiler_params=pltpu.CompilerParams(vmem_limit_bytes=vmem * 1024 * 1024),
            cost_estimate=pl.CostEstimate(
                flops=rows // ROWS * steps * 8_000_000, bytes_accessed=8 * rows * LANES, transcendentals=0
            ),
        )

    def scratch(pack):
        padded = pltpu.VMEM((pack.slabs, freq_count + 2 * PAD, LANES), jnp.float32)
        plain = pltpu.VMEM((pack.slabs, freq_count, LANES), jnp.float32)
        column = pltpu.VMEM((freq_count, LANES), jnp.float32)
        return [padded, padded, padded, plain, plain, column, column, pltpu.VMEM(table.shape, jnp.float32)]

    group_count = lax.axis_size("groups")
    chip_swap = []
    for g in range(group_count):
        for i in range(tile_count):
            other, there = g, (i + 1 if i % 2 else i - 1)
            if not 0 <= there < tile_count:
                other, there = (g ^ 1 if g ^ 1 < group_count else g), i
            chip_swap.append((g * tile_count + i, other * tile_count + there))

    def to_pair(value):
        return lax.ppermute(value, "tile", [(i, i ^ 1) for i in range(tile_count)])

    def to_next(value):
        return lax.ppermute(value, ("groups", "tile"), chip_swap)

    one_angles, two_angles = jnp.asarray(one.rows()), jnp.asarray(two.rows())
    flat = spectrum.reshape(freq_count * dir_count, cell_count)
    whole = pltpu.VMEM((freq_count * dir_count, LANES), jnp.float32)
    chunks = pltpu.SemaphoreType.DMA((freq_count // ROWS,))
    one_own, one_send = pl.pallas_call(
        functools.partial(near_kernel, one, freq_count),
        out_shape=(array(one_rows, LANES), array(one_rows, LANES)),
        in_specs=[hbm],
        out_specs=(vmem,) * 2,
        scratch_shapes=[whole, chunks],
        name="near",
        **params(1440, 1, 53),
    )(flat)
    row, own_aux, send_aux = pl.pallas_call(
        functools.partial(aux_kernel, one, two),
        out_shape=(array(ROWS, LANES), array(2 * ROWS, LANES), array(2 * ROWS, LANES)),
        in_specs=[vmem] * 3,
        out_specs=(vmem,) * 3,
        name="aux",
        **params(80, 1),
    )(sea_mask, wind.reshape(2, cell_count), card_deal)
    one_got = to_pair(one_send)
    got_aux = to_pair(send_aux)
    two_own, two_send, cross = pl.pallas_call(
        functools.partial(coast_kernel, two, freq_count),
        out_shape=(array(two_rows, LANES), array(two_rows, LANES), array(squeezed, LANES)),
        in_specs=[smem, hbm, vmem],
        out_specs=(vmem,) * 3,
        scratch_shapes=[whole, chunks],
        name="coast",
        **params(1440, 1, 53),
    )(code, flat, row)
    cross_got = to_next(cross)
    two_got = to_pair(two_send)
    one_state, one_column = pl.pallas_call(
        functools.partial(one_kernel, one, freq_count, False),
        out_shape=(array(one_rows + ROWS, LANES), array(freq_count, LANES)),
        in_specs=[vmem] * 7,
        out_specs=(vmem,) * 2,
        scratch_shapes=scratch(one),
        name="first_one",
        **params(one_rows),
    )(table, one_angles, row, one_own, one_got, own_aux, got_aux)
    column_got = to_pair(one_column)
    two_state, two_column, pair, cross = pl.pallas_call(
        functools.partial(two_kernel, two, freq_count, slot_count, False),
        out_shape=(
            array(two_rows + ROWS, LANES), array(freq_count, LANES), array(squeezed, LANES), array(squeezed, LANES),
        ),
        in_specs=[smem] + [vmem] * 8,
        out_specs=(vmem,) * 4,
        scratch_shapes=scratch(two),
        name="first_two",
        **params(two_rows),
    )(code, table, two_angles, row, two_own, two_got, own_aux, got_aux, cross_got)
    cross_got = to_next(cross)
    pair_got = to_pair(pair)
    one_state, one_energy = pl.pallas_call(
        functools.partial(one_kernel, one, freq_count, True),
        out_shape=(array(one_rows, LANES), array(ROWS, LANES)),
        in_specs=[vmem] * 6,
        out_specs=(vmem,) * 2,
        scratch_shapes=scratch(one),
        name="second_one",
        **params(one_rows),
    )(table, one_angles, row, one_state, two_column, column_got)
    one_got = to_pair(one_state)
    two_state, energy = pl.pallas_call(
        functools.partial(two_kernel, two, freq_count, slot_count, True),
        out_shape=(array(two_rows, LANES), array(tile_count, LANES)),
        in_specs=[smem] + [vmem] * 8,
        out_specs=(vmem,) * 2,
        scratch_shapes=scratch(two),
        name="second_two",
        **params(two_rows),
    )(code, table, two_angles, row, two_state, pair_got, cross_got, one_column, one_energy)
    two_got = to_pair(two_state)
    shared = lax.all_to_all(
        energy.reshape(tile_count, 1, LANES), "tile", split_axis=0, concat_axis=0, tiled=True
    )
    out, card_energy = pl.pallas_call(
        functools.partial(gather_kernel, one, two, freq_count),
        out_shape=(array(freq_count * dir_count, LANES), array(1, slot_count)),
        in_specs=[vmem] * 6,
        out_specs=(hbm, vmem),
        scratch_shapes=[whole, chunks],
        name="gather",
        **params(1440, 1),
    )(row, one_state, one_got, two_state, two_got, shared.reshape(tile_count, LANES))
    return out.reshape(freq_count, dir_count, row_count, row_width), card_energy.reshape(slot_count)


def solution(mesh):
    placed = (
        P(None, None, ("groups", "tile"), None),
        P(("groups", "tile"), None),
        P(("groups", "tile"), None),
        P(None, ("groups", "tile"), None),
    )
    return jax.shard_map(
        shards,
        mesh=mesh,
        in_specs=placed,
        out_specs=(P(None, None, ("groups", "tile"), None), P(("groups", "tile"))),
        check_vma=False,
    )
```

```python
import functools
import math

import jax
import jax.numpy as jnp
import numpy as np
from jax import lax
from jax.experimental import pallas as pl
from jax.experimental.pallas import tpu as pltpu
from jax.sharding import PartitionSpec as P

STEPS = 2
SUB = 8
COURANT_TOP = 0.7
WIND_RATE = 0.15
DECAY_RATE = 0.3
QUAD_RATE = 0.5
LIMITER = 0.25
ANGLE_UP = -11.48
ANGLE_DOWN = 33.56
SHIFT_UP = math.log(1.25) / math.log(1.1)
SHIFT_DOWN = math.log(0.75) / math.log(1.1)
GAIN_UP = 1.25 ** (-4)
GAIN_DOWN = 0.75 ** (-4)
GAIN_BOTH = 0.9375 ** (-4)

LANES = 128
ROWS = 8
PAD = 4


def split(offset):
    base = math.floor(offset)
    return base, offset - base


GAIN = 2.0 * GAIN_BOTH / (GAIN_UP * GAIN_DOWN)
STATE = SUB / LIMITER
UP_K, UP_W = split(SHIFT_UP)
DOWN_K, DOWN_W = split(SHIFT_DOWN)

COAST = 16
NEAR = 42
REST = 14
FAR = COAST + REST + NEAR


class Pack:
    def __init__(self, blocks, width, dir_count, offset):
        self.blocks, self.width, self.offset = blocks, width, offset
        self.slabs = dir_count // blocks
        self.dir_count = dir_count

    def direction(self, block, slab):
        return (block * self.slabs + slab + self.offset) % self.dir_count

    def find(self, j):
        return divmod((j - self.offset) % self.dir_count, self.slabs)

    def next_block(self, value, lane):
        if self.blocks * self.width == LANES:
            return turn(value, -self.width)
        last = (self.blocks - 1) * self.width
        return jnp.take_along_axis(value, jnp.where(lane < last, lane + self.width, lane - last), axis=1)

    def block_before(self, value, lane):
        if self.blocks * self.width == LANES:
            return turn(value, self.width)
        last = (self.blocks - 1) * self.width
        source = jnp.where(lane >= self.width, lane - self.width, lane + last)
        return jnp.take_along_axis(value, jnp.minimum(source, LANES - 1), axis=1)

    def over_blocks(self, value, lane):
        if self.blocks == 4:
            value = value + turn(value, 2 * self.width)
            return value + turn(value, self.width)
        total = value
        for b in range(1, self.blocks):
            total = total + turn(value, -b * self.width)
        spread = total
        for b in range(1, self.blocks):
            spread = jnp.where(lane >= b * self.width, turn(total, b * self.width), spread)
        return spread

    def rows(self):
        angles = 2.0 * math.pi * np.arange(self.dir_count) / self.dir_count
        out = np.zeros((4, self.slabs, LANES))
        for r in range(self.slabs):
            for b in range(self.blocks):
                at = slice(b * self.width, (b + 1) * self.width)
                angle = angles[self.direction(b, r)]
                out[:, r, at] = np.array(
                    [math.cos(angle), math.sin(angle), abs(math.cos(angle)), abs(math.sin(angle))]
                )[:, None]
        return np.broadcast_to(out[:, :, None, :], (4, self.slabs, ROWS, LANES)).astype(np.float32)


def turn(value, by):
    by %= LANES
    return pltpu.roll(value, by, 1) if by else value


def lanes():
    return lax.broadcasted_iota(jnp.int32, (ROWS, LANES), 1)


def every_row(value, row):
    return jnp.broadcast_to(value[row:row + 1, :], (ROWS, LANES))


def within(lane, first, count):
    return (lane >= first) & (lane < first + count)


def sine_up(j, dir_count):
    return math.sin(2.0 * math.pi * j / dir_count) > 0


def tables(freq_count, dir_count):
    levels = 3.0 ** (np.arange(freq_count) / (freq_count - 1))
    speeds = COURANT_TOP * 1.1 ** (-np.arange(freq_count, dtype=np.float64))
    up_j, up_z = split(ANGLE_UP * dir_count / 360.0)
    rate = (1.0 - UP_W) * up_z / LIMITER
    rows = [
        speeds,
        rate * QUAD_RATE / (GAIN * STATE ** 3) * levels,
        WIND_RATE * 0.5 / (LIMITER * STATE) * levels,
        levels / (dir_count * np.sum(levels) * STATE),
        DECAY_RATE / (LIMITER * STATE) * levels,
    ]
    return np.broadcast_to(
        np.stack(rows)[:, :, None], (len(rows), freq_count, LANES)
    ).astype(np.float32)


def clear(ref, slabs, freq_count):
    zero = jnp.zeros((PAD, LANES), jnp.float32)
    for r in range(slabs):
        ref[r, pl.ds(0, PAD), :] = zero
        ref[r, pl.ds(PAD + freq_count, PAD), :] = zero


def set_wind(pack, freq_count, table_ref, angle_ref, aux, w_ref):
    east, north = every_row(aux, 0), every_row(aux, 1)
    for r in range(pack.slabs):
        drive = east * angle_ref[0, r] + north * angle_ref[1, r]
        for kb in range(freq_count // ROWS):
            at = pl.ds(kb * ROWS, ROWS)
            w_ref[r, at, :] = jnp.maximum(table_ref[2, at, :] * drive - WIND_RATE / (LIMITER * STATE), 0.0)


def sub_steps(pack, freq_count, table_ref, e_ref, u_ref, d_ref, n_ref, w_ref, acc_ref, c_ref):
    slabs, blocks = pack.slabs, freq_count // ROWS
    lane = lanes()
    up_j, up_z = split(ANGLE_UP * pack.dir_count / 360.0)
    down_j, down_z = split(ANGLE_DOWN * pack.dir_count / 360.0)
    up_near, up_far = up_j + 1, up_j
    up_weight, up_rest = up_z, (1.0 - up_z) / up_z
    down_near, down_far = down_j, down_j + 1
    down_weight, down_rest = 1.0 - down_z, down_z / (1.0 - down_z)
    up_scale = GAIN_UP * GAIN * up_weight
    down_scale = GAIN_DOWN * GAIN * down_weight
    fold = (1.0 - UP_W) * up_weight
    up_tail = UP_W / (1.0 - UP_W)
    down_head = (1.0 - DOWN_W) * down_weight / fold
    down_tail = DOWN_W * down_weight / fold
    own = -2.0 / fold

    def around(known, make, r):
        if r not in known:
            if r < 0:
                known[r] = pack.block_before(around(known, make, r + slabs), lane)
            elif r >= slabs:
                known[r] = pack.next_block(around(known, make, r - slabs), lane)
            else:
                known[r] = make(r)
        return known[r]

    def stage_a(kb):
        base = kb * ROWS
        strength = table_ref[1, pl.ds(base, ROWS), :]
        up, down, more, less, up_c, down_c = {}, {}, {}, {}, {}, {}

        def read(r, offset):
            return e_ref[r, pl.ds(base + PAD + offset, ROWS), :]

        def make_up(r):
            return (up_scale * (1.0 - UP_W)) * read(r, UP_K) + (up_scale * UP_W) * read(r, UP_K + 1)

        def make_down(r):
            return (down_scale * (1.0 - DOWN_W)) * read(r, DOWN_K) + (down_scale * DOWN_W) * read(r, DOWN_K + 1)

        def get_up(r):
            return around(up, make_up, r)

        def get_down(r):
            return around(down, make_down, r)

        def get_up_c(r):
            if r not in up_c:
                up_c[r] = get_up(r) * up_rest
            return up_c[r]

        def get_down_c(r):
            if r not in down_c:
                down_c[r] = get_down(r) * down_rest
            return down_c[r]

        def make_quad(r, sign):
            here = read(r, 0)
            plus = get_up(r + sign * up_near) + get_up_c(r + sign * up_far)
            minus = get_down(r + sign * down_near) + get_down_c(r + sign * down_far)
            return (here * strength) * (here * (plus + minus) - plus * minus)

        def get_more(r):
            return around(more, lambda r: make_quad(r, 1), r)

        def get_less(r):
            return around(less, lambda r: make_quad(r, -1), r)

        if slabs > 9:
            for r in (slabs - 2, slabs - 1, 0, 1):
                get_up(r)
            for r in (*range(slabs - 4, slabs), *range(4)):
                get_down(r)
            for r in (-2, -1, slabs, slabs + 1):
                get_up(r)
            for r in (*range(-4, 0), *range(slabs, slabs + 4)):
                get_down(r)
            for r in (*range(slabs - 4, slabs), 0, 1):
                get_more(r)
            for r in (slabs - 2, slabs - 1, *range(4)):
                get_less(r)
            for r in (*range(-4, 0), slabs, slabs + 1):
                get_more(r)
            for r in (-2, -1, *range(slabs, slabs + 4)):
                get_less(r)
            order = (*range(4, slabs - 4), *range(4), *range(slabs - 4, slabs))
        else:
            order = range(slabs)
        for r in order:
            u_ref[r, pl.ds(base + PAD, ROWS), :] = (
                get_more(r - up_near) + get_less(r + up_near)
            ) + up_rest * (get_more(r - up_far) + get_less(r + up_far))
            d_ref[r, pl.ds(base + PAD, ROWS), :] = (
                get_more(r - down_near) + get_less(r + down_near)
            ) + down_rest * (get_more(r - down_far) + get_less(r + down_far))
            n_ref[r, pl.ds(base, ROWS), :] = own * (get_more(r) + get_less(r))

    def stage_b(kb):
        base = kb * ROWS
        decay = c_ref[pl.ds(base, ROWS), :]
        total = jnp.zeros((ROWS, LANES), jnp.float32)
        for r in range(slabs):
            here = e_ref[r, pl.ds(base + PAD, ROWS), :]
            rate = here * (w_ref[r, pl.ds(base, ROWS), :] - decay) + n_ref[r, pl.ds(base, ROWS), :]
            rate = rate + (
                u_ref[r, pl.ds(base + PAD - UP_K, ROWS), :]
                + up_tail * u_ref[r, pl.ds(base + PAD - UP_K - 1, ROWS), :]
            )
            rate = rate + (
                down_head * d_ref[r, pl.ds(base + PAD - DOWN_K, ROWS), :]
                + down_tail * d_ref[r, pl.ds(base + PAD - DOWN_K - 1, ROWS), :]
            )
            here = here + jnp.tanh(rate)
            e_ref[r, pl.ds(base + PAD, ROWS), :] = here
            total = total + here
        acc_ref[pl.ds(base, ROWS), :] = total

    def sub_step(index, carry):
        steepness = jnp.sum(acc_ref[...] * table_ref[3], axis=0, keepdims=True)
        steepness = pack.over_blocks(jnp.broadcast_to(steepness, (ROWS, LANES)), lane)[0:1]
        c_ref[...] = steepness * table_ref[4]
        for kb in range(blocks):
            stage_a(kb)
        for kb in range(blocks):
            stage_b(kb)
        return carry

    lax.fori_loop(0, SUB, sub_step, 0)


def slab_at(r, kb, freq_count):
    return pl.ds(r * freq_count + kb * ROWS, ROWS)


SQUEEZE = (0, COAST, 4 * COAST, 5 * COAST)


def flow_mask(lane, width, wanted):
    block = lane // width
    forward = ((block == 0) | (block == 3)).astype(jnp.int32)
    return (forward == wanted) & (lane % width < COAST)


def squeeze(fetch, count, chosen):
    out = []
    for start in range(0, count, len(SQUEEZE)):
        total = None
        for i in range(start, min(count, start + len(SQUEEZE))):
            value = turn(jnp.where(chosen, fetch(i), 0.0), SQUEEZE[i - start])
            total = value if total is None else total + value
        out.append(total)
    return out


def loosen(ref, i):
    g, part = divmod(i, len(SQUEEZE))
    return turn(ref[pl.ds(g * ROWS, ROWS), :], -SQUEEZE[part])


def unpack_turn(value, pack):
    return turn(value, -pack.width)


def near_kernel(one, freq_count, spec_ref, own_ref, send_ref):
    dir_count = one.dir_count
    blocks = freq_count // ROWS
    chunk = ROWS * dir_count
    lane = lanes()
    angles = 2.0 * math.pi * np.arange(dir_count) / dir_count
    first = COAST + REST
    row = lax.broadcasted_iota(jnp.int32, (ROWS, LANES), 0)
    for kb in range(blocks):
        speed = COURANT_TOP * STATE * jnp.exp((row + kb * ROWS).astype(jnp.float32) * (-math.log(1.1)))
        for some in range(0, one.slabs, 4):
            slabs = range(some, some + 4)
            keys = [(r, b) for r in slabs for b in range(one.blocks)]
            here = {
                (r, b): spec_ref[pl.ds(kb * chunk + one.direction(b, r), ROWS, stride=dir_count), :] for r, b in keys
            }
            along, moved = {}, {}
            for r, b in keys:
                if sine_up(one.direction(b, r), dir_count):
                    along[r, b] = turn(here[r, b], 1)
                else:
                    along[r, b] = jnp.where(lane == LANES - 1, 0.0, turn(here[r, b], -1))
            for r, b in keys:
                angle = angles[one.direction(b, r)]
                cosine, sine = float(abs(math.cos(angle))), float(abs(math.sin(angle)))
                value = here[r, b] * (STATE - speed * (cosine + sine)) + along[r, b] * (speed * sine)
                moved[r, b] = turn(value, b * one.width - first)
            own, sent = {}, {}
            for r in slabs:
                own[r] = sent[r] = moved[r, 0]
                for b in range(1, one.blocks):
                    at = b * one.width
                    ahead = (at + one.width) % LANES
                    own[r] = jnp.where(lane >= at, moved[r, b], own[r])
                    reached = lane >= ahead
                    if b == one.blocks - 1:
                        reached = reached | (lane < one.width - (LANES - ahead))
                    sent[r] = jnp.where(reached, moved[r, b], sent[r])
            sent = {r: unpack_turn(sent[r], one) for r in slabs}
            for r in slabs:
                own_ref[slab_at(r, kb, freq_count), :] = own[r]
                send_ref[slab_at(r, kb, freq_count), :] = sent[r]


def pack_aux(pack, aux, first, slot, count):
    lane = lanes()
    total = jnp.zeros((ROWS, LANES), jnp.float32)
    for b in range(pack.blocks):
        at = b * pack.width + slot
        total = jnp.where(within(lane, at, count), turn(aux, at - first), total)
    return total


def aux_kernel(one, two, mask_ref, wind_ref, deal_ref, row_ref, own_ref, send_ref):
    mask = mask_ref[...].astype(jnp.float32)
    aux = jnp.concatenate(
        [
            wind_ref[...] * mask,
            (deal_ref[...] + 1).astype(jnp.float32) * mask,
            mask,
            jnp.zeros((ROWS - 4, LANES), jnp.float32),
        ],
        axis=0,
    )
    row_ref[...] = jnp.concatenate(
        [mask, jnp.broadcast_to(mask[:, LANES - 1:LANES], (1, LANES)), jnp.zeros((ROWS - 2, LANES), jnp.float32)], axis=0
    )
    own_ref[pl.ds(0, ROWS), :] = pack_aux(one, aux, COAST + REST, 0, NEAR)
    own_ref[pl.ds(ROWS, ROWS), :] = pack_aux(two, aux, 0, 0, COAST + REST)
    send_ref[pl.ds(0, ROWS), :] = pack_aux(one, aux, FAR, 0, NEAR)
    send_ref[pl.ds(ROWS, ROWS), :] = pack_aux(two, aux, FAR + NEAR, COAST, REST)


def coast_kernel(two, freq_count, code_ref, spec_ref, row_ref, own_ref, send_ref, cross_ref):
    dir_count = two.dir_count
    blocks = freq_count // ROWS
    chunk = ROWS * dir_count
    lane = lanes()
    slot = lane % two.width
    mask = every_row(row_ref[...], 0)
    for kb in range(blocks):
        done = []
        for r in range(two.slabs):
            own, sent = None, None
            for b in range(two.blocks):
                j = two.direction(b, r)
                here = spec_ref[pl.ds(kb * chunk + j, ROWS, stride=dir_count), :] * mask
                here = turn(here, b * two.width)
                block = within(lane, b * two.width, two.width)
                behind = within(lane, (b - 1) % two.blocks * two.width, two.width)
                own = here if b == 0 else jnp.where(block, here, own)
                sent = here if b == 0 else jnp.where(behind, here, sent)
            done.append((own, jnp.where(slot < COAST, own, sent)))
        for r, (own, sent) in enumerate(done):
            own_ref[slab_at(r, kb, freq_count), :] = own
            send_ref[slab_at(r, kb, freq_count), :] = sent

    chosen = flow_mask(lane, two.width, code_ref[0] % 2)
    for g, value in enumerate(squeeze(lambda i: own_ref[pl.ds(i * ROWS, ROWS), :], two.slabs * blocks, chosen)):
        cross_ref[pl.ds(g * ROWS, ROWS), :] = value


def take_column(pack, fetch, slot_up, slot_down, kb, lane):
    total = jnp.zeros((ROWS, LANES), jnp.float32)
    for r in range(pack.slabs):
        value = fetch(r, kb)
        for b in range(pack.blocks):
            j = pack.direction(b, r)
            at = b * pack.width + (slot_up if sine_up(j, pack.dir_count) else slot_down)
            total = jnp.where(lane == j, turn(value, j - at), total)
    return total


def store_state(pack, freq_count, e_ref, scale, out_ref):
    for r in range(pack.slabs):
        blocks = range(freq_count // ROWS)
        done = [e_ref[r, pl.ds(PAD + kb * ROWS, ROWS), :] * scale for kb in blocks]
        for kb in blocks:
            out_ref[slab_at(r, kb, freq_count), :] = done[kb]


def one_kernel(one, freq_count, last, table_ref, angle_ref, *refs):
    if last:
        row_ref, in_ref, local_ref, column_ref, out_ref, energy_ref = refs[:6]
        scratch = refs[6:]
    else:
        row_ref, own_ref, got_ref, own_aux, got_aux, out_ref, column_ref = refs[:7]
        scratch = refs[7:]
    e_ref, u_ref, d_ref, n_ref, w_ref, acc_ref, c_ref, known_ref = scratch
    known_ref[...] = table_ref[...]
    blocks = freq_count // ROWS
    lane = lanes()
    for ref in (e_ref, u_ref, d_ref):
        clear(ref, one.slabs, freq_count)
    aux_at = pl.ds(one.slabs * freq_count, ROWS)
    owner = jnp.broadcast_to(row_ref[1:2, :], (ROWS, LANES)) > 0.5
    if last:
        aux = in_ref[aux_at, :]
        up = (lane >= 1) & (lane < one.dir_count // 2 + 1)
    else:
        aux = jnp.where(owner, own_aux[pl.ds(0, ROWS), :], got_aux[pl.ds(0, ROWS), :])
        out_ref[aux_at, :] = aux
    mask = every_row(aux, 3)
    set_wind(one, freq_count, table_ref, angle_ref, aux, w_ref)
    for kb in range(blocks):
        at = pl.ds(kb * ROWS, ROWS)
        total = jnp.zeros((ROWS, LANES), jnp.float32)
        if last:
            speed = table_ref[0, at, :]
            beyond = jnp.where(up == owner, local_ref[at, :], column_ref[at, :])
        done = []
        if last:
            state = [in_ref[slab_at(r, kb, freq_count), :] for r in range(one.slabs)]
            below = [turn(value, 1) for value in state]
            above = [turn(value, -1) for value in state]
        for r in range(one.slabs):
            if last:
                here = state[r]
                along = jnp.where(angle_ref[1, r] > 0, below[r], above[r])
                for b in range(one.blocks):
                    j = one.direction(b, r)
                    to = b * one.width + (0 if sine_up(j, one.dir_count) else NEAR - 1)
                    along = jnp.where(lane == to, turn(beyond, to - j), along)
                start = (
                    here
                    - speed * angle_ref[2, r] * here
                    - speed * angle_ref[3, r] * (here - along)
                ) * (mask * STATE)
            else:
                start = jnp.where(owner, own_ref[slab_at(r, kb, freq_count), :], got_ref[slab_at(r, kb, freq_count), :])
            done.append(start)
            total = total + start
        for r, start in enumerate(done):
            e_ref[r, pl.ds(PAD + kb * ROWS, ROWS), :] = start
        acc_ref[at, :] = total

    @pl.when(jnp.max(aux[3:4]) > 0.5)
    def _():
        sub_steps(one, freq_count, known_ref, e_ref, u_ref, d_ref, n_ref, w_ref, acc_ref, c_ref)

    store_state(one, freq_count, e_ref, mask * (1.0 / STATE), out_ref)
    if last:
        energy = jnp.sum(acc_ref[...], axis=0, keepdims=True) * (mask[0:1] * (1.0 / (STATE * freq_count * one.dir_count)))
        energy_ref[...] = jnp.concatenate(
            [energy, aux[2:3] - 1.0, jnp.zeros((ROWS - 2, LANES), jnp.float32)], axis=0
        )
    else:
        for kb in range(blocks):
            column_ref[pl.ds(kb * ROWS, ROWS), :] = take_column(
                one, lambda r, kb: out_ref[slab_at(r, kb, freq_count), :], NEAR - 1, 0, kb, lane
            )


def two_kernel(two, freq_count, slot_count, last, code_ref, table_ref, angle_ref, row_ref, *refs):
    if last:
        in_ref, pair_ref, cross_ref, local_ref, other_ref, out_ref, energy_ref = refs[:7]
        scratch = refs[7:]
    else:
        own_ref, got_ref, own_aux, got_aux, cross_ref, out_ref, column_ref, pair_out, cross_out = refs[:9]
        scratch = refs[9:]
    e_ref, u_ref, d_ref, n_ref, w_ref, acc_ref, c_ref, known_ref = scratch
    known_ref[...] = table_ref[...]
    blocks = freq_count // ROWS
    lane = lanes()
    slot = lane % two.width
    for ref in (e_ref, u_ref, d_ref):
        clear(ref, two.slabs, freq_count)
    aux_at = pl.ds(two.slabs * freq_count, ROWS)
    parity = code_ref[0] % 2
    inner = (code_ref[0] < 2).astype(jnp.float32)
    owner = jnp.broadcast_to(row_ref[1:2, :], (ROWS, LANES)) > 0.5
    from_cross = flow_mask(lane, two.width, 1 - parity)
    from_pair = flow_mask(lane, two.width, parity)
    if last:
        aux = in_ref[aux_at, :]
        mask = every_row(aux, 3)
    else:
        second = pl.ds(ROWS, ROWS)
        aux = own_aux[second, :] + got_aux[second, :]
        out_ref[aux_at, :] = aux
        mask, got_mask = every_row(own_aux[second, :], 3), every_row(got_aux[second, :], 3)
    set_wind(two, freq_count, table_ref, angle_ref, aux, w_ref)
    for kb in range(blocks):
        at = pl.ds(kb * ROWS, ROWS)
        speed = table_ref[0, at, :]
        total = jnp.zeros((ROWS, LANES), jnp.float32)
        done = []
        slabs = range(two.slabs)
        upward = [angle_ref[1, r] > 0 for r in slabs]
        flow_x = [speed * angle_ref[2, r] for r in slabs]
        flow_y = [speed * angle_ref[3, r] for r in slabs]

        def neighbours(values):
            below = [turn(value, 1) for value in values]
            above = [turn(value, -1) for value in values]
            return [jnp.where(upward[r], below[r], above[r]) for r in slabs]

        here = [(in_ref if last else own_ref)[slab_at(r, kb, freq_count), :] for r in slabs]
        along = neighbours(here)
        across = [loosen(cross_ref, r * blocks + kb) * inner for r in slabs]
        if last:
            beside = [loosen(pair_ref, r * blocks + kb) for r in slabs]
        else:
            beside = [got_ref[slab_at(r, kb, freq_count), :] for r in slabs]
        for r in slabs:
            nearby = jnp.where(from_cross, across[r], jnp.where(from_pair, beside[r], 0.0))
            if last:
                beyond = local_ref[at, :]
                for b in range(two.blocks):
                    j = two.direction(b, r)
                    start = b * two.width
                    if sine_up(j, two.dir_count):
                        to = start + COAST
                        along[r] = jnp.where((lane == to) & ~owner, turn(beyond, to - j), along[r])
                    else:
                        to = start + COAST + REST - 1
                        along[r] = jnp.where((lane == to) & owner, turn(beyond, to - j), along[r])
                        along[r] = jnp.where((lane == start + COAST - 1) & ~owner, 0.0, along[r])
            else:
                along[r] = jnp.where((slot == 0) & upward[r], 0.0, along[r])
            done.append(
                (here[r] - flow_x[r] * (here[r] - nearby) - flow_y[r] * (here[r] - along[r])) * (mask * STATE)
            )
        if not last:
            here = [turn(beside[r], COAST + REST) for r in slabs]
            along = neighbours(here)
            for r in slabs:
                nearby = jnp.where((slot == COAST + REST - 1) & ~upward[r], 0.0, along[r])
                done[r] = done[r] + (
                    here[r] - flow_x[r] * here[r] - flow_y[r] * (here[r] - nearby)
                ) * (got_mask * STATE)
        for r in slabs:
            total = total + done[r]
        for r, start in enumerate(done):
            e_ref[r, pl.ds(PAD + kb * ROWS, ROWS), :] = start
        acc_ref[at, :] = total
    sub_steps(two, freq_count, known_ref, e_ref, u_ref, d_ref, n_ref, w_ref, acc_ref, c_ref)
    scale = every_row(aux, 3) * (1.0 / STATE)
    store_state(two, freq_count, e_ref, scale, out_ref)
    if last:
        energy = jnp.sum(acc_ref[...], axis=0, keepdims=True) * (scale[0:1] / (freq_count * two.dir_count))
        total = None
        for energy, deal in ((energy, aux[2:3] - 1.0), (other_ref[0:1], other_ref[1:2])):
            deal = deal.astype(jnp.int32)
            cards = energy_ref.shape[0]
            card = lax.broadcasted_iota(jnp.int32, (cards, LANES), 0) * slot_count
            place = lax.broadcasted_iota(jnp.int32, (LANES, LANES), 0)
            to_card = jnp.where((deal >= card) & (deal < card + slot_count), energy, 0.0)
            to_slot = (lax.rem(jnp.maximum(deal, 0), slot_count) == place).astype(jnp.float32)
            part = lax.dot_general(
                to_card, to_slot, (((1,), (1,)), ((), ())),
                precision=lax.Precision.HIGHEST, preferred_element_type=jnp.float32,
            )
            total = part if total is None else total + part
        energy_ref[...] = total
    else:
        for kb in range(blocks):
            column_ref[pl.ds(kb * ROWS, ROWS), :] = take_column(
                two, lambda r, kb: out_ref[slab_at(r, kb, freq_count), :], COAST + REST - 1, COAST, kb, lane
            )
        for ref, wanted in ((pair_out, 1 - parity), (cross_out, parity)):
            chosen = flow_mask(lane, two.width, wanted)
            for g, value in enumerate(
                squeeze(lambda i: out_ref[pl.ds(i * ROWS, ROWS), :], two.slabs * blocks, chosen)
            ):
                ref[pl.ds(g * ROWS, ROWS), :] = value


def gather_kernel(
    one, two, freq_count, row_ref, one_ref, one_got, two_ref, two_got, shared_ref, out_hbm, energy_ref, out_ref, sems
):
    dir_count = one.dir_count
    chunk = ROWS * dir_count
    lane = lanes()
    mask = every_row(row_ref[...], 0)
    energy_ref[...] = jnp.sum(shared_ref[...], axis=0, keepdims=True)[:, :energy_ref.shape[1]]
    copies = []
    for kb in range(freq_count // ROWS):
        near = [turn(one_got[slab_at(r, kb, freq_count), :], one.width) for r in range(one.slabs)]
        coast = [turn(two_got[slab_at(r, kb, freq_count), :], -(COAST + REST)) for r in range(two.slabs)]
        for some in range(0, dir_count, 12):
            js = range(some, some + 12)
            value, rest = {}, {}
            for j in js:
                b, r = one.find(j)
                start = b * one.width
                mixed = jnp.where(within(lane, start, one.width), one_ref[slab_at(r, kb, freq_count), :], near[r])
                value[j] = turn(mixed, COAST + REST - start)
            for j in js:
                b, r = two.find(j)
                start = b * two.width
                mixed = jnp.where(within(lane, start, COAST + REST), two_ref[slab_at(r, kb, freq_count), :], coast[r])
                rest[j] = turn(mixed, -start)
            for j in js:
                whole = jnp.where(within(lane, COAST + REST, 2 * NEAR), value[j], rest[j]) * mask
                out_ref[pl.ds(kb * chunk + j, ROWS, stride=dir_count), :] = whole
        rows = pl.ds(kb * chunk, chunk)
        copies.append(pltpu.make_async_copy(out_ref.at[rows], out_hbm.at[rows], sems.at[kb]))
        copies[kb].start()
    for copy in copies:
        copy.wait()


def coast_width(tile_count, cell_count):
    capacity = cell_count // tile_count
    spread = tile_count * (tile_count - 8) // 8
    return -(-spread // (tile_count - 1)) * capacity


def shards(spectrum, sea_mask, card_deal, wind):
    freq_count, dir_count, row_count, row_width = spectrum.shape
    cell_count = row_count * row_width
    tile_count = lax.axis_size("tile")
    slot_count = cell_count // 8
    assert row_count == 1 and cell_count == LANES and coast_width(tile_count, cell_count) <= COAST
    here = lax.axis_index("tile")
    at_end = (here == 0) | (here == tile_count - 1)
    code = (here % 2 + 2 * at_end.astype(jnp.int32)).astype(jnp.int32).reshape(1)
    one, two = Pack(3, NEAR, dir_count, 0), Pack(4, 32, dir_count, 1)
    table = jnp.asarray(tables(freq_count, dir_count))
    one_rows, two_rows = one.slabs * freq_count, two.slabs * freq_count
    squeezed = -(-two_rows // ROWS // len(SQUEEZE)) * ROWS

    def array(*shape):
        return jax.ShapeDtypeStruct(shape, jnp.float32)

    smem = pl.BlockSpec(memory_space=pltpu.SMEM)
    vmem = pl.BlockSpec(memory_space=pltpu.VMEM)
    hbm = pl.BlockSpec(memory_space=pltpu.HBM)

    def params(rows, steps=SUB, vmem=48):
        return dict(
            compiler_params=pltpu.CompilerParams(vmem_limit_bytes=vmem * 1024 * 1024),
            cost_estimate=pl.CostEstimate(
                flops=rows // ROWS * steps * 8_000_000, bytes_accessed=8 * rows * LANES, transcendentals=0
            ),
        )

    def scratch(pack):
        padded = pltpu.VMEM((pack.slabs, freq_count + 2 * PAD, LANES), jnp.float32)
        plain = pltpu.VMEM((pack.slabs, freq_count, LANES), jnp.float32)
        column = pltpu.VMEM((freq_count, LANES), jnp.float32)
        return [padded, padded, padded, plain, plain, column, column, pltpu.VMEM(table.shape, jnp.float32)]

    group_count = lax.axis_size("groups")
    chip_swap = []
    for g in range(group_count):
        for i in range(tile_count):
            other, there = g, (i + 1 if i % 2 else i - 1)
            if not 0 <= there < tile_count:
                other, there = (g ^ 1 if g ^ 1 < group_count else g), i
            chip_swap.append((g * tile_count + i, other * tile_count + there))

    def to_pair(value):
        return lax.ppermute(value, "tile", [(i, i ^ 1) for i in range(tile_count)])

    def to_next(value):
        return lax.ppermute(value, ("groups", "tile"), chip_swap)

    one_angles, two_angles = jnp.asarray(one.rows()), jnp.asarray(two.rows())
    flat = spectrum.reshape(freq_count * dir_count, cell_count)
    whole = pltpu.VMEM((freq_count * dir_count, LANES), jnp.float32)
    chunks = pltpu.SemaphoreType.DMA((freq_count // ROWS,))
    one_own, one_send = pl.pallas_call(
        functools.partial(near_kernel, one, freq_count),
        out_shape=(array(one_rows, LANES), array(one_rows, LANES)),
        in_specs=[vmem],
        out_specs=(vmem,) * 2,
        name="near",
        **params(1440, 1),
    )(flat)
    row, own_aux, send_aux = pl.pallas_call(
        functools.partial(aux_kernel, one, two),
        out_shape=(array(ROWS, LANES), array(2 * ROWS, LANES), array(2 * ROWS, LANES)),
        in_specs=[vmem] * 3,
        out_specs=(vmem,) * 3,
        name="aux",
        **params(80, 1),
    )(sea_mask, wind.reshape(2, cell_count), card_deal)
    one_got = to_pair(one_send)
    got_aux = to_pair(send_aux)
    two_own, two_send, cross = pl.pallas_call(
        functools.partial(coast_kernel, two, freq_count),
        out_shape=(array(two_rows, LANES), array(two_rows, LANES), array(squeezed, LANES)),
        in_specs=[smem, vmem, vmem],
        out_specs=(vmem,) * 3,
        name="coast",
        **params(1440, 1),
    )(code, flat, row)
    cross_got = to_next(cross)
    two_got = to_pair(two_send)
    one_state, one_column = pl.pallas_call(
        functools.partial(one_kernel, one, freq_count, False),
        out_shape=(array(one_rows + ROWS, LANES), array(freq_count, LANES)),
        in_specs=[vmem] * 7,
        out_specs=(vmem,) * 2,
        scratch_shapes=scratch(one),
        name="first_one",
        **params(one_rows),
    )(table, one_angles, row, one_own, one_got, own_aux, got_aux)
    column_got = to_pair(one_column)
    two_state, two_column, pair, cross = pl.pallas_call(
        functools.partial(two_kernel, two, freq_count, slot_count, False),
        out_shape=(
            array(two_rows + ROWS, LANES), array(freq_count, LANES), array(squeezed, LANES), array(squeezed, LANES),
        ),
        in_specs=[smem] + [vmem] * 8,
        out_specs=(vmem,) * 4,
        scratch_shapes=scratch(two),
        name="first_two",
        **params(two_rows),
    )(code, table, two_angles, row, two_own, two_got, own_aux, got_aux, cross_got)
    cross_got = to_next(cross)
    pair_got = to_pair(pair)
    one_state, one_energy = pl.pallas_call(
        functools.partial(one_kernel, one, freq_count, True),
        out_shape=(array(one_rows, LANES), array(ROWS, LANES)),
        in_specs=[vmem] * 6,
        out_specs=(vmem,) * 2,
        scratch_shapes=scratch(one),
        name="second_one",
        **params(one_rows),
    )(table, one_angles, row, one_state, two_column, column_got)
    one_got = to_pair(one_state)
    two_state, energy = pl.pallas_call(
        functools.partial(two_kernel, two, freq_count, slot_count, True),
        out_shape=(array(two_rows, LANES), array(tile_count, LANES)),
        in_specs=[smem] + [vmem] * 8,
        out_specs=(vmem,) * 2,
        scratch_shapes=scratch(two),
        name="second_two",
        **params(two_rows),
    )(code, table, two_angles, row, two_state, pair_got, cross_got, one_column, one_energy)
    two_got = to_pair(two_state)
    shared = lax.all_to_all(
        energy.reshape(tile_count, 1, LANES), "tile", split_axis=0, concat_axis=0, tiled=True
    )
    out, card_energy = pl.pallas_call(
        functools.partial(gather_kernel, one, two, freq_count),
        out_shape=(array(freq_count * dir_count, LANES), array(1, slot_count)),
        in_specs=[vmem] * 6,
        out_specs=(hbm, vmem),
        scratch_shapes=[whole, chunks],
        name="gather",
        **params(1440, 1),
    )(row, one_state, one_got, two_state, two_got, shared.reshape(tile_count, LANES))
    return out.reshape(freq_count, dir_count, row_count, row_width), card_energy.reshape(slot_count)


def solution(mesh):
    placed = (
        P(None, None, ("groups", "tile"), None),
        P(("groups", "tile"), None),
        P(("groups", "tile"), None),
        P(None, ("groups", "tile"), None),
    )
    return jax.shard_map(
        shards,
        mesh=mesh,
        in_specs=placed,
        out_specs=(P(None, None, ("groups", "tile"), None), P(("groups", "tile"))),
        check_vma=False,
    )
```

```python
import functools
import math

import jax
import jax.numpy as jnp
import numpy as np
from jax import lax
from jax.experimental import pallas as pl
from jax.experimental.pallas import tpu as pltpu
from jax.sharding import PartitionSpec as P

STEPS = 2
SUB = 8
COURANT_TOP = 0.7
WIND_RATE = 0.15
DECAY_RATE = 0.3
QUAD_RATE = 0.5
LIMITER = 0.25
ANGLE_UP = -11.48
ANGLE_DOWN = 33.56
SHIFT_UP = math.log(1.25) / math.log(1.1)
SHIFT_DOWN = math.log(0.75) / math.log(1.1)
GAIN_UP = 1.25 ** (-4)
GAIN_DOWN = 0.75 ** (-4)
GAIN_BOTH = 0.9375 ** (-4)

LANES = 128
ROWS = 8
PAD = 4


def split(offset):
    base = math.floor(offset)
    return base, offset - base


GAIN = 2.0 * GAIN_BOTH / (GAIN_UP * GAIN_DOWN)
STATE = SUB / LIMITER
UP_K, UP_W = split(SHIFT_UP)
DOWN_K, DOWN_W = split(SHIFT_DOWN)

COAST = 16
NEAR = 42
REST = 14
FAR = COAST + REST + NEAR


class Pack:
    def __init__(self, blocks, width, dir_count, offset):
        self.blocks, self.width, self.offset = blocks, width, offset
        self.slabs = dir_count // blocks
        self.dir_count = dir_count

    def direction(self, block, slab):
        return (block * self.slabs + slab + self.offset) % self.dir_count

    def find(self, j):
        return divmod((j - self.offset) % self.dir_count, self.slabs)

    def next_block(self, value, lane):
        if self.blocks * self.width == LANES:
            return turn(value, -self.width)
        last = (self.blocks - 1) * self.width
        return jnp.take_along_axis(value, jnp.where(lane < last, lane + self.width, lane - last), axis=1)

    def block_before(self, value, lane):
        if self.blocks * self.width == LANES:
            return turn(value, self.width)
        last = (self.blocks - 1) * self.width
        source = jnp.where(lane >= self.width, lane - self.width, lane + last)
        return jnp.take_along_axis(value, jnp.minimum(source, LANES - 1), axis=1)

    def over_blocks(self, value, lane):
        if self.blocks == 4:
            value = value + turn(value, 2 * self.width)
            return value + turn(value, self.width)
        total = value
        for b in range(1, self.blocks):
            total = total + turn(value, -b * self.width)
        spread = total
        for b in range(1, self.blocks):
            spread = jnp.where(lane >= b * self.width, turn(total, b * self.width), spread)
        return spread

    def rows(self):
        angles = 2.0 * math.pi * np.arange(self.dir_count) / self.dir_count
        out = np.zeros((4, self.slabs, LANES))
        for r in range(self.slabs):
            for b in range(self.blocks):
                at = slice(b * self.width, (b + 1) * self.width)
                angle = angles[self.direction(b, r)]
                out[:, r, at] = np.array(
                    [math.cos(angle), math.sin(angle), abs(math.cos(angle)), abs(math.sin(angle))]
                )[:, None]
        return np.broadcast_to(out[:, :, None, :], (4, self.slabs, ROWS, LANES)).astype(np.float32)


def turn(value, by):
    by %= LANES
    return pltpu.roll(value, by, 1) if by else value


def lanes():
    return lax.broadcasted_iota(jnp.int32, (ROWS, LANES), 1)


def every_row(value, row):
    return jnp.broadcast_to(value[row:row + 1, :], (ROWS, LANES))


def within(lane, first, count):
    return (lane >= first) & (lane < first + count)


def sine_up(j, dir_count):
    return math.sin(2.0 * math.pi * j / dir_count) > 0


def tables(freq_count, dir_count):
    levels = 3.0 ** (np.arange(freq_count) / (freq_count - 1))
    speeds = COURANT_TOP * 1.1 ** (-np.arange(freq_count, dtype=np.float64))
    up_j, up_z = split(ANGLE_UP * dir_count / 360.0)
    rate = (1.0 - UP_W) * up_z / LIMITER
    rows = [
        speeds,
        rate * QUAD_RATE / (GAIN * STATE ** 3) * levels,
        WIND_RATE * 0.5 / (LIMITER * STATE) * levels,
        levels / (dir_count * np.sum(levels) * STATE),
        DECAY_RATE / (LIMITER * STATE) * levels,
    ]
    return np.broadcast_to(
        np.stack(rows)[:, :, None], (len(rows), freq_count, LANES)
    ).astype(np.float32)


def clear(ref, slabs, freq_count):
    zero = jnp.zeros((PAD, LANES), jnp.float32)
    for r in range(slabs):
        ref[r, pl.ds(0, PAD), :] = zero
        ref[r, pl.ds(PAD + freq_count, PAD), :] = zero


def set_wind(pack, freq_count, table_ref, angle_ref, aux, w_ref):
    east, north = every_row(aux, 0), every_row(aux, 1)
    for r in range(pack.slabs):
        drive = east * angle_ref[0, r] + north * angle_ref[1, r]
        for kb in range(freq_count // ROWS):
            at = pl.ds(kb * ROWS, ROWS)
            w_ref[r, at, :] = jnp.maximum(table_ref[2, at, :] * drive - WIND_RATE / (LIMITER * STATE), 0.0)


def sub_steps(pack, freq_count, table_ref, e_ref, u_ref, d_ref, n_ref, w_ref, acc_ref, c_ref):
    slabs, blocks = pack.slabs, freq_count // ROWS
    lane = lanes()
    up_j, up_z = split(ANGLE_UP * pack.dir_count / 360.0)
    down_j, down_z = split(ANGLE_DOWN * pack.dir_count / 360.0)
    up_near, up_far = up_j + 1, up_j
    up_weight, up_rest = up_z, (1.0 - up_z) / up_z
    down_near, down_far = down_j, down_j + 1
    down_weight, down_rest = 1.0 - down_z, down_z / (1.0 - down_z)
    up_scale = GAIN_UP * GAIN * up_weight
    down_scale = GAIN_DOWN * GAIN * down_weight
    fold = (1.0 - UP_W) * up_weight
    up_tail = UP_W / (1.0 - UP_W)
    down_head = (1.0 - DOWN_W) * down_weight / fold
    down_tail = DOWN_W * down_weight / fold
    own = -2.0 / fold

    def around(known, make, r):
        if r not in known:
            if r < 0:
                known[r] = pack.block_before(around(known, make, r + slabs), lane)
            elif r >= slabs:
                known[r] = pack.next_block(around(known, make, r - slabs), lane)
            else:
                known[r] = make(r)
        return known[r]

    def stage_a(kb):
        base = kb * ROWS
        strength = table_ref[1, pl.ds(base, ROWS), :]
        up, down, more, less, up_c, down_c, centre = {}, {}, {}, {}, {}, {}, {}

        def read(r, offset):
            return e_ref[r, pl.ds(base + PAD + offset, ROWS), :]

        def make_up(r):
            return (up_scale * (1.0 - UP_W)) * read(r, UP_K) + (up_scale * UP_W) * read(r, UP_K + 1)

        def make_down(r):
            return (down_scale * (1.0 - DOWN_W)) * read(r, DOWN_K) + (down_scale * DOWN_W) * read(r, DOWN_K + 1)

        def get_up(r):
            return around(up, make_up, r)

        def get_down(r):
            return around(down, make_down, r)

        def get_up_c(r):
            if r not in up_c:
                up_c[r] = get_up(r) * up_rest
            return up_c[r]

        def get_down_c(r):
            if r not in down_c:
                down_c[r] = get_down(r) * down_rest
            return down_c[r]

        def make_quad(r, sign):
            if r not in centre:
                here = read(r, 0)
                centre[r] = here, here * strength
            here, gain = centre[r]
            plus = get_up(r + sign * up_near) + get_up_c(r + sign * up_far)
            minus = get_down(r + sign * down_near) + get_down_c(r + sign * down_far)
            return gain * (here * (plus + minus) - plus * minus)

        def get_more(r):
            return around(more, lambda r: make_quad(r, 1), r)

        def get_less(r):
            return around(less, lambda r: make_quad(r, -1), r)

        if slabs > 9:
            for r in (slabs - 2, slabs - 1, 0, 1):
                get_up(r)
            for r in (*range(slabs - 4, slabs), *range(4)):
                get_down(r)
            for r in (-2, -1, slabs, slabs + 1):
                get_up(r)
            for r in (*range(-4, 0), *range(slabs, slabs + 4)):
                get_down(r)
            for r in (*range(slabs - 4, slabs), 0, 1):
                get_more(r)
            for r in (slabs - 2, slabs - 1, *range(4)):
                get_less(r)
            for r in (*range(-4, 0), slabs, slabs + 1):
                get_more(r)
            for r in (-2, -1, *range(slabs, slabs + 4)):
                get_less(r)
            order = (*range(4, slabs - 4), *range(4), *range(slabs - 4, slabs))
        else:
            order = range(slabs)
        for r in order:
            u_ref[r, pl.ds(base + PAD, ROWS), :] = (
                get_more(r - up_near) + get_less(r + up_near)
            ) + up_rest * (get_more(r - up_far) + get_less(r + up_far))
            d_ref[r, pl.ds(base + PAD, ROWS), :] = (
                get_more(r - down_near) + get_less(r + down_near)
            ) + down_rest * (get_more(r - down_far) + get_less(r + down_far))
            n_ref[r, pl.ds(base, ROWS), :] = own * (get_more(r) + get_less(r))

    def stage_b(kb):
        base = kb * ROWS
        decay = c_ref[pl.ds(base, ROWS), :]
        total = jnp.zeros((ROWS, LANES), jnp.float32)
        for r in range(slabs):
            here = e_ref[r, pl.ds(base + PAD, ROWS), :]
            rate = here * (w_ref[r, pl.ds(base, ROWS), :] - decay) + n_ref[r, pl.ds(base, ROWS), :]
            rate = rate + (
                u_ref[r, pl.ds(base + PAD - UP_K, ROWS), :]
                + up_tail * u_ref[r, pl.ds(base + PAD - UP_K - 1, ROWS), :]
            )
            rate = rate + (
                down_head * d_ref[r, pl.ds(base + PAD - DOWN_K, ROWS), :]
                + down_tail * d_ref[r, pl.ds(base + PAD - DOWN_K - 1, ROWS), :]
            )
            here = here + jnp.tanh(rate)
            e_ref[r, pl.ds(base + PAD, ROWS), :] = here
            total = total + here
        acc_ref[pl.ds(base, ROWS), :] = total

    def sub_step(index, carry):
        steepness = jnp.sum(acc_ref[...] * table_ref[3], axis=0, keepdims=True)
        steepness = pack.over_blocks(jnp.broadcast_to(steepness, (ROWS, LANES)), lane)[0:1]
        c_ref[...] = steepness * table_ref[4]
        for kb in range(blocks):
            stage_a(kb)
        for kb in range(blocks):
            stage_b(kb)
        return carry

    lax.fori_loop(0, SUB, sub_step, 0)


def slab_at(r, kb, freq_count):
    return pl.ds(r * freq_count + kb * ROWS, ROWS)


SQUEEZE = (0, COAST, 4 * COAST, 5 * COAST)


def flow_mask(lane, width, wanted):
    block = lane // width
    forward = ((block == 0) | (block == 3)).astype(jnp.int32)
    return (forward == wanted) & (lane % width < COAST)


def squeeze(fetch, count, chosen):
    out = []
    for start in range(0, count, len(SQUEEZE)):
        total = None
        for i in range(start, min(count, start + len(SQUEEZE))):
            value = turn(jnp.where(chosen, fetch(i), 0.0), SQUEEZE[i - start])
            total = value if total is None else total + value
        out.append(total)
    return out


def loosen(ref, i):
    g, part = divmod(i, len(SQUEEZE))
    return turn(ref[pl.ds(g * ROWS, ROWS), :], -SQUEEZE[part])


def unpack_turn(value, pack):
    return turn(value, -pack.width)


def near_kernel(one, freq_count, spec_ref, own_ref, send_ref):
    dir_count = one.dir_count
    blocks = freq_count // ROWS
    chunk = ROWS * dir_count
    lane = lanes()
    angles = 2.0 * math.pi * np.arange(dir_count) / dir_count
    first = COAST + REST
    row = lax.broadcasted_iota(jnp.int32, (ROWS, LANES), 0)
    for kb in range(blocks):
        speed = COURANT_TOP * STATE * jnp.exp((row + kb * ROWS).astype(jnp.float32) * (-math.log(1.1)))
        for some in range(0, one.slabs, 4):
            slabs = range(some, some + 4)
            keys = [(r, b) for r in slabs for b in range(one.blocks)]
            here = {
                (r, b): spec_ref[pl.ds(kb * chunk + one.direction(b, r), ROWS, stride=dir_count), :] for r, b in keys
            }
            along, moved = {}, {}
            for r, b in keys:
                if sine_up(one.direction(b, r), dir_count):
                    along[r, b] = turn(here[r, b], 1)
                else:
                    along[r, b] = jnp.where(lane == LANES - 1, 0.0, turn(here[r, b], -1))
            for r, b in keys:
                angle = angles[one.direction(b, r)]
                cosine, sine = float(abs(math.cos(angle))), float(abs(math.sin(angle)))
                value = here[r, b] * (STATE - speed * (cosine + sine)) + along[r, b] * (speed * sine)
                moved[r, b] = turn(value, b * one.width - first)
            own, sent = {}, {}
            for r in slabs:
                own[r] = sent[r] = moved[r, 0]
                for b in range(1, one.blocks):
                    at = b * one.width
                    ahead = (at + one.width) % LANES
                    own[r] = jnp.where(lane >= at, moved[r, b], own[r])
                    reached = lane >= ahead
                    if b == one.blocks - 1:
                        reached = reached | (lane < one.width - (LANES - ahead))
                    sent[r] = jnp.where(reached, moved[r, b], sent[r])
            sent = {r: unpack_turn(sent[r], one) for r in slabs}
            for r in slabs:
                own_ref[slab_at(r, kb, freq_count), :] = own[r]
                send_ref[slab_at(r, kb, freq_count), :] = sent[r]


def pack_aux(pack, aux, first, slot, count):
    lane = lanes()
    total = jnp.zeros((ROWS, LANES), jnp.float32)
    for b in range(pack.blocks):
        at = b * pack.width + slot
        total = jnp.where(within(lane, at, count), turn(aux, at - first), total)
    return total


def aux_kernel(one, two, mask_ref, wind_ref, deal_ref, row_ref, own_ref, send_ref):
    mask = mask_ref[...].astype(jnp.float32)
    aux = jnp.concatenate(
        [
            wind_ref[...] * mask,
            (deal_ref[...] + 1).astype(jnp.float32) * mask,
            mask,
            jnp.zeros((ROWS - 4, LANES), jnp.float32),
        ],
        axis=0,
    )
    row_ref[...] = jnp.concatenate(
        [mask, jnp.broadcast_to(mask[:, LANES - 1:LANES], (1, LANES)), jnp.zeros((ROWS - 2, LANES), jnp.float32)], axis=0
    )
    own_ref[pl.ds(0, ROWS), :] = pack_aux(one, aux, COAST + REST, 0, NEAR)
    own_ref[pl.ds(ROWS, ROWS), :] = pack_aux(two, aux, 0, 0, COAST + REST)
    send_ref[pl.ds(0, ROWS), :] = pack_aux(one, aux, FAR, 0, NEAR)
    send_ref[pl.ds(ROWS, ROWS), :] = pack_aux(two, aux, FAR + NEAR, COAST, REST)


def coast_kernel(two, freq_count, code_ref, spec_ref, row_ref, own_ref, send_ref, cross_ref):
    dir_count = two.dir_count
    blocks = freq_count // ROWS
    chunk = ROWS * dir_count
    lane = lanes()
    slot = lane % two.width
    mask = every_row(row_ref[...], 0)
    for kb in range(blocks):
        done = []
        for r in range(two.slabs):
            own, sent = None, None
            for b in range(two.blocks):
                j = two.direction(b, r)
                here = spec_ref[pl.ds(kb * chunk + j, ROWS, stride=dir_count), :] * mask
                here = turn(here, b * two.width)
                block = within(lane, b * two.width, two.width)
                behind = within(lane, (b - 1) % two.blocks * two.width, two.width)
                own = here if b == 0 else jnp.where(block, here, own)
                sent = here if b == 0 else jnp.where(behind, here, sent)
            done.append((own, jnp.where(slot < COAST, own, sent)))
        for r, (own, sent) in enumerate(done):
            own_ref[slab_at(r, kb, freq_count), :] = own
            send_ref[slab_at(r, kb, freq_count), :] = sent

    chosen = flow_mask(lane, two.width, code_ref[0] % 2)
    for g, value in enumerate(squeeze(lambda i: own_ref[pl.ds(i * ROWS, ROWS), :], two.slabs * blocks, chosen)):
        cross_ref[pl.ds(g * ROWS, ROWS), :] = value


def take_column(pack, fetch, slot_up, slot_down, kb, lane):
    total = jnp.zeros((ROWS, LANES), jnp.float32)
    for r in range(pack.slabs):
        value = fetch(r, kb)
        for b in range(pack.blocks):
            j = pack.direction(b, r)
            at = b * pack.width + (slot_up if sine_up(j, pack.dir_count) else slot_down)
            total = jnp.where(lane == j, turn(value, j - at), total)
    return total


def store_state(pack, freq_count, e_ref, scale, out_ref):
    for r in range(pack.slabs):
        blocks = range(freq_count // ROWS)
        done = [e_ref[r, pl.ds(PAD + kb * ROWS, ROWS), :] * scale for kb in blocks]
        for kb in blocks:
            out_ref[slab_at(r, kb, freq_count), :] = done[kb]


def one_kernel(one, freq_count, last, table_ref, angle_ref, *refs):
    if last:
        row_ref, in_ref, local_ref, column_ref, out_ref, energy_ref = refs[:6]
        scratch = refs[6:]
    else:
        row_ref, own_ref, got_ref, own_aux, got_aux, out_ref, column_ref = refs[:7]
        scratch = refs[7:]
    e_ref, u_ref, d_ref, n_ref, w_ref, acc_ref, c_ref, known_ref = scratch
    known_ref[...] = table_ref[...]
    blocks = freq_count // ROWS
    lane = lanes()
    for ref in (e_ref, u_ref, d_ref):
        clear(ref, one.slabs, freq_count)
    aux_at = pl.ds(one.slabs * freq_count, ROWS)
    owner = jnp.broadcast_to(row_ref[1:2, :], (ROWS, LANES)) > 0.5
    if last:
        aux = in_ref[aux_at, :]
        up = (lane >= 1) & (lane < one.dir_count // 2 + 1)
    else:
        aux = jnp.where(owner, own_aux[pl.ds(0, ROWS), :], got_aux[pl.ds(0, ROWS), :])
        out_ref[aux_at, :] = aux
    mask = every_row(aux, 3)
    set_wind(one, freq_count, table_ref, angle_ref, aux, w_ref)
    for kb in range(blocks):
        at = pl.ds(kb * ROWS, ROWS)
        total = jnp.zeros((ROWS, LANES), jnp.float32)
        if last:
            speed = table_ref[0, at, :]
            beyond = jnp.where(up == owner, local_ref[at, :], column_ref[at, :])
        done = []
        if last:
            state = [in_ref[slab_at(r, kb, freq_count), :] for r in range(one.slabs)]
            below = [turn(value, 1) for value in state]
            above = [turn(value, -1) for value in state]
        for r in range(one.slabs):
            if last:
                here = state[r]
                along = jnp.where(angle_ref[1, r] > 0, below[r], above[r])
                for b in range(one.blocks):
                    j = one.direction(b, r)
                    to = b * one.width + (0 if sine_up(j, one.dir_count) else NEAR - 1)
                    along = jnp.where(lane == to, turn(beyond, to - j), along)
                start = (
                    here
                    - speed * angle_ref[2, r] * here
                    - speed * angle_ref[3, r] * (here - along)
                ) * (mask * STATE)
            else:
                start = jnp.where(owner, own_ref[slab_at(r, kb, freq_count), :], got_ref[slab_at(r, kb, freq_count), :])
            done.append(start)
            total = total + start
        for r, start in enumerate(done):
            e_ref[r, pl.ds(PAD + kb * ROWS, ROWS), :] = start
        acc_ref[at, :] = total

    @pl.when(jnp.max(aux[3:4]) > 0.5)
    def _():
        sub_steps(one, freq_count, known_ref, e_ref, u_ref, d_ref, n_ref, w_ref, acc_ref, c_ref)

    store_state(one, freq_count, e_ref, mask * (1.0 / STATE), out_ref)
    if last:
        energy = jnp.sum(acc_ref[...], axis=0, keepdims=True) * (mask[0:1] * (1.0 / (STATE * freq_count * one.dir_count)))
        energy_ref[...] = jnp.concatenate(
            [energy, aux[2:3] - 1.0, jnp.zeros((ROWS - 2, LANES), jnp.float32)], axis=0
        )
    else:
        for kb in range(blocks):
            column_ref[pl.ds(kb * ROWS, ROWS), :] = take_column(
                one, lambda r, kb: out_ref[slab_at(r, kb, freq_count), :], NEAR - 1, 0, kb, lane
            )


def two_kernel(two, freq_count, slot_count, last, code_ref, table_ref, angle_ref, row_ref, *refs):
    if last:
        in_ref, pair_ref, cross_ref, local_ref, other_ref, out_ref, energy_ref = refs[:7]
        scratch = refs[7:]
    else:
        own_ref, got_ref, own_aux, got_aux, cross_ref, out_ref, column_ref, pair_out, cross_out = refs[:9]
        scratch = refs[9:]
    e_ref, u_ref, d_ref, n_ref, w_ref, acc_ref, c_ref, known_ref = scratch
    known_ref[...] = table_ref[...]
    blocks = freq_count // ROWS
    lane = lanes()
    slot = lane % two.width
    for ref in (e_ref, u_ref, d_ref):
        clear(ref, two.slabs, freq_count)
    aux_at = pl.ds(two.slabs * freq_count, ROWS)
    parity = code_ref[0] % 2
    inner = (code_ref[0] < 2).astype(jnp.float32)
    owner = jnp.broadcast_to(row_ref[1:2, :], (ROWS, LANES)) > 0.5
    from_cross = flow_mask(lane, two.width, 1 - parity)
    from_pair = flow_mask(lane, two.width, parity)
    if last:
        aux = in_ref[aux_at, :]
        mask = every_row(aux, 3)
    else:
        second = pl.ds(ROWS, ROWS)
        aux = own_aux[second, :] + got_aux[second, :]
        out_ref[aux_at, :] = aux
        mask, got_mask = every_row(own_aux[second, :], 3), every_row(got_aux[second, :], 3)
    set_wind(two, freq_count, table_ref, angle_ref, aux, w_ref)
    for kb in range(blocks):
        at = pl.ds(kb * ROWS, ROWS)
        speed = table_ref[0, at, :]
        total = jnp.zeros((ROWS, LANES), jnp.float32)
        done = []
        slabs = range(two.slabs)
        upward = [angle_ref[1, r] > 0 for r in slabs]
        flow_x = [speed * angle_ref[2, r] for r in slabs]
        flow_y = [speed * angle_ref[3, r] for r in slabs]

        def neighbours(values):
            below = [turn(value, 1) for value in values]
            above = [turn(value, -1) for value in values]
            return [jnp.where(upward[r], below[r], above[r]) for r in slabs]

        here = [(in_ref if last else own_ref)[slab_at(r, kb, freq_count), :] for r in slabs]
        along = neighbours(here)
        across = [loosen(cross_ref, r * blocks + kb) * inner for r in slabs]
        if last:
            beside = [loosen(pair_ref, r * blocks + kb) for r in slabs]
        else:
            beside = [got_ref[slab_at(r, kb, freq_count), :] for r in slabs]
        for r in slabs:
            nearby = jnp.where(from_cross, across[r], jnp.where(from_pair, beside[r], 0.0))
            if last:
                beyond = local_ref[at, :]
                for b in range(two.blocks):
                    j = two.direction(b, r)
                    start = b * two.width
                    if sine_up(j, two.dir_count):
                        to = start + COAST
                        along[r] = jnp.where((lane == to) & ~owner, turn(beyond, to - j), along[r])
                    else:
                        to = start + COAST + REST - 1
                        along[r] = jnp.where((lane == to) & owner, turn(beyond, to - j), along[r])
                        along[r] = jnp.where((lane == start + COAST - 1) & ~owner, 0.0, along[r])
            else:
                along[r] = jnp.where((slot == 0) & upward[r], 0.0, along[r])
            done.append(
                (here[r] - flow_x[r] * (here[r] - nearby) - flow_y[r] * (here[r] - along[r])) * (mask * STATE)
            )
        if not last:
            here = [turn(beside[r], COAST + REST) for r in slabs]
            along = neighbours(here)
            for r in slabs:
                nearby = jnp.where((slot == COAST + REST - 1) & ~upward[r], 0.0, along[r])
                done[r] = done[r] + (
                    here[r] - flow_x[r] * here[r] - flow_y[r] * (here[r] - nearby)
                ) * (got_mask * STATE)
        for r in slabs:
            total = total + done[r]
        for r, start in enumerate(done):
            e_ref[r, pl.ds(PAD + kb * ROWS, ROWS), :] = start
        acc_ref[at, :] = total
    sub_steps(two, freq_count, known_ref, e_ref, u_ref, d_ref, n_ref, w_ref, acc_ref, c_ref)
    scale = every_row(aux, 3) * (1.0 / STATE)
    store_state(two, freq_count, e_ref, scale, out_ref)
    if last:
        energy = jnp.sum(acc_ref[...], axis=0, keepdims=True) * (scale[0:1] / (freq_count * two.dir_count))
        total = None
        for energy, deal in ((energy, aux[2:3] - 1.0), (other_ref[0:1], other_ref[1:2])):
            deal = deal.astype(jnp.int32)
            cards = energy_ref.shape[0]
            card = lax.broadcasted_iota(jnp.int32, (cards, LANES), 0) * slot_count
            place = lax.broadcasted_iota(jnp.int32, (LANES, LANES), 0)
            to_card = jnp.where((deal >= card) & (deal < card + slot_count), energy, 0.0)
            to_slot = (lax.rem(jnp.maximum(deal, 0), slot_count) == place).astype(jnp.float32)
            part = lax.dot_general(
                to_card, to_slot, (((1,), (1,)), ((), ())),
                precision=lax.Precision.HIGHEST, preferred_element_type=jnp.float32,
            )
            total = part if total is None else total + part
        energy_ref[...] = total
    else:
        for kb in range(blocks):
            column_ref[pl.ds(kb * ROWS, ROWS), :] = take_column(
                two, lambda r, kb: out_ref[slab_at(r, kb, freq_count), :], COAST + REST - 1, COAST, kb, lane
            )
        for ref, wanted in ((pair_out, 1 - parity), (cross_out, parity)):
            chosen = flow_mask(lane, two.width, wanted)
            for g, value in enumerate(
                squeeze(lambda i: out_ref[pl.ds(i * ROWS, ROWS), :], two.slabs * blocks, chosen)
            ):
                ref[pl.ds(g * ROWS, ROWS), :] = value


def gather_kernel(
    one, two, freq_count, row_ref, one_ref, one_got, two_ref, two_got, out_hbm, after_ref, out_ref, sems
):
    dir_count = one.dir_count
    chunk = ROWS * dir_count
    lane = lanes()
    mask = every_row(row_ref[...], 0)
    copies = []
    for kb in range(freq_count // ROWS):
        near = [turn(one_got[slab_at(r, kb, freq_count), :], one.width) for r in range(one.slabs)]
        coast = [turn(two_got[slab_at(r, kb, freq_count), :], -(COAST + REST)) for r in range(two.slabs)]
        for some in range(0, dir_count, 12):
            js = range(some, some + 12)
            value, rest = {}, {}
            for j in js:
                b, r = one.find(j)
                start = b * one.width
                mixed = jnp.where(within(lane, start, one.width), one_ref[slab_at(r, kb, freq_count), :], near[r])
                value[j] = turn(mixed, COAST + REST - start)
            for j in js:
                b, r = two.find(j)
                start = b * two.width
                mixed = jnp.where(within(lane, start, COAST + REST), two_ref[slab_at(r, kb, freq_count), :], coast[r])
                rest[j] = turn(mixed, -start)
            for j in js:
                whole = jnp.where(within(lane, COAST + REST, 2 * NEAR), value[j], rest[j]) * mask
                out_ref[pl.ds(kb * chunk + j, ROWS, stride=dir_count), :] = whole
        rows = pl.ds(kb * chunk, chunk)
        copies.append(pltpu.make_async_copy(out_ref.at[rows], out_hbm.at[rows], sems.at[kb]))
        copies[kb].start()
    for copy in copies:
        copy.wait()
    after_ref[...] = row_ref[...]


def energy_kernel(shared_ref, after_ref, energy_ref):
    energy_ref[...] = jnp.sum(shared_ref[...], axis=0, keepdims=True)[:, :energy_ref.shape[1]]


def coast_width(tile_count, cell_count):
    capacity = cell_count // tile_count
    spread = tile_count * (tile_count - 8) // 8
    return -(-spread // (tile_count - 1)) * capacity


def shards(spectrum, sea_mask, card_deal, wind):
    freq_count, dir_count, row_count, row_width = spectrum.shape
    cell_count = row_count * row_width
    tile_count = lax.axis_size("tile")
    slot_count = cell_count // 8
    assert row_count == 1 and cell_count == LANES and coast_width(tile_count, cell_count) <= COAST
    here = lax.axis_index("tile")
    at_end = (here == 0) | (here == tile_count - 1)
    code = (here % 2 + 2 * at_end.astype(jnp.int32)).astype(jnp.int32).reshape(1)
    one, two = Pack(3, NEAR, dir_count, 0), Pack(4, 32, dir_count, 1)
    table = jnp.asarray(tables(freq_count, dir_count))
    one_rows, two_rows = one.slabs * freq_count, two.slabs * freq_count
    squeezed = -(-two_rows // ROWS // len(SQUEEZE)) * ROWS

    def array(*shape):
        return jax.ShapeDtypeStruct(shape, jnp.float32)

    smem = pl.BlockSpec(memory_space=pltpu.SMEM)
    vmem = pl.BlockSpec(memory_space=pltpu.VMEM)
    hbm = pl.BlockSpec(memory_space=pltpu.HBM)

    def params(rows, steps=SUB, vmem=48):
        return dict(
            compiler_params=pltpu.CompilerParams(vmem_limit_bytes=vmem * 1024 * 1024),
            cost_estimate=pl.CostEstimate(
                flops=rows // ROWS * steps * 8_000_000, bytes_accessed=8 * rows * LANES, transcendentals=0
            ),
        )

    def scratch(pack):
        padded = pltpu.VMEM((pack.slabs, freq_count + 2 * PAD, LANES), jnp.float32)
        plain = pltpu.VMEM((pack.slabs, freq_count, LANES), jnp.float32)
        column = pltpu.VMEM((freq_count, LANES), jnp.float32)
        return [padded, padded, padded, plain, plain, column, column, pltpu.VMEM(table.shape, jnp.float32)]

    group_count = lax.axis_size("groups")
    chip_swap = []
    for g in range(group_count):
        for i in range(tile_count):
            other, there = g, (i + 1 if i % 2 else i - 1)
            if not 0 <= there < tile_count:
                other, there = (g ^ 1 if g ^ 1 < group_count else g), i
            chip_swap.append((g * tile_count + i, other * tile_count + there))

    def to_pair(value):
        return lax.ppermute(value, "tile", [(i, i ^ 1) for i in range(tile_count)])

    def to_next(value):
        return lax.ppermute(value, ("groups", "tile"), chip_swap)

    one_angles, two_angles = jnp.asarray(one.rows()), jnp.asarray(two.rows())
    flat = spectrum.reshape(freq_count * dir_count, cell_count)
    whole = pltpu.VMEM((freq_count * dir_count, LANES), jnp.float32)
    chunks = pltpu.SemaphoreType.DMA((freq_count // ROWS,))
    one_own, one_send = pl.pallas_call(
        functools.partial(near_kernel, one, freq_count),
        out_shape=(array(one_rows, LANES), array(one_rows, LANES)),
        in_specs=[vmem],
        out_specs=(vmem,) * 2,
        name="near",
        **params(1440, 1),
    )(flat)
    row, own_aux, send_aux = pl.pallas_call(
        functools.partial(aux_kernel, one, two),
        out_shape=(array(ROWS, LANES), array(2 * ROWS, LANES), array(2 * ROWS, LANES)),
        in_specs=[vmem] * 3,
        out_specs=(vmem,) * 3,
        name="aux",
        **params(80, 1),
    )(sea_mask, wind.reshape(2, cell_count), card_deal)
    one_got = to_pair(one_send)
    got_aux = to_pair(send_aux)
    two_own, two_send, cross = pl.pallas_call(
        functools.partial(coast_kernel, two, freq_count),
        out_shape=(array(two_rows, LANES), array(two_rows, LANES), array(squeezed, LANES)),
        in_specs=[smem, vmem, vmem],
        out_specs=(vmem,) * 3,
        name="coast",
        **params(1440, 1),
    )(code, flat, row)
    cross_got = to_next(cross)
    two_got = to_pair(two_send)
    one_state, one_column = pl.pallas_call(
        functools.partial(one_kernel, one, freq_count, False),
        out_shape=(array(one_rows + ROWS, LANES), array(freq_count, LANES)),
        in_specs=[vmem] * 7,
        out_specs=(vmem,) * 2,
        scratch_shapes=scratch(one),
        name="first_one",
        **params(one_rows),
    )(table, one_angles, row, one_own, one_got, own_aux, got_aux)
    column_got = to_pair(one_column)
    two_state, two_column, pair, cross = pl.pallas_call(
        functools.partial(two_kernel, two, freq_count, slot_count, False),
        out_shape=(
            array(two_rows + ROWS, LANES), array(freq_count, LANES), array(squeezed, LANES), array(squeezed, LANES),
        ),
        in_specs=[smem] + [vmem] * 8,
        out_specs=(vmem,) * 4,
        scratch_shapes=scratch(two),
        name="first_two",
        **params(two_rows),
    )(code, table, two_angles, row, two_own, two_got, own_aux, got_aux, cross_got)
    cross_got = to_next(cross)
    pair_got = to_pair(pair)
    one_state, one_energy = pl.pallas_call(
        functools.partial(one_kernel, one, freq_count, True),
        out_shape=(array(one_rows, LANES), array(ROWS, LANES)),
        in_specs=[vmem] * 6,
        out_specs=(vmem,) * 2,
        scratch_shapes=scratch(one),
        name="second_one",
        **params(one_rows),
    )(table, one_angles, row, one_state, two_column, column_got)
    one_got = to_pair(one_state)
    two_state, energy = pl.pallas_call(
        functools.partial(two_kernel, two, freq_count, slot_count, True),
        out_shape=(array(two_rows, LANES), array(tile_count, LANES)),
        in_specs=[smem] + [vmem] * 8,
        out_specs=(vmem,) * 2,
        scratch_shapes=scratch(two),
        name="second_two",
        **params(two_rows),
    )(code, table, two_angles, row, two_state, pair_got, cross_got, one_column, one_energy)
    two_got = to_pair(two_state)
    shared = lax.all_to_all(
        energy.reshape(tile_count, 1, LANES), "tile", split_axis=0, concat_axis=0, tiled=True
    )
    out, after = pl.pallas_call(
        functools.partial(gather_kernel, one, two, freq_count),
        out_shape=(array(freq_count * dir_count, LANES), array(ROWS, LANES)),
        in_specs=[vmem] * 5,
        out_specs=(hbm, vmem),
        scratch_shapes=[whole, chunks],
        name="gather",
        **params(1440, 1),
    )(row, one_state, one_got, two_state, two_got)
    card_energy = pl.pallas_call(
        energy_kernel,
        out_shape=array(1, slot_count),
        in_specs=[vmem] * 2,
        out_specs=vmem,
        name="energy",
        **params(80, 1),
    )(shared.reshape(tile_count, LANES), after)
    return out.reshape(freq_count, dir_count, row_count, row_width), card_energy.reshape(slot_count)


def solution(mesh):
    placed = (
        P(None, None, ("groups", "tile"), None),
        P(("groups", "tile"), None),
        P(("groups", "tile"), None),
        P(None, ("groups", "tile"), None),
    )
    return jax.shard_map(
        shards,
        mesh=mesh,
        in_specs=placed,
        out_specs=(P(None, None, ("groups", "tile"), None), P(("groups", "tile"))),
        check_vma=False,
    )
```

```python
import functools
import math

import jax
import jax.numpy as jnp
import numpy as np
from jax import lax
from jax.experimental import pallas as pl
from jax.experimental.pallas import tpu as pltpu
from jax.sharding import PartitionSpec as P

STEPS = 2
SUB = 8
COURANT_TOP = 0.7
WIND_RATE = 0.15
DECAY_RATE = 0.3
QUAD_RATE = 0.5
LIMITER = 0.25
ANGLE_UP = -11.48
ANGLE_DOWN = 33.56
SHIFT_UP = math.log(1.25) / math.log(1.1)
SHIFT_DOWN = math.log(0.75) / math.log(1.1)
GAIN_UP = 1.25 ** (-4)
GAIN_DOWN = 0.75 ** (-4)
GAIN_BOTH = 0.9375 ** (-4)

LANES = 128
ROWS = 8
PAD = 4


def split(offset):
    base = math.floor(offset)
    return base, offset - base


GAIN = 2.0 * GAIN_BOTH / (GAIN_UP * GAIN_DOWN)
STATE = SUB / LIMITER
UP_K, UP_W = split(SHIFT_UP)
DOWN_K, DOWN_W = split(SHIFT_DOWN)

COAST = 16
NEAR = 42
REST = 14
FAR = COAST + REST + NEAR


class Pack:
    def __init__(self, blocks, width, dir_count, offset):
        self.blocks, self.width, self.offset = blocks, width, offset
        self.slabs = dir_count // blocks
        self.dir_count = dir_count

    def direction(self, block, slab):
        return (block * self.slabs + slab + self.offset) % self.dir_count

    def find(self, j):
        return divmod((j - self.offset) % self.dir_count, self.slabs)

    def next_block(self, value, lane):
        if self.blocks * self.width == LANES:
            return turn(value, -self.width)
        last = (self.blocks - 1) * self.width
        return jnp.take_along_axis(value, jnp.where(lane < last, lane + self.width, lane - last), axis=1)

    def block_before(self, value, lane):
        if self.blocks * self.width == LANES:
            return turn(value, self.width)
        last = (self.blocks - 1) * self.width
        source = jnp.where(lane >= self.width, lane - self.width, lane + last)
        return jnp.take_along_axis(value, jnp.minimum(source, LANES - 1), axis=1)

    def over_blocks(self, value, lane):
        if self.blocks == 4:
            value = value + turn(value, 2 * self.width)
            return value + turn(value, self.width)
        total = value
        for b in range(1, self.blocks):
            total = total + turn(value, -b * self.width)
        spread = total
        for b in range(1, self.blocks):
            spread = jnp.where(lane >= b * self.width, turn(total, b * self.width), spread)
        return spread

    def rows(self):
        angles = 2.0 * math.pi * np.arange(self.dir_count) / self.dir_count
        out = np.zeros((4, self.slabs, LANES))
        for r in range(self.slabs):
            for b in range(self.blocks):
                at = slice(b * self.width, (b + 1) * self.width)
                angle = angles[self.direction(b, r)]
                out[:, r, at] = np.array(
                    [math.cos(angle), math.sin(angle), abs(math.cos(angle)), abs(math.sin(angle))]
                )[:, None]
        return np.broadcast_to(out[:, :, None, :], (4, self.slabs, ROWS, LANES)).astype(np.float32)


def turn(value, by):
    by %= LANES
    return pltpu.roll(value, by, 1) if by else value


def lanes():
    return lax.broadcasted_iota(jnp.int32, (ROWS, LANES), 1)


def every_row(value, row):
    return jnp.broadcast_to(value[row:row + 1, :], (ROWS, LANES))


def within(lane, first, count):
    return (lane >= first) & (lane < first + count)


def sine_up(j, dir_count):
    return math.sin(2.0 * math.pi * j / dir_count) > 0


def tables(freq_count, dir_count):
    levels = 3.0 ** (np.arange(freq_count) / (freq_count - 1))
    speeds = COURANT_TOP * 1.1 ** (-np.arange(freq_count, dtype=np.float64))
    up_j, up_z = split(ANGLE_UP * dir_count / 360.0)
    rate = (1.0 - UP_W) * up_z / LIMITER
    rows = [
        speeds,
        rate * QUAD_RATE / (GAIN * STATE ** 3) * levels,
        WIND_RATE * 0.5 / (LIMITER * STATE) * levels,
        levels / (dir_count * np.sum(levels) * STATE),
        DECAY_RATE / (LIMITER * STATE) * levels,
    ]
    return np.broadcast_to(
        np.stack(rows)[:, :, None], (len(rows), freq_count, LANES)
    ).astype(np.float32)


def clear(ref, slabs, freq_count):
    zero = jnp.zeros((PAD, LANES), jnp.float32)
    for r in range(slabs):
        ref[r, pl.ds(0, PAD), :] = zero
        ref[r, pl.ds(PAD + freq_count, PAD), :] = zero


def set_wind(pack, freq_count, table_ref, angle_ref, aux, w_ref):
    east, north = every_row(aux, 0), every_row(aux, 1)
    for r in range(pack.slabs):
        drive = east * angle_ref[0, r] + north * angle_ref[1, r]
        for kb in range(freq_count // ROWS):
            at = pl.ds(kb * ROWS, ROWS)
            w_ref[r, at, :] = jnp.maximum(table_ref[2, at, :] * drive - WIND_RATE / (LIMITER * STATE), 0.0)


def sub_steps(pack, freq_count, table_ref, e_ref, u_ref, d_ref, n_ref, w_ref, acc_ref, c_ref):
    slabs, blocks = pack.slabs, freq_count // ROWS
    lane = lanes()
    up_j, up_z = split(ANGLE_UP * pack.dir_count / 360.0)
    down_j, down_z = split(ANGLE_DOWN * pack.dir_count / 360.0)
    up_near, up_far = up_j + 1, up_j
    up_weight, up_rest = up_z, (1.0 - up_z) / up_z
    down_near, down_far = down_j, down_j + 1
    down_weight, down_rest = 1.0 - down_z, down_z / (1.0 - down_z)
    up_scale = GAIN_UP * GAIN * up_weight
    down_scale = GAIN_DOWN * GAIN * down_weight
    fold = (1.0 - UP_W) * up_weight
    up_tail = UP_W / (1.0 - UP_W)
    down_head = (1.0 - DOWN_W) * down_weight / fold
    down_tail = DOWN_W * down_weight / fold
    own = -2.0 / fold

    def around(known, make, r):
        if r not in known:
            if r < 0:
                known[r] = pack.block_before(around(known, make, r + slabs), lane)
            elif r >= slabs:
                known[r] = pack.next_block(around(known, make, r - slabs), lane)
            else:
                known[r] = make(r)
        return known[r]

    def stage_a(kb):
        base = kb * ROWS
        strength = table_ref[1, pl.ds(base, ROWS), :]
        up, down, more, less, up_c, down_c, centre = {}, {}, {}, {}, {}, {}, {}

        def read(r, offset):
            return e_ref[r, pl.ds(base + PAD + offset, ROWS), :]

        def make_up(r):
            return (up_scale * (1.0 - UP_W)) * read(r, UP_K) + (up_scale * UP_W) * read(r, UP_K + 1)

        def make_down(r):
            return (down_scale * (1.0 - DOWN_W)) * read(r, DOWN_K) + (down_scale * DOWN_W) * read(r, DOWN_K + 1)

        def get_up(r):
            return around(up, make_up, r)

        def get_down(r):
            return around(down, make_down, r)

        def get_up_c(r):
            if r not in up_c:
                up_c[r] = get_up(r) * up_rest
            return up_c[r]

        def get_down_c(r):
            if r not in down_c:
                down_c[r] = get_down(r) * down_rest
            return down_c[r]

        def make_quad(r, sign):
            if r not in centre:
                here = read(r, 0)
                centre[r] = here, here * strength
            here, gain = centre[r]
            plus = get_up(r + sign * up_near) + get_up_c(r + sign * up_far)
            minus = get_down(r + sign * down_near) + get_down_c(r + sign * down_far)
            return gain * (here * (plus + minus) - plus * minus)

        def get_more(r):
            return around(more, lambda r: make_quad(r, 1), r)

        def get_less(r):
            return around(less, lambda r: make_quad(r, -1), r)

        if slabs > 9:
            for r in (slabs - 2, slabs - 1, 0, 1):
                get_up(r)
            for r in (*range(slabs - 4, slabs), *range(4)):
                get_down(r)
            for r in (-2, -1, slabs, slabs + 1):
                get_up(r)
            for r in (*range(-4, 0), *range(slabs, slabs + 4)):
                get_down(r)
            for r in (*range(slabs - 4, slabs), 0, 1):
                get_more(r)
            for r in (slabs - 2, slabs - 1, *range(4)):
                get_less(r)
            for r in (*range(-4, 0), slabs, slabs + 1):
                get_more(r)
            for r in (-2, -1, *range(slabs, slabs + 4)):
                get_less(r)
            order = (*range(4, slabs - 4), *range(4), *range(slabs - 4, slabs))
        else:
            order = range(slabs)
        for r in order:
            u_ref[r, pl.ds(base + PAD, ROWS), :] = (
                get_more(r - up_near) + get_less(r + up_near)
            ) + up_rest * (get_more(r - up_far) + get_less(r + up_far))
            d_ref[r, pl.ds(base + PAD, ROWS), :] = (
                get_more(r - down_near) + get_less(r + down_near)
            ) + down_rest * (get_more(r - down_far) + get_less(r + down_far))
            n_ref[r, pl.ds(base, ROWS), :] = own * (get_more(r) + get_less(r))

    def stage_b(kb):
        base = kb * ROWS
        decay = c_ref[pl.ds(base, ROWS), :]
        total = jnp.zeros((ROWS, LANES), jnp.float32)
        for r in range(slabs):
            here = e_ref[r, pl.ds(base + PAD, ROWS), :]
            rate = here * (w_ref[r, pl.ds(base, ROWS), :] - decay) + n_ref[r, pl.ds(base, ROWS), :]
            rate = rate + (
                u_ref[r, pl.ds(base + PAD - UP_K, ROWS), :]
                + up_tail * u_ref[r, pl.ds(base + PAD - UP_K - 1, ROWS), :]
            )
            rate = rate + (
                down_head * d_ref[r, pl.ds(base + PAD - DOWN_K, ROWS), :]
                + down_tail * d_ref[r, pl.ds(base + PAD - DOWN_K - 1, ROWS), :]
            )
            here = here + jnp.tanh(rate)
            e_ref[r, pl.ds(base + PAD, ROWS), :] = here
            total = total + here
        acc_ref[pl.ds(base, ROWS), :] = total

    def sub_step(index, carry):
        steepness = jnp.sum(acc_ref[...] * table_ref[3], axis=0, keepdims=True)
        steepness = pack.over_blocks(jnp.broadcast_to(steepness, (ROWS, LANES)), lane)[0:1]
        c_ref[...] = steepness * table_ref[4]
        for kb in range(blocks):
            stage_a(kb)
        for kb in range(blocks):
            stage_b(kb)
        return carry

    lax.fori_loop(0, SUB, sub_step, 0)


def slab_at(r, kb, freq_count):
    return pl.ds(r * freq_count + kb * ROWS, ROWS)


SQUEEZE = (0, COAST, 4 * COAST, 5 * COAST)


def flow_mask(lane, width, wanted):
    block = lane // width
    forward = ((block == 0) | (block == 3)).astype(jnp.int32)
    return (forward == wanted) & (lane % width < COAST)


def squeeze(fetch, count, chosen):
    out = []
    for start in range(0, count, len(SQUEEZE)):
        total = None
        for i in range(start, min(count, start + len(SQUEEZE))):
            value = turn(jnp.where(chosen, fetch(i), 0.0), SQUEEZE[i - start])
            total = value if total is None else total + value
        out.append(total)
    return out


def loosen(ref, i):
    g, part = divmod(i, len(SQUEEZE))
    return turn(ref[pl.ds(g * ROWS, ROWS), :], -SQUEEZE[part])


def in_stages(groups, stages):
    held = {}
    for t in range(len(groups) + len(stages) - 1):
        for i in reversed(range(len(stages))):
            g = t - i
            if 0 <= g < len(groups):
                held[g] = stages[i](*groups[g], *held.pop(g, ()))


def unpack_turn(value, pack):
    return turn(value, -pack.width)


def near_kernel(one, freq_count, spec_ref, own_ref, send_ref):
    dir_count = one.dir_count
    blocks = freq_count // ROWS
    chunk = ROWS * dir_count
    lane = lanes()
    angles = 2.0 * math.pi * np.arange(dir_count) / dir_count
    first = COAST + REST
    row = lax.broadcasted_iota(jnp.int32, (ROWS, LANES), 0)
    speeds = [
        COURANT_TOP * STATE * jnp.exp((row + kb * ROWS).astype(jnp.float32) * (-math.log(1.1))) for kb in range(blocks)
    ]
    groups = [(kb, range(some, some + 4)) for kb in range(blocks) for some in range(0, one.slabs, 4)]

    def read(kb, slabs):
        here, along = {}, {}
        for r in slabs:
            for b in range(one.blocks):
                j = one.direction(b, r)
                here[r, b] = spec_ref[pl.ds(kb * chunk + j, ROWS, stride=dir_count), :]
        for r, b in here:
            if sine_up(one.direction(b, r), dir_count):
                along[r, b] = turn(here[r, b], 1)
            else:
                along[r, b] = jnp.where(lane == LANES - 1, 0.0, turn(here[r, b], -1))
        return here, along

    def move(kb, slabs, here, along):
        moved = {}
        for r, b in here:
            angle = angles[one.direction(b, r)]
            cosine, sine = float(abs(math.cos(angle))), float(abs(math.sin(angle)))
            value = here[r, b] * (STATE - speeds[kb] * (cosine + sine)) + along[r, b] * (speeds[kb] * sine)
            moved[r, b] = turn(value, b * one.width - first)
        return (moved,)

    def choose(kb, slabs, moved):
        own, sent = {}, {}
        for r in slabs:
            own[r] = sent[r] = moved[r, 0]
            for b in range(1, one.blocks):
                at = b * one.width
                ahead = (at + one.width) % LANES
                own[r] = jnp.where(lane >= at, moved[r, b], own[r])
                reached = lane >= ahead
                if b == one.blocks - 1:
                    reached = reached | (lane < one.width - (LANES - ahead))
                sent[r] = jnp.where(reached, moved[r, b], sent[r])
        return own, {r: unpack_turn(sent[r], one) for r in slabs}

    def store(kb, slabs, own, sent):
        for r in slabs:
            own_ref[slab_at(r, kb, freq_count), :] = own[r]
            send_ref[slab_at(r, kb, freq_count), :] = sent[r]

    in_stages(groups, (read, move, choose, store))


def pack_aux(pack, aux, first, slot, count):
    lane = lanes()
    total = jnp.zeros((ROWS, LANES), jnp.float32)
    for b in range(pack.blocks):
        at = b * pack.width + slot
        total = jnp.where(within(lane, at, count), turn(aux, at - first), total)
    return total


def aux_kernel(one, two, mask_ref, wind_ref, deal_ref, row_ref, own_ref, send_ref):
    mask = mask_ref[...].astype(jnp.float32)
    aux = jnp.concatenate(
        [
            wind_ref[...] * mask,
            (deal_ref[...] + 1).astype(jnp.float32) * mask,
            mask,
            jnp.zeros((ROWS - 4, LANES), jnp.float32),
        ],
        axis=0,
    )
    row_ref[...] = jnp.concatenate(
        [mask, jnp.broadcast_to(mask[:, LANES - 1:LANES], (1, LANES)), jnp.zeros((ROWS - 2, LANES), jnp.float32)], axis=0
    )
    own_ref[pl.ds(0, ROWS), :] = pack_aux(one, aux, COAST + REST, 0, NEAR)
    own_ref[pl.ds(ROWS, ROWS), :] = pack_aux(two, aux, 0, 0, COAST + REST)
    send_ref[pl.ds(0, ROWS), :] = pack_aux(one, aux, FAR, 0, NEAR)
    send_ref[pl.ds(ROWS, ROWS), :] = pack_aux(two, aux, FAR + NEAR, COAST, REST)


def coast_kernel(two, freq_count, code_ref, spec_ref, row_ref, own_ref, send_ref, cross_ref):
    dir_count = two.dir_count
    blocks = freq_count // ROWS
    chunk = ROWS * dir_count
    lane = lanes()
    slot = lane % two.width
    mask = every_row(row_ref[...], 0)
    for kb in range(blocks):
        done = []
        for r in range(two.slabs):
            own, sent = None, None
            for b in range(two.blocks):
                j = two.direction(b, r)
                here = spec_ref[pl.ds(kb * chunk + j, ROWS, stride=dir_count), :] * mask
                here = turn(here, b * two.width)
                block = within(lane, b * two.width, two.width)
                behind = within(lane, (b - 1) % two.blocks * two.width, two.width)
                own = here if b == 0 else jnp.where(block, here, own)
                sent = here if b == 0 else jnp.where(behind, here, sent)
            done.append((own, jnp.where(slot < COAST, own, sent)))
        for r, (own, sent) in enumerate(done):
            own_ref[slab_at(r, kb, freq_count), :] = own
            send_ref[slab_at(r, kb, freq_count), :] = sent

    chosen = flow_mask(lane, two.width, code_ref[0] % 2)
    for g, value in enumerate(squeeze(lambda i: own_ref[pl.ds(i * ROWS, ROWS), :], two.slabs * blocks, chosen)):
        cross_ref[pl.ds(g * ROWS, ROWS), :] = value


NEAR_ENDS = NEAR - 1, 0
REST_ENDS = COAST + REST - 1, COAST


def end_lane(pack, j, ends):
    return pack.find(j)[0] * pack.width + ends[0 if sine_up(j, pack.dir_count) else 1]


def column_lane(one, j):
    return (end_lane(one, j, NEAR_ENDS) + 2 * one.find(j)[1] - 30) % LANES


def take_column(one, pack, ends, fetch, lane):
    total = jnp.zeros((ROWS, LANES), jnp.float32)
    values = [fetch(r) for r in range(pack.slabs)]
    for r, value in enumerate(values):
        turned = {}
        for b in range(pack.blocks):
            j = pack.direction(b, r)
            to = column_lane(one, j)
            by = (to - end_lane(pack, j, ends)) % LANES
            if by not in turned:
                turned[by] = turn(value, by)
            total = jnp.where(lane == to, turned[by], total)
    return total


def store_state(pack, freq_count, e_ref, scale, out_ref):
    for r in range(pack.slabs):
        blocks = range(freq_count // ROWS)
        done = [e_ref[r, pl.ds(PAD + kb * ROWS, ROWS), :] * scale for kb in blocks]
        for kb in blocks:
            out_ref[slab_at(r, kb, freq_count), :] = done[kb]


def one_kernel(one, freq_count, last, table_ref, angle_ref, *refs):
    if last:
        row_ref, in_ref, local_ref, column_ref, out_ref, energy_ref = refs[:6]
        scratch = refs[6:]
    else:
        row_ref, own_ref, got_ref, own_aux, got_aux, out_ref, column_ref = refs[:7]
        scratch = refs[7:]
    e_ref, u_ref, d_ref, n_ref, w_ref, acc_ref, c_ref, known_ref = scratch
    known_ref[...] = table_ref[...]
    blocks = freq_count // ROWS
    lane = lanes()
    for ref in (e_ref, u_ref, d_ref):
        clear(ref, one.slabs, freq_count)
    aux_at = pl.ds(one.slabs * freq_count, ROWS)
    owner = jnp.broadcast_to(row_ref[1:2, :], (ROWS, LANES)) > 0.5
    if last:
        aux = in_ref[aux_at, :]
        up = lane < 0
        for j in range(one.dir_count):
            if sine_up(j, one.dir_count):
                up = up | (lane == column_lane(one, j))
    else:
        aux = jnp.where(owner, own_aux[pl.ds(0, ROWS), :], got_aux[pl.ds(0, ROWS), :])
        out_ref[aux_at, :] = aux
    mask = every_row(aux, 3)
    set_wind(one, freq_count, table_ref, angle_ref, aux, w_ref)
    for kb in range(blocks):
        at = pl.ds(kb * ROWS, ROWS)
        total = jnp.zeros((ROWS, LANES), jnp.float32)
        if last:
            speed = table_ref[0, at, :]
            beyond = jnp.where(up == owner, local_ref[at, :], column_ref[at, :])
        done = []
        if last:
            state = [in_ref[slab_at(r, kb, freq_count), :] for r in range(one.slabs)]
            below = [turn(value, 1) for value in state]
            above = [turn(value, -1) for value in state]
        for r in range(one.slabs):
            if last:
                here = state[r]
                along = jnp.where(angle_ref[1, r] > 0, below[r], above[r])
                for b in range(one.blocks):
                    j = one.direction(b, r)
                    to = b * one.width + (0 if sine_up(j, one.dir_count) else NEAR - 1)
                    along = jnp.where(lane == to, turn(beyond, to - column_lane(one, j)), along)
                start = (
                    here
                    - speed * angle_ref[2, r] * here
                    - speed * angle_ref[3, r] * (here - along)
                ) * (mask * STATE)
            else:
                start = jnp.where(owner, own_ref[slab_at(r, kb, freq_count), :], got_ref[slab_at(r, kb, freq_count), :])
            done.append(start)
            total = total + start
        for r, start in enumerate(done):
            e_ref[r, pl.ds(PAD + kb * ROWS, ROWS), :] = start
        acc_ref[at, :] = total

    @pl.when(jnp.max(aux[3:4]) > 0.5)
    def _():
        sub_steps(one, freq_count, known_ref, e_ref, u_ref, d_ref, n_ref, w_ref, acc_ref, c_ref)

    store_state(one, freq_count, e_ref, mask * (1.0 / STATE), out_ref)
    if last:
        energy = jnp.sum(acc_ref[...], axis=0, keepdims=True) * (mask[0:1] * (1.0 / (STATE * freq_count * one.dir_count)))
        energy_ref[...] = jnp.concatenate(
            [energy, aux[2:3] - 1.0, jnp.zeros((ROWS - 2, LANES), jnp.float32)], axis=0
        )
    else:
        for kb in range(blocks):
            column_ref[pl.ds(kb * ROWS, ROWS), :] = take_column(
                one, one, NEAR_ENDS, lambda r: out_ref[slab_at(r, kb, freq_count), :], lane
            )


def two_kernel(one, two, freq_count, slot_count, last, code_ref, table_ref, angle_ref, row_ref, *refs):
    if last:
        in_ref, pair_ref, cross_ref, local_ref, other_ref, out_ref, energy_ref = refs[:7]
        scratch = refs[7:]
    else:
        own_ref, got_ref, own_aux, got_aux, cross_ref, out_ref, column_ref, pair_out, cross_out = refs[:9]
        scratch = refs[9:]
    e_ref, u_ref, d_ref, n_ref, w_ref, acc_ref, c_ref, known_ref = scratch
    known_ref[...] = table_ref[...]
    blocks = freq_count // ROWS
    lane = lanes()
    slot = lane % two.width
    for ref in (e_ref, u_ref, d_ref):
        clear(ref, two.slabs, freq_count)
    aux_at = pl.ds(two.slabs * freq_count, ROWS)
    parity = code_ref[0] % 2
    inner = (code_ref[0] < 2).astype(jnp.float32)
    owner = jnp.broadcast_to(row_ref[1:2, :], (ROWS, LANES)) > 0.5
    from_cross = flow_mask(lane, two.width, 1 - parity)
    from_pair = flow_mask(lane, two.width, parity)
    if last:
        aux = in_ref[aux_at, :]
        mask = every_row(aux, 3)
    else:
        second = pl.ds(ROWS, ROWS)
        aux = own_aux[second, :] + got_aux[second, :]
        out_ref[aux_at, :] = aux
        mask, got_mask = every_row(own_aux[second, :], 3), every_row(got_aux[second, :], 3)
    set_wind(two, freq_count, table_ref, angle_ref, aux, w_ref)
    for kb in range(blocks):
        at = pl.ds(kb * ROWS, ROWS)
        speed = table_ref[0, at, :]
        total = jnp.zeros((ROWS, LANES), jnp.float32)
        done = []
        slabs = range(two.slabs)
        upward = [angle_ref[1, r] > 0 for r in slabs]
        flow_x = [speed * angle_ref[2, r] for r in slabs]
        flow_y = [speed * angle_ref[3, r] for r in slabs]

        def neighbours(values):
            below = [turn(value, 1) for value in values]
            above = [turn(value, -1) for value in values]
            return [jnp.where(upward[r], below[r], above[r]) for r in slabs]

        here = [(in_ref if last else own_ref)[slab_at(r, kb, freq_count), :] for r in slabs]
        along = neighbours(here)
        across = [loosen(cross_ref, r * blocks + kb) * inner for r in slabs]
        if last:
            beside = [loosen(pair_ref, r * blocks + kb) for r in slabs]
        else:
            beside = [got_ref[slab_at(r, kb, freq_count), :] for r in slabs]
        for r in slabs:
            nearby = jnp.where(from_cross, across[r], jnp.where(from_pair, beside[r], 0.0))
            if last:
                beyond = local_ref[at, :]
                for b in range(two.blocks):
                    j = two.direction(b, r)
                    start = b * two.width
                    if sine_up(j, two.dir_count):
                        to = start + COAST
                        along[r] = jnp.where((lane == to) & ~owner, turn(beyond, to - column_lane(one, j)), along[r])
                    else:
                        to = start + COAST + REST - 1
                        along[r] = jnp.where((lane == to) & owner, turn(beyond, to - column_lane(one, j)), along[r])
                        along[r] = jnp.where((lane == start + COAST - 1) & ~owner, 0.0, along[r])
            else:
                along[r] = jnp.where((slot == 0) & upward[r], 0.0, along[r])
            done.append(
                (here[r] - flow_x[r] * (here[r] - nearby) - flow_y[r] * (here[r] - along[r])) * (mask * STATE)
            )
        if not last:
            here = [turn(beside[r], COAST + REST) for r in slabs]
            along = neighbours(here)
            for r in slabs:
                nearby = jnp.where((slot == COAST + REST - 1) & ~upward[r], 0.0, along[r])
                done[r] = done[r] + (
                    here[r] - flow_x[r] * here[r] - flow_y[r] * (here[r] - nearby)
                ) * (got_mask * STATE)
        for r in slabs:
            total = total + done[r]
        for r, start in enumerate(done):
            e_ref[r, pl.ds(PAD + kb * ROWS, ROWS), :] = start
        acc_ref[at, :] = total
    if last:
        cards = energy_ref.shape[0]
        card = lax.broadcasted_iota(jnp.int32, (cards, LANES), 0) * slot_count
        place = lax.broadcasted_iota(jnp.int32, (LANES, LANES), 0)

        def to_cards(energy, deal):
            deal = deal.astype(jnp.int32)
            to_card = jnp.where((deal >= card) & (deal < card + slot_count), energy, 0.0)
            to_slot = (lax.rem(jnp.maximum(deal, 0), slot_count) == place).astype(jnp.float32)
            return lax.dot_general(
                to_card, to_slot, (((1,), (1,)), ((), ())),
                precision=lax.Precision.HIGHEST, preferred_element_type=jnp.float32,
            )

        elsewhere = to_cards(other_ref[0:1], other_ref[1:2])
    sub_steps(two, freq_count, known_ref, e_ref, u_ref, d_ref, n_ref, w_ref, acc_ref, c_ref)
    scale = every_row(aux, 3) * (1.0 / STATE)
    store_state(two, freq_count, e_ref, scale, out_ref)
    if last:
        energy = jnp.sum(acc_ref[...], axis=0, keepdims=True) * (scale[0:1] / (freq_count * two.dir_count))
        energy_ref[...] = elsewhere + to_cards(energy, aux[2:3] - 1.0)
    else:
        for kb in range(blocks):
            column_ref[pl.ds(kb * ROWS, ROWS), :] = take_column(
                one, two, REST_ENDS, lambda r: out_ref[slab_at(r, kb, freq_count), :], lane
            )
        for ref, wanted in ((pair_out, 1 - parity), (cross_out, parity)):
            chosen = flow_mask(lane, two.width, wanted)
            for g, value in enumerate(
                squeeze(lambda i: out_ref[pl.ds(i * ROWS, ROWS), :], two.slabs * blocks, chosen)
            ):
                ref[pl.ds(g * ROWS, ROWS), :] = value


def gather_kernel(
    one, two, freq_count, row_ref, one_ref, one_got, two_ref, two_got, out_hbm, after_ref, out_ref, sems
):
    dir_count = one.dir_count
    chunk = ROWS * dir_count
    lane = lanes()
    mask = every_row(row_ref[...], 0)
    copies = []
    for kb in range(freq_count // ROWS):
        near = [turn(one_got[slab_at(r, kb, freq_count), :], one.width) for r in range(one.slabs)]
        coast = [turn(two_got[slab_at(r, kb, freq_count), :], -(COAST + REST)) for r in range(two.slabs)]
        for some in range(0, dir_count, 12):
            js = range(some, some + 12)
            value, rest = {}, {}
            for j in js:
                b, r = one.find(j)
                start = b * one.width
                mixed = jnp.where(within(lane, start, one.width), one_ref[slab_at(r, kb, freq_count), :], near[r])
                value[j] = turn(mixed, COAST + REST - start)
            for j in js:
                b, r = two.find(j)
                start = b * two.width
                mixed = jnp.where(within(lane, start, COAST + REST), two_ref[slab_at(r, kb, freq_count), :], coast[r])
                rest[j] = turn(mixed, -start)
            for j in js:
                whole = jnp.where(within(lane, COAST + REST, 2 * NEAR), value[j], rest[j]) * mask
                out_ref[pl.ds(kb * chunk + j, ROWS, stride=dir_count), :] = whole
        rows = pl.ds(kb * chunk, chunk)
        copies.append(pltpu.make_async_copy(out_ref.at[rows], out_hbm.at[rows], sems.at[kb]))
        copies[kb].start()
    for copy in copies:
        copy.wait()
    after_ref[...] = row_ref[...]


def energy_kernel(shared_ref, after_ref, energy_ref):
    energy_ref[...] = jnp.sum(shared_ref[...], axis=0, keepdims=True)[:, :energy_ref.shape[1]]


def coast_width(tile_count, cell_count):
    capacity = cell_count // tile_count
    spread = tile_count * (tile_count - 8) // 8
    return -(-spread // (tile_count - 1)) * capacity


def shards(spectrum, sea_mask, card_deal, wind):
    freq_count, dir_count, row_count, row_width = spectrum.shape
    cell_count = row_count * row_width
    tile_count = lax.axis_size("tile")
    slot_count = cell_count // 8
    assert row_count == 1 and cell_count == LANES and coast_width(tile_count, cell_count) <= COAST
    here = lax.axis_index("tile")
    at_end = (here == 0) | (here == tile_count - 1)
    code = (here % 2 + 2 * at_end.astype(jnp.int32)).astype(jnp.int32).reshape(1)
    one, two = Pack(3, NEAR, dir_count, 0), Pack(4, 32, dir_count, 1)
    table = jnp.asarray(tables(freq_count, dir_count))
    one_rows, two_rows = one.slabs * freq_count, two.slabs * freq_count
    squeezed = -(-two_rows // ROWS // len(SQUEEZE)) * ROWS

    def array(*shape):
        return jax.ShapeDtypeStruct(shape, jnp.float32)

    smem = pl.BlockSpec(memory_space=pltpu.SMEM)
    vmem = pl.BlockSpec(memory_space=pltpu.VMEM)
    hbm = pl.BlockSpec(memory_space=pltpu.HBM)

    def params(rows, steps=SUB, vmem=48):
        return dict(
            compiler_params=pltpu.CompilerParams(vmem_limit_bytes=vmem * 1024 * 1024),
            cost_estimate=pl.CostEstimate(
                flops=rows // ROWS * steps * 8_000_000, bytes_accessed=8 * rows * LANES, transcendentals=0
            ),
        )

    def scratch(pack):
        padded = pltpu.VMEM((pack.slabs, freq_count + 2 * PAD, LANES), jnp.float32)
        plain = pltpu.VMEM((pack.slabs, freq_count, LANES), jnp.float32)
        column = pltpu.VMEM((freq_count, LANES), jnp.float32)
        return [padded, padded, padded, plain, plain, column, column, pltpu.VMEM(table.shape, jnp.float32)]

    group_count = lax.axis_size("groups")
    chip_swap = []
    for g in range(group_count):
        for i in range(tile_count):
            other, there = g, (i + 1 if i % 2 else i - 1)
            if not 0 <= there < tile_count:
                other, there = (g ^ 1 if g ^ 1 < group_count else g), i
            chip_swap.append((g * tile_count + i, other * tile_count + there))

    def to_pair(value):
        return lax.ppermute(value, "tile", [(i, i ^ 1) for i in range(tile_count)])

    def to_next(value):
        return lax.ppermute(value, ("groups", "tile"), chip_swap)

    one_angles, two_angles = jnp.asarray(one.rows()), jnp.asarray(two.rows())
    flat = spectrum.reshape(freq_count * dir_count, cell_count)
    whole = pltpu.VMEM((freq_count * dir_count, LANES), jnp.float32)
    chunks = pltpu.SemaphoreType.DMA((freq_count // ROWS,))
    one_own, one_send = pl.pallas_call(
        functools.partial(near_kernel, one, freq_count),
        out_shape=(array(one_rows, LANES), array(one_rows, LANES)),
        in_specs=[vmem],
        out_specs=(vmem,) * 2,
        name="near",
        **params(1440, 1),
    )(flat)
    row, own_aux, send_aux = pl.pallas_call(
        functools.partial(aux_kernel, one, two),
        out_shape=(array(ROWS, LANES), array(2 * ROWS, LANES), array(2 * ROWS, LANES)),
        in_specs=[vmem] * 3,
        out_specs=(vmem,) * 3,
        name="aux",
        **params(80, 1),
    )(sea_mask, wind.reshape(2, cell_count), card_deal)
    one_got = to_pair(one_send)
    got_aux = to_pair(send_aux)
    two_own, two_send, cross = pl.pallas_call(
        functools.partial(coast_kernel, two, freq_count),
        out_shape=(array(two_rows, LANES), array(two_rows, LANES), array(squeezed, LANES)),
        in_specs=[smem, vmem, vmem],
        out_specs=(vmem,) * 3,
        name="coast",
        **params(1440, 1),
    )(code, flat, row)
    cross_got = to_next(cross)
    two_got = to_pair(two_send)
    one_state, one_column = pl.pallas_call(
        functools.partial(one_kernel, one, freq_count, False),
        out_shape=(array(one_rows + ROWS, LANES), array(freq_count, LANES)),
        in_specs=[vmem] * 7,
        out_specs=(vmem,) * 2,
        scratch_shapes=scratch(one),
        name="first_one",
        **params(one_rows),
    )(table, one_angles, row, one_own, one_got, own_aux, got_aux)
    column_got = to_pair(one_column)
    two_state, two_column, pair, cross = pl.pallas_call(
        functools.partial(two_kernel, one, two, freq_count, slot_count, False),
        out_shape=(
            array(two_rows + ROWS, LANES), array(freq_count, LANES), array(squeezed, LANES), array(squeezed, LANES),
        ),
        in_specs=[smem] + [vmem] * 8,
        out_specs=(vmem,) * 4,
        scratch_shapes=scratch(two),
        name="first_two",
        **params(two_rows),
    )(code, table, two_angles, row, two_own, two_got, own_aux, got_aux, cross_got)
    cross_got = to_next(cross)
    pair_got = to_pair(pair)
    one_state, one_energy = pl.pallas_call(
        functools.partial(one_kernel, one, freq_count, True),
        out_shape=(array(one_rows, LANES), array(ROWS, LANES)),
        in_specs=[vmem] * 6,
        out_specs=(vmem,) * 2,
        scratch_shapes=scratch(one),
        name="second_one",
        **params(one_rows),
    )(table, one_angles, row, one_state, two_column, column_got)
    one_got = to_pair(one_state)
    two_state, energy = pl.pallas_call(
        functools.partial(two_kernel, one, two, freq_count, slot_count, True),
        out_shape=(array(two_rows, LANES), array(tile_count, LANES)),
        in_specs=[smem] + [vmem] * 8,
        out_specs=(vmem,) * 2,
        scratch_shapes=scratch(two),
        name="second_two",
        **params(two_rows),
    )(code, table, two_angles, row, two_state, pair_got, cross_got, one_column, one_energy)
    two_got = to_pair(two_state)
    shared = lax.all_to_all(
        energy.reshape(tile_count, 1, LANES), "tile", split_axis=0, concat_axis=0, tiled=True
    )
    out, after = pl.pallas_call(
        functools.partial(gather_kernel, one, two, freq_count),
        out_shape=(array(freq_count * dir_count, LANES), array(ROWS, LANES)),
        in_specs=[vmem] * 5,
        out_specs=(hbm, vmem),
        scratch_shapes=[whole, chunks],
        name="gather",
        **params(1440, 1),
    )(row, one_state, one_got, two_state, two_got)
    card_energy = pl.pallas_call(
        energy_kernel,
        out_shape=array(1, slot_count),
        in_specs=[vmem] * 2,
        out_specs=vmem,
        name="energy",
        **params(80, 1),
    )(shared.reshape(tile_count, LANES), after)
    return out.reshape(freq_count, dir_count, row_count, row_width), card_energy.reshape(slot_count)


def solution(mesh):
    placed = (
        P(None, None, ("groups", "tile"), None),
        P(("groups", "tile"), None),
        P(("groups", "tile"), None),
        P(None, ("groups", "tile"), None),
    )
    return jax.shard_map(
        shards,
        mesh=mesh,
        in_specs=placed,
        out_specs=(P(None, None, ("groups", "tile"), None), P(("groups", "tile"))),
        check_vma=False,
    )
```

```python
import functools
import math

import jax
import jax.numpy as jnp
import numpy as np
from jax import lax
from jax.experimental import pallas as pl
from jax.experimental.pallas import tpu as pltpu
from jax.sharding import PartitionSpec as P

STEPS = 2
SUB = 8
COURANT_TOP = 0.7
WIND_RATE = 0.15
DECAY_RATE = 0.3
QUAD_RATE = 0.5
LIMITER = 0.25
ANGLE_UP = -11.48
ANGLE_DOWN = 33.56
SHIFT_UP = math.log(1.25) / math.log(1.1)
SHIFT_DOWN = math.log(0.75) / math.log(1.1)
GAIN_UP = 1.25 ** (-4)
GAIN_DOWN = 0.75 ** (-4)
GAIN_BOTH = 0.9375 ** (-4)

LANES = 128
ROWS = 8
PAD = 4


def split(offset):
    base = math.floor(offset)
    return base, offset - base


GAIN = 2.0 * GAIN_BOTH / (GAIN_UP * GAIN_DOWN)
STATE = SUB / LIMITER
UP_K, UP_W = split(SHIFT_UP)
DOWN_K, DOWN_W = split(SHIFT_DOWN)

COAST = 16
NEAR = 42
REST = 14
FAR = COAST + REST + NEAR


class Pack:
    def __init__(self, blocks, width, dir_count, offset):
        self.blocks, self.width, self.offset = blocks, width, offset
        self.slabs = dir_count // blocks
        self.dir_count = dir_count

    def direction(self, block, slab):
        return (block * self.slabs + slab + self.offset) % self.dir_count

    def find(self, j):
        return divmod((j - self.offset) % self.dir_count, self.slabs)

    def next_block(self, value, lane):
        if self.blocks * self.width == LANES:
            return turn(value, -self.width)
        last = (self.blocks - 1) * self.width
        return jnp.take_along_axis(value, jnp.where(lane < last, lane + self.width, lane - last), axis=1)

    def block_before(self, value, lane):
        if self.blocks * self.width == LANES:
            return turn(value, self.width)
        last = (self.blocks - 1) * self.width
        source = jnp.where(lane >= self.width, lane - self.width, lane + last)
        return jnp.take_along_axis(value, jnp.minimum(source, LANES - 1), axis=1)

    def over_blocks(self, value, lane):
        if self.blocks == 4:
            value = value + turn(value, 2 * self.width)
            return value + turn(value, self.width)
        total = value
        for b in range(1, self.blocks):
            total = total + turn(value, -b * self.width)
        spread = total
        for b in range(1, self.blocks):
            spread = jnp.where(lane >= b * self.width, turn(total, b * self.width), spread)
        return spread

    def rows(self):
        angles = 2.0 * math.pi * np.arange(self.dir_count) / self.dir_count
        out = np.zeros((4, self.slabs, LANES))
        for r in range(self.slabs):
            for b in range(self.blocks):
                at = slice(b * self.width, (b + 1) * self.width)
                angle = angles[self.direction(b, r)]
                out[:, r, at] = np.array(
                    [math.cos(angle), math.sin(angle), abs(math.cos(angle)), abs(math.sin(angle))]
                )[:, None]
        return np.broadcast_to(out[:, :, None, :], (4, self.slabs, ROWS, LANES)).astype(np.float32)


def turn(value, by):
    by %= LANES
    return pltpu.roll(value, by, 1) if by else value


def lanes():
    return lax.broadcasted_iota(jnp.int32, (ROWS, LANES), 1)


def every_row(value, row):
    return jnp.broadcast_to(value[row:row + 1, :], (ROWS, LANES))


def within(lane, first, count):
    return (lane >= first) & (lane < first + count)


def sine_up(j, dir_count):
    return math.sin(2.0 * math.pi * j / dir_count) > 0


def tables(freq_count, dir_count):
    levels = 3.0 ** (np.arange(freq_count) / (freq_count - 1))
    speeds = COURANT_TOP * 1.1 ** (-np.arange(freq_count, dtype=np.float64))
    up_j, up_z = split(ANGLE_UP * dir_count / 360.0)
    rate = (1.0 - UP_W) * up_z / LIMITER
    rows = [
        speeds,
        rate * QUAD_RATE / (GAIN * STATE ** 3) * levels,
        WIND_RATE * 0.5 / (LIMITER * STATE) * levels,
        levels / (dir_count * np.sum(levels) * STATE),
        DECAY_RATE / (LIMITER * STATE) * levels,
    ]
    return np.broadcast_to(
        np.stack(rows)[:, :, None], (len(rows), freq_count, LANES)
    ).astype(np.float32)


def clear(ref, slabs, freq_count):
    zero = jnp.zeros((PAD, LANES), jnp.float32)
    for r in range(slabs):
        ref[r, pl.ds(0, PAD), :] = zero
        ref[r, pl.ds(PAD + freq_count, PAD), :] = zero


def set_wind(pack, freq_count, table_ref, angle_ref, aux, w_ref):
    east, north = every_row(aux, 0), every_row(aux, 1)
    for r in range(pack.slabs):
        drive = east * angle_ref[0, r] + north * angle_ref[1, r]
        for kb in range(freq_count // ROWS):
            at = pl.ds(kb * ROWS, ROWS)
            w_ref[r, at, :] = jnp.maximum(table_ref[2, at, :] * drive - WIND_RATE / (LIMITER * STATE), 0.0)


def sub_steps(pack, freq_count, table_ref, e_ref, u_ref, d_ref, n_ref, w_ref, acc_ref, c_ref):
    slabs, blocks = pack.slabs, freq_count // ROWS
    lane = lanes()
    up_j, up_z = split(ANGLE_UP * pack.dir_count / 360.0)
    down_j, down_z = split(ANGLE_DOWN * pack.dir_count / 360.0)
    up_near, up_far = up_j + 1, up_j
    up_weight, up_rest = up_z, (1.0 - up_z) / up_z
    down_near, down_far = down_j, down_j + 1
    down_weight, down_rest = 1.0 - down_z, down_z / (1.0 - down_z)
    up_scale = GAIN_UP * GAIN * up_weight
    down_scale = GAIN_DOWN * GAIN * down_weight
    fold = (1.0 - UP_W) * up_weight
    up_tail = UP_W / (1.0 - UP_W)
    down_head = (1.0 - DOWN_W) * down_weight / fold
    down_tail = DOWN_W * down_weight / fold
    own = -2.0 / fold

    def around(known, make, r):
        if r not in known:
            if r < 0:
                known[r] = pack.block_before(around(known, make, r + slabs), lane)
            elif r >= slabs:
                known[r] = pack.next_block(around(known, make, r - slabs), lane)
            else:
                known[r] = make(r)
        return known[r]

    def stage_a(kb):
        base = kb * ROWS
        strength = table_ref[1, pl.ds(base, ROWS), :]
        up, down, more, less, up_c, down_c, centre = {}, {}, {}, {}, {}, {}, {}

        def read(r, offset):
            return e_ref[r, pl.ds(base + PAD + offset, ROWS), :]

        def make_up(r):
            return (up_scale * (1.0 - UP_W)) * read(r, UP_K) + (up_scale * UP_W) * read(r, UP_K + 1)

        def make_down(r):
            return (down_scale * (1.0 - DOWN_W)) * read(r, DOWN_K) + (down_scale * DOWN_W) * read(r, DOWN_K + 1)

        def get_up(r):
            return around(up, make_up, r)

        def get_down(r):
            return around(down, make_down, r)

        def get_up_c(r):
            if r not in up_c:
                up_c[r] = get_up(r) * up_rest
            return up_c[r]

        def get_down_c(r):
            if r not in down_c:
                down_c[r] = get_down(r) * down_rest
            return down_c[r]

        def make_quad(r, sign):
            if r not in centre:
                here = read(r, 0)
                centre[r] = here, here * strength
            here, gain = centre[r]
            plus = get_up(r + sign * up_near) + get_up_c(r + sign * up_far)
            minus = get_down(r + sign * down_near) + get_down_c(r + sign * down_far)
            return gain * (here * (plus + minus) - plus * minus)

        def get_more(r):
            return around(more, lambda r: make_quad(r, 1), r)

        def get_less(r):
            return around(less, lambda r: make_quad(r, -1), r)

        if slabs > 9:
            for r in (slabs - 2, slabs - 1, 0, 1):
                get_up(r)
            for r in (*range(slabs - 4, slabs), *range(4)):
                get_down(r)
            for r in (-2, -1, slabs, slabs + 1):
                get_up(r)
            for r in (*range(-4, 0), *range(slabs, slabs + 4)):
                get_down(r)
            for r in (*range(slabs - 4, slabs), 0, 1):
                get_more(r)
            for r in (slabs - 2, slabs - 1, *range(4)):
                get_less(r)
            for r in (*range(-4, 0), slabs, slabs + 1):
                get_more(r)
            for r in (-2, -1, *range(slabs, slabs + 4)):
                get_less(r)
            order = (*range(4, slabs - 4), *range(4), *range(slabs - 4, slabs))
        else:
            order = range(slabs)
        for r in order:
            u_ref[r, pl.ds(base + PAD, ROWS), :] = (
                get_more(r - up_near) + get_less(r + up_near)
            ) + up_rest * (get_more(r - up_far) + get_less(r + up_far))
            d_ref[r, pl.ds(base + PAD, ROWS), :] = (
                get_more(r - down_near) + get_less(r + down_near)
            ) + down_rest * (get_more(r - down_far) + get_less(r + down_far))
            n_ref[r, pl.ds(base, ROWS), :] = own * (get_more(r) + get_less(r))

    def stage_b(kb):
        base = kb * ROWS
        decay = c_ref[pl.ds(base, ROWS), :]
        total = jnp.zeros((ROWS, LANES), jnp.float32)
        for r in range(slabs):
            here = e_ref[r, pl.ds(base + PAD, ROWS), :]
            rate = here * (w_ref[r, pl.ds(base, ROWS), :] - decay) + n_ref[r, pl.ds(base, ROWS), :]
            rate = rate + (
                u_ref[r, pl.ds(base + PAD - UP_K, ROWS), :]
                + up_tail * u_ref[r, pl.ds(base + PAD - UP_K - 1, ROWS), :]
            )
            rate = rate + (
                down_head * d_ref[r, pl.ds(base + PAD - DOWN_K, ROWS), :]
                + down_tail * d_ref[r, pl.ds(base + PAD - DOWN_K - 1, ROWS), :]
            )
            here = here + jnp.tanh(rate)
            e_ref[r, pl.ds(base + PAD, ROWS), :] = here
            total = total + here
        acc_ref[pl.ds(base, ROWS), :] = total

    def sub_step(index, carry):
        steepness = jnp.sum(acc_ref[...] * table_ref[3], axis=0, keepdims=True)
        steepness = pack.over_blocks(jnp.broadcast_to(steepness, (ROWS, LANES)), lane)[0:1]
        c_ref[...] = steepness * table_ref[4]
        for kb in range(blocks):
            stage_a(kb)
        for kb in range(blocks):
            stage_b(kb)
        return carry

    lax.fori_loop(0, SUB, sub_step, 0)


def slab_at(r, kb, freq_count, base=0):
    return pl.ds(base + r * freq_count + kb * ROWS, ROWS)


SQUEEZE = (0, COAST)


def flow_mask(lane, width, wanted):
    block = lane // width
    forward = ((block == 0) | (block == 3)).astype(jnp.int32)
    return (forward == wanted) & (lane % width < COAST)


def squeeze(fetch, count, chosen):
    out = []
    for start in range(0, count, len(SQUEEZE)):
        total = None
        for i in range(start, min(count, start + len(SQUEEZE))):
            value = turn(jnp.where(chosen, fetch(i), 0.0), SQUEEZE[i - start])
            total = value if total is None else total + value
        out.append(total)
    return out


def loosen(ref, i):
    g, part = divmod(i, len(SQUEEZE))
    return turn(ref[pl.ds(g * ROWS, ROWS), :], -SQUEEZE[part])


def in_stages(groups, stages):
    held = {}
    for t in range(len(groups) + len(stages) - 1):
        for i in reversed(range(len(stages))):
            g = t - i
            if 0 <= g < len(groups):
                held[g] = stages[i](*groups[g], *held.pop(g, ()))


def unpack_turn(value, pack):
    return turn(value, -pack.width)


def near_kernel(one, freq_count, spec_ref, own_ref, send_ref):
    dir_count = one.dir_count
    blocks = freq_count // ROWS
    chunk = ROWS * dir_count
    lane = lanes()
    angles = 2.0 * math.pi * np.arange(dir_count) / dir_count
    first = COAST + REST
    row = lax.broadcasted_iota(jnp.int32, (ROWS, LANES), 0)
    speeds = [
        COURANT_TOP * STATE * jnp.exp((row + kb * ROWS).astype(jnp.float32) * (-math.log(1.1))) for kb in range(blocks)
    ]
    groups = [(kb, range(some, some + 4)) for kb in range(blocks) for some in range(0, one.slabs, 4)]

    def read(kb, slabs):
        here, along = {}, {}
        for r in slabs:
            for b in range(one.blocks):
                j = one.direction(b, r)
                here[r, b] = spec_ref[pl.ds(kb * chunk + j, ROWS, stride=dir_count), :]
        for r, b in here:
            if sine_up(one.direction(b, r), dir_count):
                along[r, b] = turn(here[r, b], 1)
            else:
                along[r, b] = jnp.where(lane == LANES - 1, 0.0, turn(here[r, b], -1))
        return here, along

    def move(kb, slabs, here, along):
        moved = {}
        for r, b in here:
            angle = angles[one.direction(b, r)]
            cosine, sine = float(abs(math.cos(angle))), float(abs(math.sin(angle)))
            value = here[r, b] * (STATE - speeds[kb] * (cosine + sine)) + along[r, b] * (speeds[kb] * sine)
            moved[r, b] = turn(value, b * one.width - first)
        return (moved,)

    def choose(kb, slabs, moved):
        own, sent = {}, {}
        for r in slabs:
            own[r] = sent[r] = moved[r, 0]
            for b in range(1, one.blocks):
                at = b * one.width
                ahead = (at + one.width) % LANES
                own[r] = jnp.where(lane >= at, moved[r, b], own[r])
                reached = lane >= ahead
                if b == one.blocks - 1:
                    reached = reached | (lane < one.width - (LANES - ahead))
                sent[r] = jnp.where(reached, moved[r, b], sent[r])
        return own, {r: unpack_turn(sent[r], one) for r in slabs}

    def store(kb, slabs, own, sent):
        for r in slabs:
            own_ref[slab_at(r, kb, freq_count), :] = own[r]
            send_ref[slab_at(r, kb, freq_count), :] = sent[r]

    in_stages(groups, (read, move, choose, store))


def pack_aux(pack, aux, first, slot, count):
    lane = lanes()
    total = jnp.zeros((ROWS, LANES), jnp.float32)
    for b in range(pack.blocks):
        at = b * pack.width + slot
        total = jnp.where(within(lane, at, count), turn(aux, at - first), total)
    return total


def aux_rows(one, two, mask, wind, deal):
    aux = jnp.concatenate(
        [wind * mask, (deal + 1).astype(jnp.float32) * mask, mask, jnp.zeros((ROWS - 4, LANES), jnp.float32)], axis=0
    )
    own = pack_aux(one, aux, COAST + REST, 0, NEAR), pack_aux(two, aux, 0, 0, COAST + REST)
    sent = pack_aux(one, aux, FAR, 0, NEAR), pack_aux(two, aux, FAR + NEAR, COAST, REST)
    return jnp.concatenate(own, axis=0), jnp.concatenate(sent, axis=0)


def coast_kernel(
    one, two, freq_count, spec_ref, mask_ref, wind_ref, deal_ref,
    own_ref, send_ref, cross_ref, row_ref, own_aux,
):
    dir_count = two.dir_count
    blocks = freq_count // ROWS
    chunk = ROWS * dir_count
    lane = lanes()
    slot = lane % two.width
    mask = mask_ref[...].astype(jnp.float32)
    row_ref[...] = jnp.concatenate(
        [mask, jnp.broadcast_to(mask[:, LANES - 1:LANES], (1, LANES)), jnp.zeros((ROWS - 2, LANES), jnp.float32)], axis=0
    )
    own, sent = aux_rows(one, two, mask, wind_ref[...], deal_ref[...])
    own_aux[...] = own
    send_ref[pl.ds(two.slabs * freq_count, 2 * ROWS), :] = sent
    mask = every_row(mask, 0)
    for kb in range(blocks):
        done = []
        for r in range(two.slabs):
            own, sent = None, None
            for b in range(two.blocks):
                j = two.direction(b, r)
                here = spec_ref[pl.ds(kb * chunk + j, ROWS, stride=dir_count), :] * mask
                here = turn(here, b * two.width)
                block = within(lane, b * two.width, two.width)
                behind = within(lane, (b - 1) % two.blocks * two.width, two.width)
                own = here if b == 0 else jnp.where(block, here, own)
                sent = here if b == 0 else jnp.where(behind, here, sent)
            done.append((own, jnp.where(slot < COAST, own, sent)))
        for r, (own, sent) in enumerate(done):
            own_ref[slab_at(r, kb, freq_count), :] = own
            send_ref[slab_at(r, kb, freq_count), :] = sent

    for g, value in enumerate(squeeze(lambda i: own_ref[pl.ds(i * ROWS, ROWS), :], two.slabs * blocks, slot < COAST)):
        cross_ref[pl.ds(g * ROWS, ROWS), :] = value


NEAR_ENDS = NEAR - 1, 0
REST_ENDS = COAST + REST - 1, COAST


def end_lane(pack, j, ends):
    return pack.find(j)[0] * pack.width + ends[0 if sine_up(j, pack.dir_count) else 1]


def column_lane(one, j):
    return (end_lane(one, j, NEAR_ENDS) + 2 * one.find(j)[1] - 30) % LANES


def take_column(one, pack, ends, fetch, lane):
    total = jnp.zeros((ROWS, LANES), jnp.float32)
    values = [fetch(r) for r in range(pack.slabs)]
    for r, value in enumerate(values):
        turned = {}
        for b in range(pack.blocks):
            j = pack.direction(b, r)
            to = column_lane(one, j)
            by = (to - end_lane(pack, j, ends)) % LANES
            if by not in turned:
                turned[by] = turn(value, by)
            total = jnp.where(lane == to, turned[by], total)
    return total


def store_state(pack, freq_count, e_ref, scale, out_ref):
    for r in range(pack.slabs):
        blocks = range(freq_count // ROWS)
        done = [e_ref[r, pl.ds(PAD + kb * ROWS, ROWS), :] * scale for kb in blocks]
        for kb in blocks:
            out_ref[slab_at(r, kb, freq_count), :] = done[kb]


def one_kernel(one, freq_count, last, table_ref, angle_ref, *refs):
    if last:
        row_ref, in_ref, local_ref, column_ref, out_ref, energy_ref = refs[:6]
        scratch = refs[6:]
    else:
        row_ref, own_ref, got_ref, own_aux, got_aux, out_ref, column_ref = refs[:7]
        scratch = refs[7:]
    e_ref, u_ref, d_ref, n_ref, w_ref, acc_ref, c_ref, known_ref = scratch
    known_ref[...] = table_ref[...]
    blocks = freq_count // ROWS
    lane = lanes()
    for ref in (e_ref, u_ref, d_ref):
        clear(ref, one.slabs, freq_count)
    aux_at = pl.ds(one.slabs * freq_count, ROWS)
    owner = jnp.broadcast_to(row_ref[1:2, :], (ROWS, LANES)) > 0.5
    if last:
        aux = in_ref[aux_at, :]
        up = lane < 0
        for j in range(one.dir_count):
            if sine_up(j, one.dir_count):
                up = up | (lane == column_lane(one, j))
    else:
        aux = jnp.where(owner, own_aux[pl.ds(0, ROWS), :], got_aux[pl.ds(got_aux.shape[0] - 2 * ROWS, ROWS), :])
        out_ref[aux_at, :] = aux
    mask = every_row(aux, 3)
    set_wind(one, freq_count, table_ref, angle_ref, aux, w_ref)
    for kb in range(blocks):
        at = pl.ds(kb * ROWS, ROWS)
        total = jnp.zeros((ROWS, LANES), jnp.float32)
        if last:
            speed = table_ref[0, at, :]
            beyond = jnp.where(up == owner, local_ref[at, :], column_ref[at, :])
        done = []
        if last:
            state = [in_ref[slab_at(r, kb, freq_count), :] for r in range(one.slabs)]
            below = [turn(value, 1) for value in state]
            above = [turn(value, -1) for value in state]
        for r in range(one.slabs):
            if last:
                here = state[r]
                along = jnp.where(angle_ref[1, r] > 0, below[r], above[r])
                for b in range(one.blocks):
                    j = one.direction(b, r)
                    to = b * one.width + (0 if sine_up(j, one.dir_count) else NEAR - 1)
                    along = jnp.where(lane == to, turn(beyond, to - column_lane(one, j)), along)
                start = (
                    here
                    - speed * angle_ref[2, r] * here
                    - speed * angle_ref[3, r] * (here - along)
                ) * (mask * STATE)
            else:
                start = jnp.where(owner, own_ref[slab_at(r, kb, freq_count), :], got_ref[slab_at(r, kb, freq_count), :])
            done.append(start)
            total = total + start
        for r, start in enumerate(done):
            e_ref[r, pl.ds(PAD + kb * ROWS, ROWS), :] = start
        acc_ref[at, :] = total

    @pl.when(jnp.max(aux[3:4]) > 0.5)
    def _():
        sub_steps(one, freq_count, known_ref, e_ref, u_ref, d_ref, n_ref, w_ref, acc_ref, c_ref)

    store_state(one, freq_count, e_ref, mask * (1.0 / STATE), out_ref)
    if last:
        energy = jnp.sum(acc_ref[...], axis=0, keepdims=True) * (mask[0:1] * (1.0 / (STATE * freq_count * one.dir_count)))
        energy_ref[...] = jnp.concatenate(
            [energy, aux[2:3] - 1.0, jnp.zeros((ROWS - 2, LANES), jnp.float32)], axis=0
        )
    else:
        for kb in range(blocks):
            column_ref[pl.ds(kb * ROWS, ROWS), :] = take_column(
                one, one, NEAR_ENDS, lambda r: out_ref[slab_at(r, kb, freq_count), :], lane
            )


def two_kernel(one, two, freq_count, slot_count, last, code_ref, table_ref, angle_ref, row_ref, *refs):
    if last:
        in_ref, pair_ref, cross_ref, local_ref, other_ref, one_ref, out_ref, energy_ref = refs[:8]
        scratch = refs[8:]
    else:
        own_ref, got_ref, own_aux, cross_ref, out_ref, column_ref, coast_out = refs[:7]
        scratch = refs[7:]
    e_ref, u_ref, d_ref, n_ref, w_ref, acc_ref, c_ref, known_ref = scratch
    known_ref[...] = table_ref[...]
    blocks = freq_count // ROWS
    lane = lanes()
    slot = lane % two.width
    for ref in (e_ref, u_ref, d_ref):
        clear(ref, two.slabs, freq_count)
    aux_at = pl.ds(two.slabs * freq_count, ROWS)
    parity = code_ref[0] % 2
    inner = (code_ref[0] < 2).astype(jnp.float32)
    owner = jnp.broadcast_to(row_ref[1:2, :], (ROWS, LANES)) > 0.5
    from_cross = flow_mask(lane, two.width, 1 - parity)
    from_pair = flow_mask(lane, two.width, parity)
    if last:
        aux = in_ref[aux_at, :]
        mask = every_row(aux, 3)
    else:
        own_rows, got_rows = own_aux[pl.ds(ROWS, ROWS), :], got_ref[pl.ds(got_ref.shape[0] - ROWS, ROWS), :]
        aux = own_rows + got_rows
        out_ref[aux_at, :] = aux
        mask, got_mask = every_row(own_rows, 3), every_row(got_rows, 3)
    set_wind(two, freq_count, table_ref, angle_ref, aux, w_ref)
    for kb in range(blocks):
        at = pl.ds(kb * ROWS, ROWS)
        speed = table_ref[0, at, :]
        total = jnp.zeros((ROWS, LANES), jnp.float32)
        done = []
        slabs = range(two.slabs)
        upward = [angle_ref[1, r] > 0 for r in slabs]
        flow_x = [speed * angle_ref[2, r] for r in slabs]
        flow_y = [speed * angle_ref[3, r] for r in slabs]

        def neighbours(values):
            below = [turn(value, 1) for value in values]
            above = [turn(value, -1) for value in values]
            return [jnp.where(upward[r], below[r], above[r]) for r in slabs]

        here = [(in_ref if last else own_ref)[slab_at(r, kb, freq_count), :] for r in slabs]
        along = neighbours(here)
        across = [loosen(cross_ref, r * blocks + kb) * inner for r in slabs]
        if last:
            beside = [loosen(pair_ref, r * blocks + kb) for r in slabs]
        else:
            beside = [got_ref[slab_at(r, kb, freq_count), :] for r in slabs]
        for r in slabs:
            nearby = jnp.where(from_cross, across[r], jnp.where(from_pair, beside[r], 0.0))
            if last:
                beyond = local_ref[at, :]
                for b in range(two.blocks):
                    j = two.direction(b, r)
                    start = b * two.width
                    if sine_up(j, two.dir_count):
                        to = start + COAST
                        along[r] = jnp.where((lane == to) & ~owner, turn(beyond, to - column_lane(one, j)), along[r])
                    else:
                        to = start + COAST + REST - 1
                        along[r] = jnp.where((lane == to) & owner, turn(beyond, to - column_lane(one, j)), along[r])
                        along[r] = jnp.where((lane == start + COAST - 1) & ~owner, 0.0, along[r])
            else:
                along[r] = jnp.where((slot == 0) & upward[r], 0.0, along[r])
            done.append(
                (here[r] - flow_x[r] * (here[r] - nearby) - flow_y[r] * (here[r] - along[r])) * (mask * STATE)
            )
        if not last:
            here = [turn(beside[r], COAST + REST) for r in slabs]
            along = neighbours(here)
            for r in slabs:
                nearby = jnp.where((slot == COAST + REST - 1) & ~upward[r], 0.0, along[r])
                done[r] = done[r] + (
                    here[r] - flow_x[r] * here[r] - flow_y[r] * (here[r] - nearby)
                ) * (got_mask * STATE)
        for r in slabs:
            total = total + done[r]
        for r, start in enumerate(done):
            e_ref[r, pl.ds(PAD + kb * ROWS, ROWS), :] = start
        acc_ref[at, :] = total
    if last:
        cards = energy_ref.shape[0]
        card = lax.broadcasted_iota(jnp.int32, (cards, LANES), 0) * slot_count
        place = lax.broadcasted_iota(jnp.int32, (LANES, LANES), 0)

        def to_cards(energy, deal):
            deal = deal.astype(jnp.int32)
            to_card = jnp.where((deal >= card) & (deal < card + slot_count), energy, 0.0)
            to_slot = (lax.rem(jnp.maximum(deal, 0), slot_count) == place).astype(jnp.float32)
            return lax.dot_general(
                to_card, to_slot, (((1,), (1,)), ((), ())),
                precision=lax.Precision.HIGHEST, preferred_element_type=jnp.float32,
            )

        out_ref[pl.ds(two.slabs * freq_count, one.slabs * freq_count), :] = one_ref[...]
        elsewhere = to_cards(other_ref[0:1], other_ref[1:2])
    sub_steps(two, freq_count, known_ref, e_ref, u_ref, d_ref, n_ref, w_ref, acc_ref, c_ref)
    scale = every_row(aux, 3) * (1.0 / STATE)
    store_state(two, freq_count, e_ref, scale, out_ref)
    if last:
        energy = jnp.sum(acc_ref[...], axis=0, keepdims=True) * (scale[0:1] / (freq_count * two.dir_count))
        energy_ref[...] = elsewhere + to_cards(energy, aux[2:3] - 1.0)
    else:
        for kb in range(blocks):
            column_ref[pl.ds(kb * ROWS, ROWS), :] = take_column(
                one, two, REST_ENDS, lambda r: out_ref[slab_at(r, kb, freq_count), :], lane
            )
        fetch = lambda i: out_ref[pl.ds(i * ROWS, ROWS), :]
        for g, value in enumerate(squeeze(fetch, two.slabs * blocks, slot < COAST)):
            coast_out[pl.ds(g * ROWS, ROWS), :] = value


def gather_kernel(
    one, two, freq_count, row_ref, two_ref, two_got, out_hbm, after_ref, out_ref, sems
):
    dir_count = one.dir_count
    chunk = ROWS * dir_count
    lane = lanes()
    mask = every_row(row_ref[...], 0)
    base = two.slabs * freq_count
    copies = []
    for kb in range(freq_count // ROWS):
        near = [turn(two_got[slab_at(r, kb, freq_count, base), :], one.width) for r in range(one.slabs)]
        coast = [turn(two_got[slab_at(r, kb, freq_count), :], -(COAST + REST)) for r in range(two.slabs)]
        for some in range(0, dir_count, 12):
            js = range(some, some + 12)
            value, rest = {}, {}
            for j in js:
                b, r = one.find(j)
                start = b * one.width
                mixed = jnp.where(within(lane, start, one.width), two_ref[slab_at(r, kb, freq_count, base), :], near[r])
                value[j] = turn(mixed, COAST + REST - start)
            for j in js:
                b, r = two.find(j)
                start = b * two.width
                mixed = jnp.where(within(lane, start, COAST + REST), two_ref[slab_at(r, kb, freq_count), :], coast[r])
                rest[j] = turn(mixed, -start)
            for j in js:
                whole = jnp.where(within(lane, COAST + REST, 2 * NEAR), value[j], rest[j]) * mask
                out_ref[pl.ds(kb * chunk + j, ROWS, stride=dir_count), :] = whole
        rows = pl.ds(kb * chunk, chunk)
        copies.append(pltpu.make_async_copy(out_ref.at[rows], out_hbm.at[rows], sems.at[kb]))
        copies[kb].start()
    for copy in copies:
        copy.wait()
    after_ref[...] = row_ref[...]


def energy_kernel(shared_ref, after_ref, energy_ref):
    energy_ref[...] = jnp.sum(shared_ref[...], axis=0, keepdims=True)[:, :energy_ref.shape[1]]


def coast_width(tile_count, cell_count):
    capacity = cell_count // tile_count
    spread = tile_count * (tile_count - 8) // 8
    return -(-spread // (tile_count - 1)) * capacity


def shards(spectrum, sea_mask, card_deal, wind):
    freq_count, dir_count, row_count, row_width = spectrum.shape
    cell_count = row_count * row_width
    tile_count = lax.axis_size("tile")
    slot_count = cell_count // 8
    assert row_count == 1 and cell_count == LANES and coast_width(tile_count, cell_count) <= COAST
    here = lax.axis_index("tile")
    at_end = (here == 0) | (here == tile_count - 1)
    code = (here % 2 + 2 * at_end.astype(jnp.int32)).astype(jnp.int32).reshape(1)
    one, two = Pack(3, NEAR, dir_count, 0), Pack(4, 32, dir_count, 1)
    table = jnp.asarray(tables(freq_count, dir_count))
    one_rows, two_rows = one.slabs * freq_count, two.slabs * freq_count
    squeezed = -(-two_rows // ROWS // len(SQUEEZE)) * ROWS

    def array(*shape):
        return jax.ShapeDtypeStruct(shape, jnp.float32)

    smem = pl.BlockSpec(memory_space=pltpu.SMEM)
    vmem = pl.BlockSpec(memory_space=pltpu.VMEM)
    hbm = pl.BlockSpec(memory_space=pltpu.HBM)

    def params(rows, steps=SUB, vmem=48):
        return dict(
            compiler_params=pltpu.CompilerParams(vmem_limit_bytes=vmem * 1024 * 1024),
            cost_estimate=pl.CostEstimate(
                flops=rows // ROWS * steps * 8_000_000, bytes_accessed=8 * rows * LANES, transcendentals=0
            ),
        )

    def scratch(pack):
        padded = pltpu.VMEM((pack.slabs, freq_count + 2 * PAD, LANES), jnp.float32)
        plain = pltpu.VMEM((pack.slabs, freq_count, LANES), jnp.float32)
        column = pltpu.VMEM((freq_count, LANES), jnp.float32)
        return [padded, padded, padded, plain, plain, column, column, pltpu.VMEM(table.shape, jnp.float32)]

    group_count = lax.axis_size("groups")
    chip_swap = []
    for g in range(group_count):
        for i in range(tile_count):
            other, there = g, (i + 1 if i % 2 else i - 1)
            if not 0 <= there < tile_count:
                other, there = (g ^ 1 if g ^ 1 < group_count else g), i
            chip_swap.append((g * tile_count + i, other * tile_count + there))

    def to_pair(value):
        return lax.ppermute(value, "tile", [(i, i ^ 1) for i in range(tile_count)])

    def to_next(value):
        return lax.ppermute(value, ("groups", "tile"), chip_swap)

    one_angles, two_angles = jnp.asarray(one.rows()), jnp.asarray(two.rows())
    flat = spectrum.reshape(freq_count * dir_count, cell_count)
    whole = pltpu.VMEM((freq_count * dir_count, LANES), jnp.float32)
    chunks = pltpu.SemaphoreType.DMA((freq_count // ROWS,))
    one_own, one_send = pl.pallas_call(
        functools.partial(near_kernel, one, freq_count),
        out_shape=(array(one_rows, LANES), array(one_rows, LANES)),
        in_specs=[vmem],
        out_specs=(vmem,) * 2,
        name="near",
        **params(1440, 1),
    )(flat)
    one_got = to_pair(one_send)
    two_own, two_send, cross, row, own_aux = pl.pallas_call(
        functools.partial(coast_kernel, one, two, freq_count),
        out_shape=(
            array(two_rows, LANES), array(two_rows + 2 * ROWS, LANES), array(squeezed, LANES),
            array(ROWS, LANES), array(2 * ROWS, LANES),
        ),
        in_specs=[vmem] * 4,
        out_specs=(vmem,) * 5,
        name="coast",
        **params(1440, 1),
    )(flat, sea_mask, wind.reshape(2, cell_count), card_deal)
    two_got = to_pair(two_send)
    cross_got = to_next(cross)
    one_state, one_column = pl.pallas_call(
        functools.partial(one_kernel, one, freq_count, False),
        out_shape=(array(one_rows + ROWS, LANES), array(freq_count, LANES)),
        in_specs=[vmem] * 7,
        out_specs=(vmem,) * 2,
        scratch_shapes=scratch(one),
        name="first_one",
        **params(one_rows),
    )(table, one_angles, row, one_own, one_got, own_aux, two_got)
    column_got = to_pair(one_column)
    two_state, two_column, coast = pl.pallas_call(
        functools.partial(two_kernel, one, two, freq_count, slot_count, False),
        out_shape=(
            array(two_rows + ROWS, LANES), array(freq_count, LANES), array(squeezed, LANES),
        ),
        in_specs=[smem] + [vmem] * 7,
        out_specs=(vmem,) * 3,
        scratch_shapes=scratch(two),
        name="first_two",
        **params(two_rows),
    )(code, table, two_angles, row, two_own, two_got, own_aux, cross_got)
    cross_got = to_next(coast)
    pair_got = to_pair(coast)
    one_state, one_energy = pl.pallas_call(
        functools.partial(one_kernel, one, freq_count, True),
        out_shape=(array(one_rows, LANES), array(ROWS, LANES)),
        in_specs=[vmem] * 6,
        out_specs=(vmem,) * 2,
        scratch_shapes=scratch(one),
        name="second_one",
        **params(one_rows),
    )(table, one_angles, row, one_state, two_column, column_got)
    two_state, energy = pl.pallas_call(
        functools.partial(two_kernel, one, two, freq_count, slot_count, True),
        out_shape=(array(two_rows + one_rows, LANES), array(tile_count, LANES)),
        in_specs=[smem] + [vmem] * 9,
        out_specs=(vmem,) * 2,
        scratch_shapes=scratch(two),
        name="second_two",
        **params(two_rows),
    )(code, table, two_angles, row, two_state, pair_got, cross_got, one_column, one_energy, one_state)
    two_got = to_pair(two_state)
    shared = lax.all_to_all(
        energy.reshape(tile_count, 1, LANES), "tile", split_axis=0, concat_axis=0, tiled=True
    )
    out, after = pl.pallas_call(
        functools.partial(gather_kernel, one, two, freq_count),
        out_shape=(array(freq_count * dir_count, LANES), array(ROWS, LANES)),
        in_specs=[vmem] * 3,
        out_specs=(hbm, vmem),
        scratch_shapes=[whole, chunks],
        name="gather",
        **params(1440, 1),
    )(row, two_state, two_got)
    card_energy = pl.pallas_call(
        energy_kernel,
        out_shape=array(1, slot_count),
        in_specs=[vmem] * 2,
        out_specs=vmem,
        name="energy",
        **params(80, 1),
    )(shared.reshape(tile_count, LANES), after)
    return out.reshape(freq_count, dir_count, row_count, row_width), card_energy.reshape(slot_count)


def solution(mesh):
    placed = (
        P(None, None, ("groups", "tile"), None),
        P(("groups", "tile"), None),
        P(("groups", "tile"), None),
        P(None, ("groups", "tile"), None),
    )
    return jax.shard_map(
        shards,
        mesh=mesh,
        in_specs=placed,
        out_specs=(P(None, None, ("groups", "tile"), None), P(("groups", "tile"))),
        check_vma=False,
    )
```
